256 devices in a mesh: lat: 8 (over z), lon: 32 (over x, y, core).
Axes of the slice: x: 4, y: 4, z: 8, core: 2. Of those that a mesh axis runs over, the one named last changes fastest.
Arguments:
- displacement: float32 [3, 32, 128, 512], P(None, 'lat', 'lon'), may hold values from -0.12 to 0.12
- velocity: float32 [3, 32, 128, 512], P(None, 'lat', 'lon'), may hold values from -6 to 6
- acceleration: float32 [3, 32, 128, 512], P(None, 'lat', 'lon'), may hold values from -6 to 6
- potential: float32 [32, 128, 512], P('lat', 'lon'), may hold values from -0.6 to 0.6
- memory_vars: bfloat16 [3, 5, 5, 8, 5, 32, 5, 128], P(None, None, None, 'lat', None, 'lon'), may hold values from -0.59765625 to 0.59765625
- materials: int32 [8, 32, 128], P('lat', 'lon'), may hold values from 0 to 7
- shell_flags: int32 [8, 32, 128], P('lat', 'lon'), may hold values from 0 to 1, as said below
- moduli: float32 [8, 6, 6], replicated, as said below
- densities: float32 [8], replicated, may hold values from 1.5 to 4.5
- decay: float32 [3], replicated, may hold values from 0.3 to 0.95
- strength: float32 [3], replicated, may hold values from 0.1 to 0.5
Outputs:
- disp_new: float32 [3, 32, 128, 512], P(None, 'lat', 'lon')
- vel_new: float32 [3, 32, 128, 512], P(None, 'lat', 'lon')
- acc_new: float32 [3, 32, 128, 512], P(None, 'lat', 'lon')
- phi_new: float32 [32, 128, 512], P('lat', 'lon')
- memory_new: bfloat16 [3, 5, 5, 8, 5, 32, 5, 128], P(None, None, None, 'lat', None, 'lon')
The draws below stay inside these ranges and needn't reach their ends.
Inputs may be any that keep to these rules, and one draw needn't show every extreme that they name: `shell_flags`: in every radial column of elements the flagged ones are the outermost ones along the radius, at least one. `moduli`: each material's table is symmetric, each diagonal entry larger than the sum of magnitudes of the rest of its row.
All inputs are finite; a program needn't handle non-finite values.
Results may differ from the reference program's by a relative error of at most 0.0013.
Values sent between devices are 32-bit elements; how exact they have to be, the bound alone decides.
No kernel may reach another device: no remote copies, remote signals or barrier semaphores. Data moves between devices by JAX's collectives and lax.ppermute only.
A program may use at most 128 MiB of HBM per device.

```python
import jax
import jax.numpy as jnp
import numpy as np
from jax import lax

NGLL = 5
SLS = 3
NMAT = 8
ITERS = 3
EX = 1
EZ = 128
NEX = 8
NEY = 32
NX = 32
NY = 128
PZ = 512
N_LAT = 8


def draw_shell_flags(key, part):
    key = jax.random.fold_in(key, 11)
    depth = jax.random.randint(key, (NEX, NEY, 1), max(1, EZ // 8), EZ // 4 + 1)
    levels = jnp.arange(EZ, dtype=jnp.int32)[None, None, :]
    return (levels >= EZ - depth).astype(jnp.int32)


def draw_moduli(key, part):
    key = jax.random.fold_in(key, 12)
    key_diag, key_side = jax.random.split(key)
    identity = jnp.eye(6, dtype=jnp.float32)
    diagonal = jax.random.uniform(key_diag, (NMAT, 6), jnp.float32, 2.0, 4.0)
    side_range = 0.3
    offdiag = jax.random.uniform(key_side, (NMAT, 6, 6), jnp.float32, -side_range, side_range)
    offdiag = 0.5 * (offdiag + jnp.swapaxes(offdiag, 1, 2)) * (1.0 - identity)
    return offdiag + diagonal[:, :, None] * identity


def with_ends(result, key, least, high):
    index_at = [jax.random.randint(jax.random.fold_in(key, axis), (), 0, length) for axis, length in enumerate(result.shape)]
    widest = result.shape.index(max(result.shape))
    next_to = index_at[:widest] + [(index_at[widest] + 1) % result.shape[widest]] + index_at[widest + 1:]
    return result.at[tuple(index_at)].set(least).at[tuple(next_to)].set(high)


def block_levels(own_key, extent, cuts, low, top_value):
    gain, own = 1.0, jax.random.fold_in(own_key, 6)
    for position, shards_of in cuts:
        heights = jnp.exp(jax.random.uniform(jax.random.fold_in(own, position), (shards_of,), jnp.float32, low / len(cuts), top_value / len(cuts)))
        gain = gain * jnp.repeat(heights, extent[position] // shards_of).reshape([-1 if axis == position else 1 for axis in range(len(extent))])
    return gain


def normal_values(stream_key, dims, scale, most, cuts=(), held_as=jnp.bfloat16):
    drawn = scale * jax.random.normal(stream_key, dims, jnp.float32)
    if cuts:
        drawn = drawn * block_levels(stream_key, dims, cuts, -0.22, 0.18)
    return jnp.clip(drawn, -most, most).astype(held_as)


def setup_inputs(seed: int = 0) -> dict:
    streams_of = jax.random.split(jax.random.key(seed), 12)
    return {
        "displacement": normal_values(streams_of[0], (3, NX, NY, PZ), 0.02, 0.12, ((1, 8), (2, 32)), jnp.float32),
        "velocity": normal_values(streams_of[1], (3, NX, NY, PZ), 1.0, 6.0, ((1, 8), (2, 32)), jnp.float32),
        "acceleration": normal_values(streams_of[2], (3, NX, NY, PZ), 1.0, 6.0, ((1, 8), (2, 32)), jnp.float32),
        "potential": normal_values(streams_of[3], (NX, NY, PZ), 0.1, 0.6, ((0, 8), (1, 32)), jnp.float32),
        "memory_vars": normal_values(streams_of[4], (SLS, 5, NGLL, NEX, NGLL, NEY, NGLL, EZ), 0.1, 0.59765625, ((3, 8), (5, 32))),
        "materials": with_ends(jax.random.randint(streams_of[5], (NEX, NEY, EZ), 0, NMAT), jax.random.fold_in(streams_of[5], 1), 0, NMAT - 1).astype(jnp.int32),
        "shell_flags": draw_shell_flags(jax.random.fold_in(streams_of[11], 71), 0),
        "moduli": draw_moduli(jax.random.fold_in(streams_of[11], 71), 0),
        "densities": jnp.clip(jax.random.uniform(streams_of[8], (NMAT,), jnp.float32, 1.5, 4.5), 1.5, 4.5),
        "decay": jnp.clip(jax.random.uniform(streams_of[9], (SLS,), jnp.float32, 0.3, 0.95), 0.3, 0.95),
        "strength": jnp.clip(jax.random.uniform(streams_of[10], (SLS,), jnp.float32, 0.1, 0.5), 0.1, 0.5),
    }


time_step = 0.1
shell_stretch = 3.0
grav_coef = 1.0
highest = lax.Precision.HIGHEST

def gll_tables():
    points = np.array([-1.0, -np.sqrt(3.0 / 7.0), 0.0, np.sqrt(3.0 / 7.0), 1.0])
    weights = np.array([0.1, 49.0 / 90.0, 32.0 / 45.0, 49.0 / 90.0, 0.1])
    differ = points[:, None] - points[None, :] + np.eye(5)
    factors = np.prod(differ, axis=1)
    deriv_mat = factors[:, None] / factors[None, :] / differ * (1.0 - np.eye(5))
    deriv_mat = deriv_mat - np.eye(5) * np.sum(deriv_mat, axis=1)[:, None]
    cube = weights[:, None, None] * weights[None, :, None] * weights[None, None, :] * 0.125
    weight_cube = cube.reshape(1, 5, 1, 5, 1, 5, 1)
    return (jnp.asarray(deriv_mat, jnp.float32), jnp.asarray(deriv_mat.T, jnp.float32), jnp.asarray((deriv_mat ** 2).T, jnp.float32), jnp.asarray(weight_cube, jnp.float32))

def contract(field_vals, matrix, direction):
    if direction == 0:
        return jnp.einsum('pa,caxbydz->cpxbydz', matrix, field_vals, precision=highest)
    if direction == 1:
        return jnp.einsum('pb,caxbydz->caxpydz', matrix, field_vals, precision=highest)
    return jnp.einsum('pd,caxbydz->caxbypz', matrix, field_vals, precision=highest)

def spread(values):
    return values[None, None, :, None, :, None, :]

def split_axis(array, dim_pos, elem_count):
    pieces = [lax.slice_in_dim(array, start, start + 4 * (elem_count - 1) + 1, 4, dim_pos) for start in range(5)]
    return jnp.stack(pieces, dim_pos)

def to_elements(extended):
    values = split_axis(extended, 1, (extended.shape[1] - 1) // 4)
    values = split_axis(values, 3, (extended.shape[2] - 1) // 4)
    return split_axis(values, 5, (extended.shape[3] - 1) // 4)

def merge_axis(values, dim_pos):
    leading = lax.slice_in_dim(values, 0, 4, 1, dim_pos)
    trailing = jnp.concatenate([jnp.zeros_like(lax.slice_in_dim(values, 0, 3, 1, dim_pos)), lax.slice_in_dim(values, 4, 5, 1, dim_pos)], dim_pos)

    def alternate(block):
        block = jnp.swapaxes(block, dim_pos, dim_pos + 1)
        block_shape = block.shape
        return block.reshape(block_shape[:dim_pos] + (block_shape[dim_pos] * 4,) + block_shape[dim_pos + 2:])
    widths_end = [(0, 0)] * (values.ndim - 1)
    widths_front = [(0, 0)] * (values.ndim - 1)
    widths_end[dim_pos] = (0, 1)
    widths_front[dim_pos] = (1, 0)
    return jnp.pad(alternate(leading), widths_end) + jnp.pad(alternate(trailing), widths_front)

def to_points(values):
    values = merge_axis(values, 5)
    values = merge_axis(values, 3)
    return merge_axis(values, 1)

def grad_three(values, z_scale, tables):
    return (2.0 * contract(values, tables[0], 0), 2.0 * contract(values, tables[0], 1), z_scale * contract(values, tables[0], 2))

def div_three(flux_x, flux_y, flux_z, z_scale, tables):
    return 2.0 * contract(flux_x, tables[1], 0) + 2.0 * contract(flux_y, tables[1], 1) + z_scale * contract(flux_z, tables[1], 2)

def shell_geometry(shell_flags):
    stretch = 1.0 + (shell_stretch - 1.0) * spread(shell_flags.astype(jnp.float32))
    return (stretch, 2.0 / stretch)

def poisson_elements(values, shell_flags, tables):
    stretch, z_scale = shell_geometry(shell_flags)
    volume = tables[3] * stretch
    grad_x, grad_y, grad_z = grad_three(values, z_scale, tables)
    return div_three(volume * grad_x, volume * grad_y, volume * grad_z, z_scale, tables)

def density_lookup(materials, densities):
    onehot = (materials[..., None] == jnp.arange(densities.shape[0], dtype=jnp.int32)).astype(jnp.float32)
    return (onehot, jnp.einsum('xyzm,m->xyz', onehot, densities, precision=highest))

def first_block(extended, materials, shell_flags, memory_vars, moduli, densities, decay, strength, tables):
    values = to_elements(extended)
    displaced = values[0:3]
    potential_vals = values[3:4]
    onehot, density = density_lookup(materials, densities)
    stiffness = jnp.einsum('xyzm,mkl->klxyz', onehot, moduli, precision=highest)
    weight_cube = tables[3]
    grad_x, grad_y, grad_z = grad_three(displaced, 2.0, tables)
    strain = jnp.stack([grad_x[0], grad_y[1], grad_z[2], grad_y[0] + grad_x[1], grad_z[0] + grad_x[2], grad_z[1] + grad_y[2]])
    elastic = jnp.einsum('klxyz,laxbydz->kaxbydz', stiffness, strain, precision=highest)
    pressure = (elastic[0] + elastic[1] + elastic[2]) / 3.0
    deviator = jnp.stack([elastic[0] - pressure, elastic[1] - pressure, elastic[3], elastic[4], elastic[5]])
    decay_rate = decay.reshape(-1, 1, 1, 1, 1, 1, 1, 1)
    gain_rate = strength.reshape(-1, 1, 1, 1, 1, 1, 1, 1)
    memory_new = (decay_rate * memory_vars.astype(jnp.float32) + (1.0 - decay_rate) * gain_rate * deviator[None]).astype(jnp.bfloat16)
    memory_new = lax.optimization_barrier(memory_new)
    relaxed = lax.optimization_barrier(jnp.sum(memory_new.astype(jnp.float32), 0))
    stress = [elastic[0] - relaxed[0], elastic[1] - relaxed[1], elastic[2] + relaxed[0] + relaxed[1], elastic[3] - relaxed[2], elastic[4] - relaxed[3], elastic[5] - relaxed[4]]
    flux_x = weight_cube * jnp.stack([stress[0], stress[3], stress[4]])
    flux_y = weight_cube * jnp.stack([stress[3], stress[1], stress[5]])
    flux_z = weight_cube * jnp.stack([stress[4], stress[5], stress[2]])
    elastic_force = div_three(flux_x, flux_y, flux_z, 2.0, tables)
    mass_vals = weight_cube * spread(density)
    carried = weight_cube * spread(density * (1.0 - shell_flags.astype(jnp.float32))) * displaced
    source = -grav_coef * div_three(carried[0:1], carried[1:2], carried[2:3], 2.0, tables)
    stretch, z_scale = shell_geometry(shell_flags)
    volume = weight_cube * stretch
    precond = 4.0 * contract(volume, tables[2], 0) + 4.0 * contract(volume, tables[2], 1) + z_scale * z_scale * contract(volume, tables[2], 2)
    poisson_vals = poisson_elements(potential_vals, shell_flags, tables)
    joined = jnp.concatenate([elastic_force, source, mass_vals, precond, poisson_vals], 0)
    return (to_points(joined), memory_new)

def gravity_block(extended, materials, shell_flags, densities, tables):
    values = to_elements(extended)
    onehot, density = density_lookup(materials, densities)
    stretch, z_scale = shell_geometry(shell_flags)
    grad_x, grad_y, grad_z = grad_three(values, z_scale, tables)
    coefficient = -tables[3] * spread(density)
    return to_points(jnp.concatenate([coefficient * grad_x, coefficient * grad_y, coefficient * grad_z], 0))

def reference(displacement, velocity, acceleration, potential, memory_vars, materials, shell_flags, moduli, densities, decay, strength):
    tables = gll_tables()
    width = 4 * EX
    disp_new = displacement + time_step * velocity + 0.5 * time_step * time_step * acceleration

    def extend_all(fields):
        fields = jnp.concatenate([fields, jnp.zeros_like(fields[:, :1])], 1)
        fields = jnp.concatenate([fields, fields[:, :, :1]], 2)
        return jnp.pad(fields, ((0, 0), (0, 0), (0, 0), (0, 1)))

    def slabs(array):
        return array.reshape((N_LAT, EX) + array.shape[1:])

    def over_slabs(extended, work, extras):

        def one_slab(item):
            slab = lax.dynamic_slice_in_dim(extended, item[0] * width, width + 1, 1)
            return work(slab, *item[1:])
        return lax.map(one_slab, (jnp.arange(N_LAT, dtype=jnp.int32),) + extras)

    def assemble_all(contrib):
        trimmed = contrib[..., :-1]
        main_part = trimmed[:, :, :, :-1]
        main_part = main_part.at[:, :, :, 0].add(trimmed[:, :, :, -1])
        row_part = main_part[:, :, :-1]
        upper_part = main_part[:, :, -1]
        row_part = row_part.at[1:, :, 0].add(upper_part[:-1])
        channels = row_part.shape[1]
        return jnp.moveaxis(row_part, 0, 1).reshape(channels, NX, NY, PZ)
    flag_slabs = slabs(shell_flags)
    mat_slabs = slabs(materials)
    mem_slabs = jnp.moveaxis(memory_vars.reshape(SLS, 5, NGLL, N_LAT, EX, NGLL, NEY, NGLL, EZ), 3, 0)

    def first_work(slab, mat_slab, flag_slab, mem_slab):
        return first_block(slab, mat_slab, flag_slab, mem_slab, moduli, densities, decay, strength, tables)
    contrib, mem_out = over_slabs(extend_all(jnp.concatenate([disp_new, potential[None]], 0)), first_work, (mat_slabs, flag_slabs, mem_slabs))
    memory_new = jnp.moveaxis(mem_out, 0, 3).reshape(SLS, 5, NGLL, NEX, NGLL, NEY, NGLL, EZ)
    assembled = assemble_all(contrib)
    elastic_force = assembled[0:3]
    source = assembled[3]
    mass_diag = assembled[4]
    precond = assembled[5]
    kpotential = assembled[6]

    def poisson_work(slab, flag_slab):
        return to_points(poisson_elements(to_elements(slab), flag_slab, tables))

    def apply_poisson(search_dir):
        return assemble_all(over_slabs(extend_all(search_dir[None]), poisson_work, (flag_slabs,)))[0]
    phi_now = potential
    residual = source - kpotential
    precond_res = residual / precond
    rz_now = jnp.sum(residual * precond_res)
    search_dir = precond_res
    for step in range(ITERS):
        image_dir = apply_poisson(search_dir)
        step_len = rz_now / jnp.sum(search_dir * image_dir)
        phi_now = phi_now + step_len * search_dir
        residual = residual - step_len * image_dir
        if step + 1 < ITERS:
            precond_res = residual / precond
            rz_next = jnp.sum(residual * precond_res)
            search_dir = precond_res + rz_next / rz_now * search_dir
            rz_now = rz_next

    def gravity_work(slab, mat_slab, flag_slab):
        return gravity_block(slab, mat_slab, flag_slab, densities, tables)
    gravity = assemble_all(over_slabs(extend_all(phi_now[None]), gravity_work, (mat_slabs, flag_slabs)))
    acc_new = (gravity - elastic_force) / mass_diag[None]
    vel_new = velocity + 0.5 * time_step * (acceleration + acc_new)
    return (disp_new, vel_new, acc_new, phi_now, memory_new)
```

```python
import functools

import jax
import jax.numpy as jnp
import numpy as np
from jax import lax
from jax.experimental import pallas as pl
from jax.experimental.pallas import tpu as pltpu
from jax.sharding import PartitionSpec as P

TIME_STEP = 0.1
F32 = jnp.float32
BF16 = jnp.bfloat16
LAT, LON = 8, 32
AXES = ("lat", "lon")
VMEM = pl.BlockSpec(memory_space=pltpu.VMEM)
SMEM = pl.BlockSpec(memory_space=pltpu.SMEM)


def gll():
    points = np.array([-1.0, -np.sqrt(3.0 / 7.0), 0.0, np.sqrt(3.0 / 7.0), 1.0])
    weights = np.array([0.1, 49.0 / 90.0, 32.0 / 45.0, 49.0 / 90.0, 0.1])
    differ = points[:, None] - points[None, :] + np.eye(5)
    factors = np.prod(differ, axis=1)
    deriv = factors[:, None] / factors[None, :] / differ * (1.0 - np.eye(5))
    deriv = deriv - np.eye(5) * np.sum(deriv, axis=1)[:, None]
    return deriv, weights


DERIV, WEIGHTS = gll()
W = [float(v) for v in WEIGHTS]
M_POISSON = (DERIV.T @ np.diag(WEIGHTS) @ DERIV).tolist()
M_SOURCE = (np.diag(WEIGHTS) @ DERIV).T.tolist()
M_GRAVITY = (np.diag(WEIGHTS) @ DERIV).tolist()


def lanes(shape):
    return lax.broadcasted_iota(jnp.int32, shape, len(shape) - 1)


def sublanes(shape):
    return lax.broadcasted_iota(jnp.int32, shape, len(shape) - 2)


def by_index(index, values):
    out = jnp.full(index.shape, float(values[-1]), F32)
    for pos in range(len(values) - 2, -1, -1):
        out = jnp.where(index == pos, float(values[pos]), out)
    return out


def column(values, rows=4, width=512):
    return by_index(sublanes((rows, width)), list(values))


def row_of(array, pos, rows=4):
    return jnp.broadcast_to(array[pos : pos + 1], (rows, array.shape[1]))


def radial(field, matrix):
    lane = lanes((4, 512))
    node = lane & 3
    own, before = None, None
    for shift in range(-4, 5):
        moved = field if shift == 0 else pltpu.roll(field, (-shift) % 512, 1)
        if shift > -4:
            factors = [
                matrix[c][c + shift] if 0 <= c + shift <= 4 else 0.0 for c in range(4)
            ]
            table = by_index(node, factors)
            if shift > 0:
                table = jnp.where(lane < 512 - shift, table, 0.0)
            own = table * moved if own is None else own + table * moved
        if shift <= 0:
            term = float(matrix[4][4 + shift]) * moved
            before = term if before is None else before + term
    return own, before


def mix(matrix_row, arrays):
    total = None
    for factor, array in zip(matrix_row, arrays):
        term = float(factor) * array
        total = term if total is None else total + term
    return total


def lat_part(fields, above, below, matrix, own_row, back_row):
    out = []
    for i in range(4):
        value = own_row * mix(matrix[i], fields + [above])
        if i == 0:
            value = value + back_row * (float(matrix[4][4]) * fields[0] + below)
        out.append(value)
    return out


def lon_part(fields, above, below, matrix, own_col, back_col):
    columns = [column([matrix[b][p] for b in range(4)]) for p in range(5)]
    first = column([1.0, 0.0, 0.0, 0.0])
    out = []
    for i in range(4):
        value = columns[4] * row_of(above, i)
        for p in range(4):
            value = value + columns[p] * row_of(fields[i], p)
        edge = float(matrix[4][4]) * fields[i][0:1] + below[i : i + 1]
        kind = min(i, 1)
        value = own_col[kind] * value + first * (back_col[kind] * edge)
        out.append(W[i] * value)
    return out


def radial_part(fields, matrix, own, before):
    out = []
    for i in range(4):
        first, second = radial(fields[i], matrix)
        kind = min(i, 1)
        out.append(W[i] * (own[kind] * first + before[kind] * second))
    return out


def partial_lat(fields, matrix):
    return mix(matrix[4][:4], fields)


def partial_lon(field, matrix):
    weighted = column(matrix[4][:4]) * field
    return jnp.sum(weighted, axis=0, keepdims=True)


def messages(fields, up_lat, down_lat, up_lon, down_lon):
    up_lat[0:4, :] = partial_lat(fields, M_POISSON)
    up_lat[4:8, :] = partial_lat(fields, M_GRAVITY)
    down_lat[0:4, :] = fields[0]
    for i in range(4):
        up_lon[i : i + 1, :] = partial_lon(fields[i], M_POISSON)
        up_lon[4 + i : 5 + i, :] = partial_lon(fields[i], M_GRAVITY)
        down_lon[i : i + 1, :] = fields[i][0:1]


def has_next():
    return jnp.where(lax.axis_index("lat") < LAT - 1, 1.0, 0.0).astype(F32)


def has_before():
    return jnp.where(lax.axis_index("lat") > 0, 1.0, 0.0).astype(F32)


def start_kernel(disp, vel, acc, phi, mat, flag, disp_new, up_lat, down_lat, up_lon, down_lon, code):
    u = []
    for comp in range(3):
        planes = []
        for i in range(4):
            value = (
                disp[comp, i]
                + TIME_STEP * vel[comp, i]
                + 0.5 * TIME_STEP * TIME_STEP * acc[comp, i]
            )
            disp_new[comp, i] = value
            planes.append(value)
        u.append(planes)
    potential = [phi[i] for i in range(4)]
    kind = (1 + mat[0] + 8 * flag[0]).astype(F32).astype(BF16)
    spread = (
        lax.broadcasted_iota(jnp.int32, (128, 512), 1) // 4
        == lax.broadcasted_iota(jnp.int32, (128, 512), 0)
    )
    spread = jnp.where(spread, 1.0, 0.0).astype(BF16)
    kinds = jnp.dot(jnp.broadcast_to(kind, (16, 128)), spread, preferred_element_type=F32)
    kinds = kinds[0:8]
    code[...] = kinds
    up_lat[0:4, :] = partial_lat(u[0], M_SOURCE)
    up_lat[4:8, :] = partial_lat(potential, M_POISSON)
    up_lat[8:12, :] = partial_lat(potential, M_GRAVITY)
    up_lat[12:16, :] = kinds[0:4]
    up_lon[12:16, :] = kinds[0:4]
    for comp in range(3):
        down_lat[4 * comp : 4 * comp + 4, :] = u[comp][0]
        for i in range(4):
            row = 4 * comp + i
            down_lon[row : row + 1, :] = u[comp][i][0:1]
    down_lat[12:16, :] = potential[0]
    for i in range(4):
        up_lon[i : i + 1, :] = partial_lon(u[1][i], M_SOURCE)
        up_lon[4 + i : 5 + i, :] = partial_lon(potential[i], M_POISSON)
        up_lon[8 + i : 9 + i, :] = partial_lon(potential[i], M_GRAVITY)
        down_lon[12 + i : 13 + i, :] = potential[i][0:1]


def lat_rows(factor):
    cols, first = column(W[:4]), column([W[0], 0.0, 0.0, 0.0])
    own = cols * row_of(factor, 0) + first * row_of(factor, 2)
    back = cols * row_of(factor, 1) + first * row_of(factor, 3)
    return own, back


def lon_cols(factor):
    own = (factor[0:1] + factor[1:2], factor[0:1])
    back = (factor[2:3] + factor[3:4], factor[2:3])
    return own, back


def residual_kernel(
    disp_new, phi, own_code, lat_below, lat_above, lon_below, lon_above, diag_code, dens,
    coef, rho_coef, precond_out, w0_out, up_lat, down_lat, up_lon, down_lon,
):
    following, before = has_next(), has_before()
    codes = jnp.concatenate(
        [
            own_code[0:1, :],
            before * lat_below[12:13, :],
            lon_below[12:13, :],
            before * diag_code[0:1, :],
        ],
        0,
    )
    flagged = codes > 8.5
    material = jnp.where(flagged, codes - 9.0, codes - 1.0)
    valid = codes > 0.5
    rho = jnp.zeros((4, 512), F32)
    for m in range(8):
        rho = jnp.where(jnp.abs(material - m) < 0.5, dens[m], rho)
    rho = jnp.where(valid, rho, 0.0)
    stretch = jnp.where(valid, jnp.where(flagged, 3.0, 1.0), 0.0)
    inverse = jnp.where(valid, jnp.where(flagged, 1.0 / 3.0, 1.0), 0.0)
    rho_in = jnp.where(flagged, 0.0, rho)
    lane = lanes((4, 512))
    node = lane & 3
    joint = jnp.logical_and(node == 0, lane >= 4)
    weight = by_index(node, W[:4])

    def earlier(factor):
        return jnp.where(joint, pltpu.roll(factor, 4, 1), 0.0)

    def weighted(factor):
        return weight * factor + W[4] * earlier(factor)

    s_points = 0.5 * weighted(stretch)
    s_own, s_back = lat_rows(s_points)
    s_col, s_col_back = lon_cols(s_points)
    i_own, i_back = lat_rows(0.5 * inverse)
    j_own, j_back = lat_rows(0.5 * earlier(inverse))
    i_both, j_both = (i_own + i_back, i_own), (j_own + j_back, j_own)
    coef[0:4, :] = s_own
    coef[4:8, :] = s_back
    coef[8:12, :] = i_both[0]
    coef[12:16, :] = i_both[1]
    coef[16:20, :] = j_both[0]
    coef[20:24, :] = j_both[1]
    coef[24:25, :] = s_col[0]
    coef[25:26, :] = s_col[1]
    coef[26:27, :] = s_col_back[0]
    coef[27:28, :] = s_col_back[1]
    r_points = 0.25 * weighted(rho)
    r_own, r_back = lat_rows(r_points)
    r_col, r_col_back = lon_cols(r_points)
    scaled = 0.25 * rho * inverse
    g_own, g_back = lat_rows(scaled)
    h_own, h_back = lat_rows(earlier(scaled))
    rho_coef[0:4, :] = r_own
    rho_coef[4:8, :] = r_back
    rho_coef[8:12, :] = g_own + g_back
    rho_coef[12:16, :] = g_own
    rho_coef[16:20, :] = h_own + h_back
    rho_coef[20:24, :] = h_own
    rho_coef[24:25, :] = r_col[0]
    rho_coef[25:26, :] = r_col[1]
    rho_coef[26:27, :] = r_col_back[0]
    rho_coef[27:28, :] = r_col_back[1]
    q_points = 0.25 * weighted(rho_in)
    q_own, q_back = lat_rows(q_points)
    q_col, q_col_back = lon_cols(q_points)
    t_own, t_back = lat_rows(0.25 * rho_in)
    v_own, v_back = lat_rows(0.25 * earlier(rho_in))

    u = [[disp_new[comp, i] for i in range(4)] for comp in range(3)]
    potential = [phi[i] for i in range(4)]
    source_x = lat_part(
        u[0], following * lat_above[0:4, :], lat_below[0:4, :], M_SOURCE, q_own, q_back
    )
    source_y = lon_part(
        u[1], lon_above[4:8, :], lon_below[0:4, :], M_SOURCE, q_col, q_col_back
    )
    source_z = radial_part(u[2], M_SOURCE, (t_own + t_back, t_own), (v_own + v_back, v_own))
    image_x = lat_part(
        potential, following * lat_above[12:16, :], lat_below[4:8, :], M_POISSON, s_own, s_back
    )
    image_y = lon_part(
        potential, lon_above[12:16, :], lon_below[4:8, :], M_POISSON, s_col, s_col_back
    )
    image_z = radial_part(potential, M_POISSON, i_both, j_both)
    diag = [M_POISSON[a][a] for a in range(5)]
    diag_node = by_index(node, diag[:4])
    diag_col = column(diag[:4])
    first = column([1.0, 0.0, 0.0, 0.0])
    w0 = []
    for i in range(4):
        kind = min(i, 1)
        precond = diag[i] * s_own
        if i == 0:
            precond = precond + diag[4] * s_back
        precond = precond + W[i] * (
            diag_col * s_col[kind]
            + first * (diag[4] * s_col_back[kind])
            + i_both[kind] * diag_node
            + diag[4] * j_both[kind]
        )
        precond_out[i] = precond
        source = -(source_x[i] + source_y[i] + source_z[i])
        image = image_x[i] + image_y[i] + image_z[i]
        value = (source - image) / precond
        w0_out[i] = value
        w0.append(value)
    messages(w0, up_lat, down_lat, up_lon, down_lon)
    for comp in range(3):
        down_lat[4 + comp : 5 + comp, :] = lon_above[4 * comp : 4 * comp + 1, :]
    down_lat[7:8, :] = jnp.zeros((1, 512), F32)


def poisson(fields, coef, lat_below, lat_above, lon_below, lon_above):
    following = has_next()
    s_col = (coef[24:25, :], coef[25:26, :])
    s_col_back = (coef[26:27, :], coef[27:28, :])
    x = lat_part(
        fields, following * lat_above[0:4, :], lat_below[0:4, :], M_POISSON, coef[0:4, :], coef[4:8, :]
    )
    y = lon_part(fields, lon_above[0:4, :], lon_below[0:4, :], M_POISSON, s_col, s_col_back)
    z = radial_part(
        fields, M_POISSON, (coef[8:12, :], coef[12:16, :]), (coef[16:20, :], coef[20:24, :])
    )
    return [x[i] + y[i] + z[i] for i in range(4)]


def next_kernel(
    last, field, coef, precond, lat_below, lat_above, lon_below, lon_above, *rest
):
    if last:
        lat_force, lon_force, out, up_lat, down_lat, up_lon, down_lon = rest
    else:
        out, up_lat, down_lat, up_lon, down_lon = rest
    fields = [field[i] for i in range(4)]
    image = poisson(fields, coef, lat_below, lat_above, lon_below, lon_above)
    result = []
    for i in range(4):
        value = image[i] / precond[i] - fields[i]
        out[i] = value
        result.append(value)
    messages(result, up_lat, down_lat, up_lon, down_lon)
    down_lat[4:8, :] = jnp.zeros((4, 512), F32)
    down_lon[4:8, :] = jnp.zeros((4, 512), F32)
    if last:
        up_lat[8:24, :] = lat_force[...]
        up_lon[8:24, :] = lon_force[...]


def moment_kernel(w0, w1, w2, coef, precond, lat_below, lat_above, lon_below, lon_above, out):
    fields = [w2[i] for i in range(4)]
    image = poisson(fields, coef, lat_below, lat_above, lon_below, lon_above)
    sums = [None] * 6
    for i in range(4):
        m = precond[i]
        a, b, c = w0[i], w1[i], w2[i]
        ma, mb, mc = m * a, m * b, m * c
        terms = [a * ma, b * ma, b * mb, c * mb, c * mc, c * (image[i] - mc)]
        for k in range(6):
            sums[k] = terms[k] if sums[k] is None else sums[k] + terms[k]
    lane = lanes((1, 128))
    line = jnp.zeros((1, 128), F32)
    for k in range(6):
        total = jnp.sum(jnp.sum(sums[k], axis=0, keepdims=True), axis=1, keepdims=True)
        line = jnp.where(lane == k, total, line)
    out[...] = jnp.broadcast_to(line, out.shape)


def cg_coefficients(mu):
    zero = jnp.zeros_like(mu[0])

    def inner(a):
        total = zero
        for i in range(len(a)):
            for j in range(len(a)):
                total = total + a[i] * a[j] * mu[i + j]
        return total

    def energy(a):
        total = zero
        for i in range(len(a)):
            for j in range(len(a)):
                total = total + a[i] * a[j] * (mu[i + j + 1] + mu[i + j])
        return total

    def ratio(a, b):
        return jnp.where(b == 0.0, 0.0, a / jnp.where(b == 0.0, 1.0, b))

    y = [zero, zero, zero]
    z = [zero + 1.0]
    search = [zero + 1.0]
    rz = mu[0]
    for step in range(3):
        length = ratio(rz, energy(search))
        for i in range(len(search)):
            y[i] = y[i] + length * search[i]
        if step < 2:
            grown = [zero] * (len(search) + 1)
            for i in range(len(search)):
                grown[i] = grown[i] + search[i]
                grown[i + 1] = grown[i + 1] + search[i]
            z = z + [zero]
            z = [z[i] - length * grown[i] for i in range(len(z))]
            rz_next = inner(z)
            beta = ratio(rz_next, rz)
            padded = search + [zero]
            search = [z[i] + beta * padded[i] for i in range(len(z))]
            rz = rz_next
    return y


def final_kernel(
    moments, phi, w0, w1, w2, rho_coef, own_force, corner,
    ma, mb, mc, md, na, nb, nc, nd, fa, fb, fc, fd, ga, gb, gc, gd,
    vel, acc, phi_new, acc_new, vel_new,
):
    total = jnp.sum(moments[...], axis=0, keepdims=True)
    lane = lanes((1, 128))
    mu = [
        jnp.broadcast_to(
            jnp.sum(jnp.where(lane == k, total, 0.0), axis=1, keepdims=True), (1, 128)
        )
        for k in range(6)
    ]
    y = cg_coefficients(mu)
    y = [jnp.concatenate([v] * 4, 1) for v in y]

    def combined(first, one, two, three):
        return first + y[0] * one + y[1] * two + y[2] * three

    potential = []
    for i in range(4):
        value = combined(phi[i], w0[i], w1[i], w2[i])
        phi_new[i] = value
        potential.append(value)
    following, before = has_next(), has_before()
    lat_below = combined(ma[8:12, :], mb[4:8, :], mc[4:8, :], md[4:8, :])
    lat_above = following * combined(na[12:16, :], nb[0:4, :], nc[0:4, :], nd[0:4, :])
    lon_below = combined(fa[8:12, :], fb[4:8, :], fc[4:8, :], fd[4:8, :])
    lon_above = combined(ga[12:16, :], gb[0:4, :], gc[0:4, :], gd[0:4, :])
    r_own, r_back = rho_coef[0:4, :], rho_coef[4:8, :]
    r_col = (rho_coef[24:25, :], rho_coef[25:26, :])
    r_col_back = (rho_coef[26:27, :], rho_coef[27:28, :])
    x = lat_part(potential, lat_above, lat_below, M_GRAVITY, r_own, r_back)
    y_part = lon_part(potential, lon_above, lon_below, M_GRAVITY, r_col, r_col_back)
    z = radial_part(
        potential,
        M_GRAVITY,
        (rho_coef[8:12, :], rho_coef[12:16, :]),
        (rho_coef[16:20, :], rho_coef[20:24, :]),
    )
    cols = column(W[:4])
    first = column([1.0, 0.0, 0.0, 0.0])
    gravity = (x, y_part, z)
    for i in range(4):
        mass = r_own + r_back if i == 0 else r_own
        mass = 0.5 * W[i] * mass
        for comp in range(3):
            force = own_force[comp, i]
            force = force + first * fd[8 + 5 * comp + i : 9 + 5 * comp + i, :]
            if i == 0:
                edge = md[8 + 4 * comp : 12 + 4 * comp, :]
                edge = edge + first * corner[comp : comp + 1, :]
                force = force + before * edge
            value = (-gravity[comp][i] - force) / mass
            acc_new[comp, i] = value
            vel_new[comp, i] = vel[comp, i] + 0.5 * TIME_STEP * (acc[comp, i] + value)


def split3(value):
    high = value.astype(BF16)
    rest = value - high.astype(F32)
    mid = rest.astype(BF16)
    low = (rest - mid.astype(F32)).astype(BF16)
    return high, mid, low


def elastic_kernel(
    disp, lat_above, lon_above, corner, mat, moduli, decay, strength, memory,
    memory_new, force, lat_force, lon_force, corner_force,
    points, elems, stiff, devs, old, new, flux, perm,
):
    following = has_next()
    points[...] = jnp.zeros(points.shape, F32)
    for comp in range(3):
        for a in range(4):
            base = (comp * 5 + a) * 8
            points[base : base + 4, :] = disp[comp, a]
            row = 4 * comp + a
            points[base + 4 : base + 5, :] = lon_above[row : row + 1, :]
        base = (comp * 5 + 4) * 8
        points[base : base + 4, :] = following * lat_above[4 * comp : 4 * comp + 4, :]
        points[base + 4 : base + 5, :] = following * corner[4 + comp : 5 + comp, :]
    for c in range(4):
        hit = lax.broadcasted_iota(jnp.int32, (128, 512), 1) == (
            4 * lax.broadcasted_iota(jnp.int32, (128, 512), 0) + c
        )
        perm[128 * c : 128 * c + 128, :] = jnp.where(hit, 1.0, 0.0).astype(BF16)
    parts = jnp.concatenate(split3(points[...]), 0)
    taken = lax.dot_general(
        parts, perm[...], (((1,), (1,)), ((), ())), preferred_element_type=F32
    )
    taken = taken[0:128] + taken[128:256] + taken[256:384]
    for c in range(4):
        elems[c] = taken[:, 128 * c : 128 * c + 128]
    lane = lanes((128, 128))
    elems[4] = jnp.where(lane < 127, pltpu.roll(taken[:, 0:128], 127, 1), 0.0)
    onehot = [mat[0] == m for m in range(8)]
    for k in range(6):
        for l in range(k, 6):
            value = jnp.zeros((1, 128), F32)
            for m in range(8):
                value = jnp.where(onehot[m], moduli[m, k, l], value)
            stiff[6 * k + l : 6 * k + l + 1, :] = value
    slopes = [
        by_index(sublanes((8, 128)), [2.0 * DERIV[b][p] for b in range(5)] + [0.0])
        for p in range(5)
    ]
    turned = [
        by_index(sublanes((8, 128)), [2.0 * DERIV[p][b] for b in range(5)] + [0.0])
        for p in range(5)
    ]
    weight_col = by_index(sublanes((8, 128)), W + [0.0])

    def slab(comp, a, c):
        base = (comp * 5 + a) * 8
        return elems[c, base : base + 8, :]

    def along_lon(cols, value):
        total = None
        for p in range(5):
            term = cols[p] * row_of(value, p, 8)
            total = term if total is None else total + term
        return total

    for a in range(5):
        elastic_of = []
        for c in range(5):
            dx, dy, dz = [], [], []
            for comp in range(3):
                dx.append(mix([2.0 * DERIV[a][p] for p in range(5)], [slab(comp, p, c) for p in range(5)]))
                dy.append(along_lon(slopes, slab(comp, a, c)))
                dz.append(mix([2.0 * DERIV[c][p] for p in range(5)], [slab(comp, a, p) for p in range(5)]))
            strain = [dx[0], dy[1], dz[2], dy[0] + dx[1], dz[0] + dx[2], dz[1] + dy[2]]
            elastic = []
            for k in range(6):
                total = None
                for l in range(6):
                    pos = 6 * min(k, l) + max(k, l)
                    term = stiff[pos : pos + 1, :] * strain[l]
                    total = term if total is None else total + term
                elastic.append(total)
            pressure = (elastic[0] + elastic[1] + elastic[2]) * (1.0 / 3.0)
            dev = [elastic[0] - pressure, elastic[1] - pressure, elastic[3], elastic[4], elastic[5]]
            for d in range(5):
                devs[d * 5 + c] = dev[d]
            elastic_of.append(elastic)
        relaxed = []
        for d in range(5):
            for b in range(5):
                for c in range(5):
                    row = (b * 5 + c) * 4
                    old[row : row + 3, :] = memory[d, a, b, c].astype(F32)
            sums = []
            for c in range(5):
                dev = devs[d * 5 + c]
                total = None
                for l in range(3):
                    was = old[pl.ds(4 * c + l, 8, stride=20), :]
                    rate = decay[l]
                    now = rate * was + ((1.0 - rate) * strength[l]) * dev
                    now = now.astype(BF16).astype(F32)
                    new[pl.ds(4 * c + l, 8, stride=20), :] = now
                    total = now if total is None else total + now
                sums.append(total)
            for b in range(5):
                for c in range(5):
                    row = (b * 5 + c) * 4
                    memory_new[d, a, b, c] = new[row : row + 3, :].astype(BF16)
            relaxed.append(sums)
        for c in range(5):
            e = elastic_of[c]
            r = [relaxed[d][c] for d in range(5)]
            weight = weight_col * (W[a] * W[c] / 8.0)
            stress = [e[0] - r[0], e[1] - r[1], e[2] + r[0] + r[1], e[3] - r[2], e[4] - r[3], e[5] - r[4]]
            for k in range(6):
                flux[k, a * 5 + c] = jnp.where(weight_col > 0.0, weight * stress[k], 0.0)
    flux_of = [[0, 3, 4], [3, 1, 5], [4, 5, 2]]
    for c in range(5):
        elems[c, 120:128, :] = jnp.zeros((8, 128), F32)
        for comp in range(3):
            for a in range(5):
                value = mix(
                    [2.0 * DERIV[p][a] for p in range(5)],
                    [flux[flux_of[comp][0], p * 5 + c] for p in range(5)],
                )
                value = value + along_lon(turned, flux[flux_of[comp][1], a * 5 + c])
                value = value + mix(
                    [2.0 * DERIV[p][c] for p in range(5)],
                    [flux[flux_of[comp][2], a * 5 + p] for p in range(5)],
                )
                base = (comp * 5 + a) * 8
                elems[c, base : base + 8, :] = value
    carried = jnp.where(lane > 0, pltpu.roll(elems[4], 1, 1), 0.0)
    merged = jnp.concatenate([elems[0] + carried, elems[1], elems[2], elems[3]], 1)
    parts = jnp.concatenate(split3(merged), 0)
    given = jnp.dot(parts, perm[...], preferred_element_type=F32)
    given = given[0:128] + given[128:256] + given[256:384]
    lat_force[12:16, :] = jnp.zeros((4, 512), F32)
    lon_force[15:16, :] = jnp.zeros((1, 512), F32)
    corner_force[...] = jnp.zeros((8, 512), F32)
    for comp in range(3):
        for a in range(5):
            base = (comp * 5 + a) * 8
            if a < 4:
                force[comp, a] = given[base : base + 4]
                lon_force[5 * comp + a : 5 * comp + a + 1, :] = given[base + 4 : base + 5]
            else:
                lat_force[4 * comp : 4 * comp + 4, :] = given[base : base + 4]
                lon_force[5 * comp + 4 : 5 * comp + 5, :] = given[base + 4 : base + 5]
                corner_force[comp : comp + 1, :] = given[base + 4 : base + 5]


def call(kernel, name, outs, ins, args, scratch=(), flops=1000000, moved=500000):
    return pl.pallas_call(
        kernel,
        name=name,
        out_shape=[jax.ShapeDtypeStruct(s, d) for s, d in outs],
        in_specs=ins,
        out_specs=[VMEM] * len(outs),
        scratch_shapes=list(scratch),
        compiler_params=pltpu.CompilerParams(vmem_limit_bytes=24 * 1024 * 1024),
        cost_estimate=pl.CostEstimate(flops=flops, bytes_accessed=moved, transcendentals=0),
    )(*args)


def lat_ring(array, by):
    return lax.ppermute(array, "lat", [(i, (i + by) % LAT) for i in range(LAT)])


def lon_ring(array, by):
    return lax.ppermute(array, "lon", [(i, (i + by) % LON) for i in range(LON)])


def diagonal(array):
    pairs = [
        (e * LON + f, (e + 1) % LAT * LON + (f + 1) % LON)
        for e in range(LAT)
        for f in range(LON)
    ]
    return lax.ppermute(array, AXES, pairs)


def star(up_lat, down_lat, up_lon, down_lon):
    return (lat_ring(up_lat, 1), lat_ring(down_lat, -1), lon_ring(up_lon, 1), lon_ring(down_lon, -1))


def per_device(
    displacement, velocity, acceleration, potential, memory_vars, materials, shell_flags,
    moduli, densities, decay, strength,
):
    field = ((4, 4, 512), F32)
    vector = ((3, 4, 4, 512), F32)
    r8, r16, r24, r32 = (((n, 512), F32) for n in (8, 16, 24, 32))
    disp_new, *sent, code = call(
        start_kernel, "start", [vector, r16, r16, r16, r16, r8], [VMEM] * 6,
        (displacement, velocity, acceleration, potential, materials, shell_flags),
    )
    halo_a = star(*sent)
    diag_code = diagonal(code)
    coef, rho_coef, precond, w0, *sent = call(
        residual_kernel, "residual", [r32, r32, field, field, r8, r8, r8, r8],
        [VMEM] * 8 + [SMEM],
        (disp_new, potential, code, *halo_a, diag_code, densities),
    )
    halo_b = star(*sent)
    w1, *sent = call(
        functools.partial(next_kernel, False), "second", [field, r8, r8, r8, r8], [VMEM] * 7,
        (w0, coef, precond, *halo_b),
    )
    halo_c = star(*sent)
    memory = memory_vars.reshape(3, 5, 5, 5, 5, 128).transpose(1, 2, 3, 4, 0, 5)
    memory_new, force, lat_force, lon_force, corner_force = call(
        elastic_kernel, "elastic",
        [((5, 5, 5, 5, 3, 128), BF16), vector, r16, r16, r8],
        [VMEM] * 5 + [SMEM] * 3 + [VMEM],
        (disp_new, halo_a[1], halo_a[3], halo_b[1], materials, moduli, decay, strength, memory),
        [
            pltpu.VMEM((128, 512), F32),
            pltpu.VMEM((5, 128, 128), F32),
            pltpu.VMEM((40, 128), F32),
            pltpu.VMEM((25, 8, 128), F32),
            pltpu.VMEM((160, 128), F32),
            pltpu.VMEM((160, 128), F32),
            pltpu.VMEM((6, 25, 8, 128), F32),
            pltpu.VMEM((512, 512), BF16),
        ],
        flops=20000000, moved=2000000,
    )
    w2, *sent = call(
        functools.partial(next_kernel, True), "third", [field, r24, r8, r24, r8], [VMEM] * 9,
        (w1, coef, precond, *halo_c, lat_force, lon_force),
    )
    halo_d = star(*sent)
    corner = diagonal(corner_force)
    (line,) = call(
        moment_kernel, "moments", [((LAT * LON, 128), F32)], [VMEM] * 9,
        (w0, w1, w2, coef, precond, *halo_d),
    )
    moments = lax.all_to_all(line, AXES, 0, 0, tiled=True)
    phi_new, acc_new, vel_new = call(
        final_kernel, "final", [field, vector, vector], [VMEM] * 26,
        (
            moments, potential, w0, w1, w2, rho_coef, force, corner,
            *(halo[k] for k in range(4) for halo in (halo_a, halo_b, halo_c, halo_d)),
            velocity, acceleration,
        ),
    )
    memory_new = memory_new.transpose(4, 0, 1, 2, 3, 5).reshape(memory_vars.shape)
    return (disp_new, vel_new, acc_new, phi_new, memory_new)


def solution(mesh):
    vector = P(None, "lat", "lon", None)
    scalar = P("lat", "lon", None)
    memory = P(None, None, None, "lat", None, "lon", None, None)
    return jax.shard_map(
        per_device,
        mesh=mesh,
        in_specs=(vector, vector, vector, scalar, memory, scalar, scalar, P(), P(), P(), P()),
        out_specs=(vector, vector, vector, scalar, memory),
        check_vma=False,
    )
```

```python
import jax
import jax.numpy as jnp
import numpy as np
from jax import lax
from jax.experimental import pallas as pl
from jax.experimental.pallas import tpu as pltpu
from jax.sharding import PartitionSpec as P

TIME_STEP = 0.1
F32 = jnp.float32
BF16 = jnp.bfloat16
LAT, LON = 8, 32
AXES = ("lat", "lon")
VMEM = pl.BlockSpec(memory_space=pltpu.VMEM)
HBM = pl.BlockSpec(memory_space=pltpu.HBM)


def gll():
    points = np.array([-1.0, -np.sqrt(3.0 / 7.0), 0.0, np.sqrt(3.0 / 7.0), 1.0])
    weights = np.array([0.1, 49.0 / 90.0, 32.0 / 45.0, 49.0 / 90.0, 0.1])
    differ = points[:, None] - points[None, :] + np.eye(5)
    factors = np.prod(differ, axis=1)
    deriv = factors[:, None] / factors[None, :] / differ * (1.0 - np.eye(5))
    deriv = deriv - np.eye(5) * np.sum(deriv, axis=1)[:, None]
    return deriv, weights


DERIV, WEIGHTS = gll()
W = [float(v) for v in WEIGHTS]
M_POISSON = (DERIV.T @ np.diag(WEIGHTS) @ DERIV).tolist()
M_SOURCE = (np.diag(WEIGHTS) @ DERIV).T.tolist()
M_GRAVITY = (np.diag(WEIGHTS) @ DERIV).tolist()


def lanes(shape):
    return lax.broadcasted_iota(jnp.int32, shape, len(shape) - 1)


def sublanes(shape):
    return lax.broadcasted_iota(jnp.int32, shape, len(shape) - 2)


def by_index(index, values):
    out = jnp.full(index.shape, float(values[-1]), F32)
    for pos in range(len(values) - 2, -1, -1):
        out = jnp.where(index == pos, float(values[pos]), out)
    return out


def column(values, rows=4, width=512):
    return by_index(sublanes((rows, width)), list(values))


def row_of(array, pos, rows=4):
    return jnp.broadcast_to(array[pos : pos + 1], (rows, array.shape[1]))


def radial(field, matrix):
    lane = lanes((4, 512))
    node = lane & 3
    own, before = None, None
    for shift in range(-4, 5):
        moved = field if shift == 0 else pltpu.roll(field, (-shift) % 512, 1)
        if shift > -4:
            factors = [
                matrix[c][c + shift] if 0 <= c + shift <= 4 else 0.0 for c in range(4)
            ]
            table = by_index(node, factors)
            if shift > 0:
                table = jnp.where(lane < 512 - shift, table, 0.0)
            own = table * moved if own is None else own + table * moved
        if shift <= 0:
            term = float(matrix[4][4 + shift]) * moved
            before = term if before is None else before + term
    return own, before


def mix(matrix_row, arrays):
    total = None
    for factor, array in zip(matrix_row, arrays):
        term = float(factor) * array
        total = term if total is None else total + term
    return total


def lat_part(fields, above, below, matrix, own_row, back_row):
    out = []
    for i in range(4):
        value = own_row * mix(matrix[i], fields + [above])
        if i == 0:
            value = value + back_row * (float(matrix[4][4]) * fields[0] + below)
        out.append(value)
    return out


def lon_part(fields, above, below, matrix, own_col, back_col):
    columns = [column([matrix[b][p] for b in range(4)]) for p in range(5)]
    first = column([1.0, 0.0, 0.0, 0.0])
    out = []
    for i in range(4):
        value = columns[4] * row_of(above, i)
        for p in range(4):
            value = value + columns[p] * row_of(fields[i], p)
        edge = float(matrix[4][4]) * fields[i][0:1] + below[i : i + 1]
        kind = min(i, 1)
        value = own_col[kind] * value + first * (back_col[kind] * edge)
        out.append(W[i] * value)
    return out


def radial_part(fields, matrix, own, before):
    out = []
    for i in range(4):
        first, second = radial(fields[i], matrix)
        kind = min(i, 1)
        out.append(W[i] * (own[kind] * first + before[kind] * second))
    return out


def partial_lat(fields, matrix):
    return mix(matrix[4][:4], fields)


def partial_lon(field, matrix):
    weighted = column(matrix[4][:4]) * field
    return jnp.sum(weighted, axis=0, keepdims=True)


def even(axis):
    return lax.rem(lax.axis_index(axis), 2) == 0


def pick(axis, for_even, for_odd):
    return jnp.where(even(axis), for_even, for_odd)


def post(axis, outs, up, down):
    for out, sent in zip(outs, (pick(axis, up, down), pick(axis, down, up))):
        out[...] = sent[: out.shape[0]]


def arrived(axis, first, second):
    height = min(first.shape[0], second.shape[0])
    first, second = first[0:height], second[0:height]
    return pick(axis, second, first), pick(axis, first, second)


def stack(rows, height):
    total = sum(r.shape[0] for r in rows)
    if total < height:
        rows = rows + [jnp.zeros((height - total, 512), F32)]
    return jnp.concatenate(rows, 0)


def messages(fields, lat_out, lon_out, extra_lat=(), extra_lon=()):
    up = [partial_lat(fields, M_POISSON), partial_lat(fields, M_GRAVITY)]
    height = max(out.shape[0] for out in lat_out)
    post("lat", lat_out, stack(up + list(extra_lat), height), stack([fields[0]], height))
    up = [partial_lon(fields[i], M_POISSON) for i in range(4)]
    up += [partial_lon(fields[i], M_GRAVITY) for i in range(4)]
    down = [fields[i][0:1] for i in range(4)]
    height = max(out.shape[0] for out in lon_out)
    post("lon", lon_out, stack(up + list(extra_lon), height), stack(down, height))


def has_next():
    return jnp.where(lax.axis_index("lat") < LAT - 1, 1.0, 0.0).astype(F32)


def has_before():
    return jnp.where(lax.axis_index("lat") > 0, 1.0, 0.0).astype(F32)


def start_kernel(
    disp_h, vel_h, acc_h, phi_h, mat_h, flag_h, dens_h,
    disp_new, disp_out, phi_out, info_out, lon0, lon1,
    disp, vel, acc, mat, flag, dens, sems,
):
    moves = [
        pltpu.make_async_copy(src, dst, sems.at[n])
        for n, (src, dst) in enumerate(
            [
                (mat_h, mat), (flag_h, flag), (dens_h, dens), (phi_h, phi_out),
                (disp_h, disp), (vel_h, vel), (acc_h, acc),
            ]
        )
    ]
    for move in moves:
        move.start()
    for move in moves[:3]:
        move.wait()
    rho = jnp.zeros((1, 128), F32)
    for m in range(8):
        rho = jnp.where(mat[0] == m, dens[m], rho)
    shell = 1.0 + flag[0].astype(F32)
    info = jnp.concatenate([rho, shell, jnp.zeros((1, 256), F32)], 1)
    info_out[...] = jnp.concatenate([rho, shell, jnp.zeros((6, 128), F32)], 0)
    moves[3].wait()
    potential = [phi_out[i] for i in range(4)]
    for move in moves[4:]:
        move.wait()
    u = []
    for comp in range(3):
        planes = []
        for i in range(4):
            value = (
                disp[comp, i]
                + TIME_STEP * vel[comp, i]
                + 0.5 * TIME_STEP * TIME_STEP * acc[comp, i]
            )
            disp_new[comp, i] = value
            disp_out[comp, i] = value
            planes.append(value)
        u.append(planes)
    up = [partial_lon(u[1][i], M_SOURCE) for i in range(4)]
    up += [partial_lon(potential[i], M_POISSON) for i in range(4)]
    up += [partial_lon(potential[i], M_GRAVITY) for i in range(4)]
    down = [u[comp][i][0:1] for comp in range(3) for i in range(4)]
    down += [potential[i][0:1] for i in range(4)]
    post("lon", (lon0, lon1), stack(up + [info], 24), stack(down, 24))

def pack_kernel(disp, phi, own_info, lon_first, lon_second, _, lat0, lat1):
    below, above = arrived("lon", lon_first, lon_second)
    potential = [phi[i] for i in range(4)]
    info = jnp.concatenate(
        [own_info[0:1, :], own_info[1:2, :], jnp.zeros((1, 256), F32)], 1
    )
    up = [
        partial_lat([disp[0, i] for i in range(4)], M_SOURCE),
        partial_lat(potential, M_POISSON),
        partial_lat(potential, M_GRAVITY),
        info,
        below[12:13],
    ]
    down = [disp[0, 0], disp[1, 0], disp[2, 0], potential[0]]
    down += [above[4 * comp : 4 * comp + 1] for comp in range(3)]
    post("lat", (lat0, lat1), stack(up, 24), stack(down, 24))


def lat_rows(factor):
    cols, first = column(W[:4]), column([W[0], 0.0, 0.0, 0.0])
    own = cols * row_of(factor, 0) + first * row_of(factor, 2)
    back = cols * row_of(factor, 1) + first * row_of(factor, 3)
    return own, back


def lon_cols(factor):
    own = (factor[0:1] + factor[1:2], factor[0:1])
    back = (factor[2:3] + factor[3:4], factor[2:3])
    return own, back


def residual_kernel(
    disp_new, phi, own_info, lat_first, lat_second, lon_first, lon_second,
    coef, rho_coef, precond_out, w0_out, lat0, lat1, lon0, lon1,
):
    following, before = has_next(), has_before()
    lat_below, lat_above = arrived("lat", lat_first, lat_second)
    lon_below, lon_above = arrived("lon", lon_first, lon_second)
    rho, shell = (
        jnp.concatenate(
            [
                own_info[n : n + 1, :],
                before * lat_below[12:13, 128 * n : 128 * n + 128],
                lon_below[12:13, 128 * n : 128 * n + 128],
                before * lat_below[13:14, 128 * n : 128 * n + 128],
            ],
            0,
        )
        for n in range(2)
    )
    spread = (
        lax.broadcasted_iota(jnp.int32, (128, 512), 1) // 4
        == lax.broadcasted_iota(jnp.int32, (128, 512), 0)
    )
    spread = jnp.where(spread, 1.0, 0.0).astype(BF16)
    high, mid, low = split3(rho)
    parts = jnp.concatenate(
        [high.astype(F32), mid.astype(F32), low.astype(F32), shell], 0
    ).astype(BF16)
    parts = jnp.dot(parts, spread, preferred_element_type=F32)
    rho = parts[0:4] + parts[4:8] + parts[8:12]
    shell = parts[12:16]
    flagged = shell > 1.5
    valid = shell > 0.5
    stretch = jnp.where(valid, jnp.where(flagged, 3.0, 1.0), 0.0)
    inverse = jnp.where(valid, jnp.where(flagged, 1.0 / 3.0, 1.0), 0.0)
    rho_in = jnp.where(flagged, 0.0, rho)
    lane = lanes((4, 512))
    node = lane & 3
    joint = jnp.logical_and(node == 0, lane >= 4)
    weight = by_index(node, W[:4])

    def earlier(factor):
        return jnp.where(joint, pltpu.roll(factor, 4, 1), 0.0)

    def weighted(factor):
        return weight * factor + W[4] * earlier(factor)

    s_points = 0.5 * weighted(stretch)
    s_own, s_back = lat_rows(s_points)
    s_col, s_col_back = lon_cols(s_points)
    i_own, i_back = lat_rows(0.5 * inverse)
    j_own, j_back = lat_rows(0.5 * earlier(inverse))
    i_both, j_both = (i_own + i_back, i_own), (j_own + j_back, j_own)
    coef[0:4, :] = s_own
    coef[4:8, :] = s_back
    coef[8:12, :] = i_both[0]
    coef[12:16, :] = i_both[1]
    coef[16:20, :] = j_both[0]
    coef[20:24, :] = j_both[1]
    coef[24:25, :] = s_col[0]
    coef[25:26, :] = s_col[1]
    coef[26:27, :] = s_col_back[0]
    coef[27:28, :] = s_col_back[1]
    r_points = 0.25 * weighted(rho)
    r_own, r_back = lat_rows(r_points)
    r_col, r_col_back = lon_cols(r_points)
    scaled = 0.25 * rho * inverse
    g_own, g_back = lat_rows(scaled)
    h_own, h_back = lat_rows(earlier(scaled))
    rho_coef[0:4, :] = r_own
    rho_coef[4:8, :] = r_back
    rho_coef[8:12, :] = g_own + g_back
    rho_coef[12:16, :] = g_own
    rho_coef[16:20, :] = h_own + h_back
    rho_coef[20:24, :] = h_own
    rho_coef[24:25, :] = r_col[0]
    rho_coef[25:26, :] = r_col[1]
    rho_coef[26:27, :] = r_col_back[0]
    rho_coef[27:28, :] = r_col_back[1]
    q_points = 0.25 * weighted(rho_in)
    q_own, q_back = lat_rows(q_points)
    q_col, q_col_back = lon_cols(q_points)
    t_own, t_back = lat_rows(0.25 * rho_in)
    v_own, v_back = lat_rows(0.25 * earlier(rho_in))

    u = [[disp_new[comp, i] for i in range(4)] for comp in range(3)]
    potential = [phi[i] for i in range(4)]
    source_x = lat_part(
        u[0], following * lat_above[0:4, :], lat_below[0:4, :], M_SOURCE, q_own, q_back
    )
    source_y = lon_part(
        u[1], lon_above[4:8, :], lon_below[0:4, :], M_SOURCE, q_col, q_col_back
    )
    source_z = radial_part(u[2], M_SOURCE, (t_own + t_back, t_own), (v_own + v_back, v_own))
    image_x = lat_part(
        potential, following * lat_above[12:16, :], lat_below[4:8, :], M_POISSON, s_own, s_back
    )
    image_y = lon_part(
        potential, lon_above[12:16, :], lon_below[4:8, :], M_POISSON, s_col, s_col_back
    )
    image_z = radial_part(potential, M_POISSON, i_both, j_both)
    diag = [M_POISSON[a][a] for a in range(5)]
    diag_node = by_index(node, diag[:4])
    diag_col = column(diag[:4])
    first = column([1.0, 0.0, 0.0, 0.0])
    w0 = []
    for i in range(4):
        kind = min(i, 1)
        precond = diag[i] * s_own
        if i == 0:
            precond = precond + diag[4] * s_back
        precond = precond + W[i] * (
            diag_col * s_col[kind]
            + first * (diag[4] * s_col_back[kind])
            + i_both[kind] * diag_node
            + diag[4] * j_both[kind]
        )
        precond_out[i] = precond
        source = -(source_x[i] + source_y[i] + source_z[i])
        image = image_x[i] + image_y[i] + image_z[i]
        value = (source - image) / precond
        w0_out[i] = value
        w0.append(value)
    messages(w0, (lat0, lat1), (lon0, lon1))


def poisson(fields, coef, lat_first, lat_second, lon_first, lon_second):
    following = has_next()
    lat_below, lat_above = arrived("lat", lat_first, lat_second)
    lon_below, lon_above = arrived("lon", lon_first, lon_second)
    s_col = (coef[24:25, :], coef[25:26, :])
    s_col_back = (coef[26:27, :], coef[27:28, :])
    x = lat_part(
        fields, following * lat_above[0:4, :], lat_below[0:4, :], M_POISSON, coef[0:4, :], coef[4:8, :]
    )
    y = lon_part(fields, lon_above[0:4, :], lon_below[0:4, :], M_POISSON, s_col, s_col_back)
    z = radial_part(
        fields, M_POISSON, (coef[8:12, :], coef[12:16, :]), (coef[16:20, :], coef[20:24, :])
    )
    return [x[i] + y[i] + z[i] for i in range(4)]


def step(field, coef, precond, halo, out):
    fields = [field[i] for i in range(4)]
    image = poisson(fields, coef, *halo)
    result = []
    for i in range(4):
        value = image[i] / precond[i] - fields[i]
        out[i] = value
        result.append(value)
    return result


def second_kernel(
    field, coef, precond, lat_first, lat_second, lon_first, lon_second, lon_force,
    out, lat0, lat1, lon0, lon1,
):
    result = step(field, coef, precond, (lat_first, lat_second, lon_first, lon_second), out)
    messages(result, (lat0, lat1), (lon0, lon1), (), (lon_force[...],))


def third_kernel(
    field, coef, precond, lat_first, lat_second, lon_first, lon_second, lat_force,
    out, lat0, lat1, lon0, lon1,
):
    result = step(field, coef, precond, (lat_first, lat_second, lon_first, lon_second), out)
    below, _ = arrived("lon", lon_first, lon_second)
    first = column([1.0, 0.0, 0.0, 0.0])
    edges = []
    for comp in range(3):
        corner = 12 + 5 * comp
        edges.append(
            lat_force[4 * comp : 4 * comp + 4, :] + first * below[corner : corner + 1]
        )
    messages(result, (lat0, lat1), (lon0, lon1), edges)


def moment_kernel(w0, w1, w2, coef, precond, lat_first, lat_second, lon_first, lon_second, out):
    fields = [w2[i] for i in range(4)]
    image = poisson(fields, coef, lat_first, lat_second, lon_first, lon_second)
    sums = [None] * 6
    for i in range(4):
        m = precond[i]
        a, b, c = w0[i], w1[i], w2[i]
        ma, mb, mc = m * a, m * b, m * c
        terms = [a * ma, b * ma, b * mb, c * mb, c * mc, c * (image[i] - mc)]
        for k in range(6):
            sums[k] = terms[k] if sums[k] is None else sums[k] + terms[k]
    lane = lanes((1, 128))
    line = jnp.zeros((1, 128), F32)
    for k in range(6):
        total = jnp.sum(jnp.sum(sums[k], axis=0, keepdims=True), axis=1, keepdims=True)
        line = jnp.where(lane == k, total, line)
    out[...] = jnp.broadcast_to(line, out.shape)


def cg_coefficients(mu):
    zero = jnp.zeros_like(mu[0])

    def inner(a):
        total = zero
        for i in range(len(a)):
            for j in range(len(a)):
                total = total + a[i] * a[j] * mu[i + j]
        return total

    def energy(a):
        total = zero
        for i in range(len(a)):
            for j in range(len(a)):
                total = total + a[i] * a[j] * (mu[i + j + 1] + mu[i + j])
        return total

    def ratio(a, b):
        return jnp.where(b == 0.0, 0.0, a / jnp.where(b == 0.0, 1.0, b))

    y = [zero, zero, zero]
    z = [zero + 1.0]
    search = [zero + 1.0]
    rz = mu[0]
    for step in range(3):
        length = ratio(rz, energy(search))
        for i in range(len(search)):
            y[i] = y[i] + length * search[i]
        if step < 2:
            grown = [zero] * (len(search) + 1)
            for i in range(len(search)):
                grown[i] = grown[i] + search[i]
                grown[i + 1] = grown[i + 1] + search[i]
            z = z + [zero]
            z = [z[i] - length * grown[i] for i in range(len(z))]
            rz_next = inner(z)
            beta = ratio(rz_next, rz)
            padded = search + [zero]
            search = [z[i] + beta * padded[i] for i in range(len(z))]
            rz = rz_next
    return y


def final_kernel(
    moments, phi, w0, w1, w2, rho_coef, own_force,
    a0, a1, a2, a3, b0, b1, b2, b3, c0, c1, c2, c3, d0, d1, d2, d3,
    vel, acc, phi_new, acc_new, vel_new,
):
    total = jnp.sum(moments[...], axis=0, keepdims=True)
    lane = lanes((1, 128))
    mu = [
        jnp.broadcast_to(
            jnp.sum(jnp.where(lane == k, total, 0.0), axis=1, keepdims=True), (1, 128)
        )
        for k in range(6)
    ]
    y = cg_coefficients(mu)
    y = [jnp.concatenate([v] * 4, 1) for v in y]

    def combined(first, one, two, three):
        return first + y[0] * one + y[1] * two + y[2] * three

    potential = []
    for i in range(4):
        value = combined(phi[i], w0[i], w1[i], w2[i])
        phi_new[i] = value
        potential.append(value)
    following, before = has_next(), has_before()
    ma, na = arrived("lat", a0, a1)
    mb, nb = arrived("lat", b0, b1)
    mc, nc = arrived("lat", c0, c1)
    md, nd = arrived("lat", d0, d1)
    fa, ga = arrived("lon", a2, a3)
    fb, gb = arrived("lon", b2, b3)
    fc, gc = arrived("lon", c2, c3)
    fd, gd = arrived("lon", d2, d3)
    lat_below = combined(ma[8:12, :], mb[4:8, :], mc[4:8, :], md[4:8, :])
    lat_above = following * combined(na[12:16, :], nb[0:4, :], nc[0:4, :], nd[0:4, :])
    lon_below = combined(fa[8:12, :], fb[4:8, :], fc[4:8, :], fd[4:8, :])
    lon_above = combined(ga[12:16, :], gb[0:4, :], gc[0:4, :], gd[0:4, :])
    r_own, r_back = rho_coef[0:4, :], rho_coef[4:8, :]
    r_col = (rho_coef[24:25, :], rho_coef[25:26, :])
    r_col_back = (rho_coef[26:27, :], rho_coef[27:28, :])
    x = lat_part(potential, lat_above, lat_below, M_GRAVITY, r_own, r_back)
    y_part = lon_part(potential, lon_above, lon_below, M_GRAVITY, r_col, r_col_back)
    z = radial_part(
        potential,
        M_GRAVITY,
        (rho_coef[8:12, :], rho_coef[12:16, :]),
        (rho_coef[16:20, :], rho_coef[20:24, :]),
    )
    cols = column(W[:4])
    first = column([1.0, 0.0, 0.0, 0.0])
    gravity = (x, y_part, z)
    for i in range(4):
        mass = r_own + r_back if i == 0 else r_own
        mass = 0.5 * W[i] * mass
        for comp in range(3):
            force = own_force[comp, i]
            force = force + first * fc[8 + 5 * comp + i : 9 + 5 * comp + i, :]
            if i == 0:
                edge = md[8 + 4 * comp : 12 + 4 * comp, :]
                force = force + before * edge
            value = (-gravity[comp][i] - force) / mass
            acc_new[comp, i] = value
            vel_new[comp, i] = vel[comp, i] + 0.5 * TIME_STEP * (acc[comp, i] + value)


def split3(value):
    high = value.astype(BF16)
    rest = value - high.astype(F32)
    mid = rest.astype(BF16)
    low = (rest - mid.astype(F32)).astype(BF16)
    return high, mid, low


def prepare_kernel(
    disp, mat_h, moduli_h, decay_h, strength_h, stiff, rates, perm, elems,
    points, mat, moduli, decay, strength, sems,
):
    moves = [
        pltpu.make_async_copy(src, dst, sems.at[n])
        for n, (src, dst) in enumerate(
            [(mat_h, mat), (moduli_h, moduli), (decay_h, decay), (strength_h, strength)]
        )
    ]
    for move in moves:
        move.start()
    for c in range(4):
        hit = lax.broadcasted_iota(jnp.int32, (128, 512), 1) == (
            4 * lax.broadcasted_iota(jnp.int32, (128, 512), 0) + c
        )
        perm[128 * c : 128 * c + 128, :] = jnp.where(hit, 1.0, 0.0).astype(BF16)
    points[...] = jnp.zeros(points.shape, F32)
    for comp in range(3):
        for a in range(4):
            base = (comp * 4 + a) * 8
            points[base : base + 4, :] = disp[comp, a]
    to_nodes(points[...], perm, elems)
    for move in moves:
        move.wait()
    onehot = [mat[0] == m for m in range(8)]
    for k in range(6):
        for l in range(k, 6):
            value = jnp.zeros((1, 128), F32)
            for m in range(8):
                value = jnp.where(onehot[m], moduli[k, m, l], value)
            stiff[6 * k + l : 6 * k + l + 1, :] = value
    for l in range(3):
        rates[l : l + 1, :] = jnp.full((1, 128), decay[l], F32)
        rates[3 + l : 4 + l, :] = jnp.full((1, 128), (1.0 - decay[l]) * strength[l], F32)


def to_nodes(points, perm, elems):
    rows = points.shape[0]
    parts = jnp.concatenate(split3(points), 0)
    taken = lax.dot_general(
        parts, perm[...], (((1,), (1,)), ((), ())), preferred_element_type=F32
    )
    taken = taken[0:rows] + taken[rows : 2 * rows] + taken[2 * rows : 3 * rows]
    for c in range(4):
        elems[c] = taken[:, 128 * c : 128 * c + 128]
    lane = lanes((rows, 128))
    elems[4] = jnp.where(lane < 127, pltpu.roll(taken[:, 0:128], 127, 1), 0.0)


def elastic_kernel(
    lat_first, lat_second, lon_first, lon_second, stiff, rates, perm, own, memory,
    memory_new, force, lat_force, lon_force,
    points, edge, elems, devs, old, new, flux,
):
    following = has_next()
    _, lat_above = arrived("lat", lat_first, lat_second)
    _, lon_above = arrived("lon", lon_first, lon_second)
    points[...] = jnp.zeros(points.shape, F32)
    for comp in range(3):
        points[8 * comp : 8 * comp + 4, :] = following * lat_above[4 * comp : 4 * comp + 4]
        points[8 * comp + 4 : 8 * comp + 5, :] = following * lat_above[16 + comp : 17 + comp]
    points[24:36, :] = lon_above[0:12]
    to_nodes(points[...], perm, edge)
    fifth = sublanes((8, 128)) == 4
    for c in range(5):
        for comp in range(3):
            for a in range(4):
                base, row = (comp * 5 + a) * 8, 24 + 4 * comp + a
                kept = own[c, (comp * 4 + a) * 8 : (comp * 4 + a) * 8 + 8, :]
                elems[c, base : base + 8, :] = jnp.where(
                    fifth, row_of(edge[c, 24:40, :], row - 24, 8), kept
                )
            base = (comp * 5 + 4) * 8
            elems[c, base : base + 8, :] = edge[c, 8 * comp : 8 * comp + 8, :]
    lane = lanes((128, 128))
    slopes = [
        by_index(sublanes((8, 128)), [2.0 * DERIV[b][p] for b in range(5)] + [0.0])
        for p in range(5)
    ]
    turned = [
        by_index(sublanes((8, 128)), [2.0 * DERIV[p][b] for b in range(5)] + [0.0])
        for p in range(5)
    ]
    weight_col = by_index(sublanes((8, 128)), W + [0.0])

    def slab(comp, a, c):
        base = (comp * 5 + a) * 8
        return elems[c, base : base + 8, :]

    def along_lon(cols, value):
        total = None
        for p in range(5):
            term = cols[p] * row_of(value, p, 8)
            total = term if total is None else total + term
        return total

    for a in range(5):
        elastic_of = []
        for c in range(5):
            dx, dy, dz = [], [], []
            for comp in range(3):
                dx.append(mix([2.0 * DERIV[a][p] for p in range(5)], [slab(comp, p, c) for p in range(5)]))
                dy.append(along_lon(slopes, slab(comp, a, c)))
                dz.append(mix([2.0 * DERIV[c][p] for p in range(5)], [slab(comp, a, p) for p in range(5)]))
            strain = [dx[0], dy[1], dz[2], dy[0] + dx[1], dz[0] + dx[2], dz[1] + dy[2]]
            elastic = []
            for k in range(6):
                total = None
                for l in range(6):
                    pos = 6 * min(k, l) + max(k, l)
                    term = stiff[pos : pos + 1, :] * strain[l]
                    total = term if total is None else total + term
                elastic.append(total)
            pressure = (elastic[0] + elastic[1] + elastic[2]) * (1.0 / 3.0)
            dev = [elastic[0] - pressure, elastic[1] - pressure, elastic[3], elastic[4], elastic[5]]
            for d in range(5):
                devs[d * 5 + c] = dev[d]
            elastic_of.append(elastic)
        relaxed = []
        for d in range(5):
            for b in range(5):
                for c in range(5):
                    row = (b * 5 + c) * 4
                    old[row : row + 3, :] = memory[d, a, b, c].astype(F32)
            sums = []
            for c in range(5):
                dev = devs[d * 5 + c]
                total = None
                for l in range(3):
                    was = old[pl.ds(4 * c + l, 8, stride=20), :]
                    now = rates[l : l + 1, :] * was + rates[3 + l : 4 + l, :] * dev
                    now = now.astype(BF16).astype(F32)
                    new[pl.ds(4 * c + l, 8, stride=20), :] = now
                    total = now if total is None else total + now
                sums.append(total)
            for b in range(5):
                for c in range(5):
                    row = (b * 5 + c) * 4
                    memory_new[d, a, b, c] = new[row : row + 3, :].astype(BF16)
            relaxed.append(sums)
        for c in range(5):
            e = elastic_of[c]
            r = [relaxed[d][c] for d in range(5)]
            weight = weight_col * (W[a] * W[c] / 8.0)
            stress = [e[0] - r[0], e[1] - r[1], e[2] + r[0] + r[1], e[3] - r[2], e[4] - r[3], e[5] - r[4]]
            for k in range(6):
                flux[k, a * 5 + c] = jnp.where(weight_col > 0.0, weight * stress[k], 0.0)
    flux_of = [[0, 3, 4], [3, 1, 5], [4, 5, 2]]
    for c in range(5):
        elems[c, 120:128, :] = jnp.zeros((8, 128), F32)
        for comp in range(3):
            for a in range(5):
                value = mix(
                    [2.0 * DERIV[p][a] for p in range(5)],
                    [flux[flux_of[comp][0], p * 5 + c] for p in range(5)],
                )
                value = value + along_lon(turned, flux[flux_of[comp][1], a * 5 + c])
                value = value + mix(
                    [2.0 * DERIV[p][c] for p in range(5)],
                    [flux[flux_of[comp][2], a * 5 + p] for p in range(5)],
                )
                base = (comp * 5 + a) * 8
                elems[c, base : base + 8, :] = value
    carried = jnp.where(lane > 0, pltpu.roll(elems[4], 1, 1), 0.0)
    merged = jnp.concatenate([elems[0] + carried, elems[1], elems[2], elems[3]], 1)
    parts = jnp.concatenate(split3(merged), 0)
    given = jnp.dot(parts, perm[...], preferred_element_type=F32)
    given = given[0:128] + given[128:256] + given[256:384]
    lat_force[12:16, :] = jnp.zeros((4, 512), F32)
    lon_force[15:16, :] = jnp.zeros((1, 512), F32)
    for comp in range(3):
        for a in range(5):
            base = (comp * 5 + a) * 8
            if a < 4:
                force[comp, a] = given[base : base + 4]
                lon_force[5 * comp + a : 5 * comp + a + 1, :] = given[base + 4 : base + 5]
            else:
                lat_force[4 * comp : 4 * comp + 4, :] = given[base : base + 4]
                lon_force[5 * comp + 4 : 5 * comp + 5, :] = given[base + 4 : base + 5]


def call(kernel, name, outs, ins, args, scratch=(), flops=1000000, moved=500000, vmem=24):
    return pl.pallas_call(
        kernel,
        name=name,
        out_shape=[jax.ShapeDtypeStruct(s, d) for s, d in outs],
        in_specs=ins,
        out_specs=[VMEM] * len(outs),
        scratch_shapes=list(scratch),
        compiler_params=pltpu.CompilerParams(vmem_limit_bytes=vmem * 1024 * 1024),
        cost_estimate=pl.CostEstimate(flops=flops, bytes_accessed=moved, transcendentals=0),
    )(*args)


def swap(array, axis, size, parity):
    pairs = []
    for i in range(parity, size, 2):
        j = (i + 1) % size
        pairs += [(i, j), (j, i)]
    return lax.ppermute(array, axis, pairs)


def swap_lat(first, second):
    return swap(first, "lat", LAT, 0), swap(second, "lat", LAT, 1)


def swap_lon(first, second):
    other = swap(second, "lon", LON, 1)
    return swap(first, "lon", LON, 0), other


def per_device(
    displacement, velocity, acceleration, potential, memory_vars, materials, shell_flags,
    moduli, densities, decay, strength,
):
    field = ((4, 4, 512), F32)
    vector = ((3, 4, 4, 512), F32)
    r8, r16, r24, r32 = (((n, 512), F32) for n in (8, 16, 24, 32))
    info = ((8, 128), F32)
    kept = pltpu.with_memory_space_constraint
    disp_new, disp, phi, own_info, *sent = call(
        start_kernel, "start", [vector, vector, field, info, r16, r24], [HBM] * 7,
        [
            kept(array, pltpu.HBM)
            for array in (
                displacement, velocity, acceleration, potential, materials, shell_flags, densities
            )
        ],
        [
            pltpu.VMEM((3, 4, 4, 512), F32),
            pltpu.VMEM((3, 4, 4, 512), F32),
            pltpu.VMEM((3, 4, 4, 512), F32),
            pltpu.VMEM((1, 1, 128), jnp.int32),
            pltpu.VMEM((1, 1, 128), jnp.int32),
            pltpu.SMEM((8,), F32),
            pltpu.SemaphoreType.DMA((7,)),
        ],
    )
    lon_a = swap_lon(*sent)
    tables = call(
        prepare_kernel, "prepare",
        [((40, 128), F32), info, ((512, 512), BF16), ((5, 96, 128), F32)],
        [VMEM] + [HBM] * 4,
        [disp]
        + [
            kept(array, pltpu.HBM)
            for array in (materials, moduli.transpose(1, 0, 2), decay, strength)
        ],
        [
            pltpu.VMEM((96, 512), F32),
            pltpu.VMEM((1, 1, 128), jnp.int32),
            pltpu.SMEM((6, 8, 6), F32),
            pltpu.SMEM((3,), F32),
            pltpu.SMEM((3,), F32),
            pltpu.SemaphoreType.DMA((4,)),
        ],
    )
    lat_a = call(
        pack_kernel, "pack", [r24, r24], [VMEM] * 6,
        (disp, phi, own_info, *lon_a, tables[1]),
    )
    halo_a = (*swap_lat(*lat_a), *lon_a)
    coef, rho_coef, precond, w0, *sent = call(
        residual_kernel, "residual", [r32, r32, field, field, r8, r8, r8, r16], [VMEM] * 7,
        (disp, phi, own_info, *halo_a),
    )
    lon_b = swap_lon(*sent[2:])
    halo_b = (*swap_lat(*sent[:2]), *lon_b)
    memory = memory_vars.reshape(3, 5, 5, 5, 5, 128).transpose(1, 2, 3, 4, 0, 5)
    memory_new, force, lat_force, lon_force = call(
        elastic_kernel, "elastic",
        [((5, 5, 5, 5, 3, 128), BF16), vector, r16, r16],
        [VMEM] * 9,
        (*halo_a, *tables, memory),
        [
            pltpu.VMEM((48, 512), F32),
            pltpu.VMEM((5, 48, 128), F32),
            pltpu.VMEM((5, 128, 128), F32),
            pltpu.VMEM((25, 8, 128), F32),
            pltpu.VMEM((160, 128), F32),
            pltpu.VMEM((160, 128), F32),
            pltpu.VMEM((6, 25, 8, 128), F32),
        ],
        flops=20000000, moved=2000000,
    )
    w1, *sent = call(
        second_kernel, "second", [field, r8, r8, r24, r32], [VMEM] * 8,
        (w0, coef, precond, *halo_b, lon_force),
    )
    lon_c = swap_lon(*sent[2:])
    halo_c = (*swap_lat(*sent[:2]), *lon_c)
    w2, *sent = call(
        third_kernel, "third", [field, r24, r24, r8, r32], [VMEM] * 8,
        (w1, coef, precond, *halo_c, lat_force),
    )
    lon_d = swap_lon(*sent[2:])
    halo_d = (*swap_lat(*sent[:2]), *lon_d)
    (line,) = call(
        moment_kernel, "moments", [((LAT * LON, 128), F32)], [VMEM] * 9,
        (w0, w1, w2, coef, precond, *halo_d),
    )
    moments = lax.all_to_all(line, AXES, 0, 0, tiled=True)
    phi_new, acc_new, vel_new = call(
        final_kernel, "final", [field, vector, vector], [VMEM] * 25,
        (
            moments, phi, w0, w1, w2, rho_coef, force, *halo_a, *halo_b, *halo_c, *halo_d,
            velocity, acceleration,
        ),
    )
    memory_new = memory_new.transpose(4, 0, 1, 2, 3, 5).reshape(memory_vars.shape)
    return (disp_new, vel_new, acc_new, phi_new, memory_new)


def solution(mesh):
    vector = P(None, "lat", "lon", None)
    scalar = P("lat", "lon", None)
    memory = P(None, None, None, "lat", None, "lon", None, None)
    return jax.shard_map(
        per_device,
        mesh=mesh,
        in_specs=(vector, vector, vector, scalar, memory, scalar, scalar, P(), P(), P(), P()),
        out_specs=(vector, vector, vector, scalar, memory),
        check_vma=False,
    )
```

```python
import jax
import jax.numpy as jnp
import numpy as np
from jax import lax
from jax.experimental import pallas as pl
from jax.experimental.pallas import tpu as pltpu
from jax.sharding import PartitionSpec as P

TIME_STEP = 0.1
F32 = jnp.float32
BF16 = jnp.bfloat16
LAT, LON = 8, 32
AXES = ("lat", "lon")
VMEM = pl.BlockSpec(memory_space=pltpu.VMEM)
HBM = pl.BlockSpec(memory_space=pltpu.HBM)


def gll():
    points = np.array([-1.0, -np.sqrt(3.0 / 7.0), 0.0, np.sqrt(3.0 / 7.0), 1.0])
    weights = np.array([0.1, 49.0 / 90.0, 32.0 / 45.0, 49.0 / 90.0, 0.1])
    differ = points[:, None] - points[None, :] + np.eye(5)
    factors = np.prod(differ, axis=1)
    deriv = factors[:, None] / factors[None, :] / differ * (1.0 - np.eye(5))
    deriv = deriv - np.eye(5) * np.sum(deriv, axis=1)[:, None]
    return deriv, weights


DERIV, WEIGHTS = gll()
W = [float(v) for v in WEIGHTS]
M_POISSON = (DERIV.T @ np.diag(WEIGHTS) @ DERIV).tolist()
M_SOURCE = (np.diag(WEIGHTS) @ DERIV).T.tolist()
M_GRAVITY = (np.diag(WEIGHTS) @ DERIV).tolist()


def lanes(shape):
    return lax.broadcasted_iota(jnp.int32, shape, len(shape) - 1)


def sublanes(shape):
    return lax.broadcasted_iota(jnp.int32, shape, len(shape) - 2)


def by_index(index, values):
    out = jnp.full(index.shape, float(values[-1]), F32)
    for pos in range(len(values) - 2, -1, -1):
        out = jnp.where(index == pos, float(values[pos]), out)
    return out


def column(values, rows=4, width=512):
    return by_index(sublanes((rows, width)), list(values))


def row_of(array, pos, rows=4):
    return jnp.broadcast_to(array[pos : pos + 1], (rows, array.shape[1]))


def radial(field, matrix):
    lane = lanes((4, 512))
    node = lane & 3
    own, before = None, None
    for shift in range(-4, 5):
        moved = field if shift == 0 else pltpu.roll(field, (-shift) % 512, 1)
        if shift > -4:
            factors = [
                matrix[c][c + shift] if 0 <= c + shift <= 4 else 0.0 for c in range(4)
            ]
            table = by_index(node, factors)
            if shift > 0:
                table = jnp.where(lane < 512 - shift, table, 0.0)
            own = table * moved if own is None else own + table * moved
        if shift <= 0:
            term = float(matrix[4][4 + shift]) * moved
            before = term if before is None else before + term
    return own, before


def mix(matrix_row, arrays):
    total = None
    for factor, array in zip(matrix_row, arrays):
        term = float(factor) * array
        total = term if total is None else total + term
    return total


def lat_part(fields, above, below, matrix, own_row, back_row):
    out = []
    for i in range(4):
        value = own_row * mix(matrix[i], fields + [above])
        if i == 0:
            value = value + back_row * (float(matrix[4][4]) * fields[0] + below)
        out.append(value)
    return out


def lon_part(fields, above, below, matrix, own_col, back_col):
    columns = [column([matrix[b][p] for b in range(4)]) for p in range(5)]
    first = column([1.0, 0.0, 0.0, 0.0])
    out = []
    for i in range(4):
        value = columns[4] * row_of(above, i)
        for p in range(4):
            value = value + columns[p] * row_of(fields[i], p)
        edge = float(matrix[4][4]) * fields[i][0:1] + below[i : i + 1]
        kind = min(i, 1)
        value = own_col[kind] * value + first * (back_col[kind] * edge)
        out.append(W[i] * value)
    return out


def radial_part(fields, matrix, own, before):
    out = []
    for i in range(4):
        first, second = radial(fields[i], matrix)
        kind = min(i, 1)
        out.append(W[i] * (own[kind] * first + before[kind] * second))
    return out


def partial_lat(fields, matrix):
    return mix(matrix[4][:4], fields)


def partial_lon(field, matrix):
    weighted = column(matrix[4][:4]) * field
    return jnp.sum(weighted, axis=0, keepdims=True)


def even(axis):
    return lax.rem(lax.axis_index(axis), 2) == 0


def pick(axis, for_even, for_odd):
    return jnp.where(even(axis), for_even, for_odd)


def post(axis, outs, up, down):
    for out, sent in zip(outs, (pick(axis, up, down), pick(axis, down, up))):
        out[...] = sent[: out.shape[0]]


def arrived(axis, first, second):
    height = min(first.shape[0], second.shape[0])
    first, second = first[0:height], second[0:height]
    return pick(axis, second, first), pick(axis, first, second)


def stack(rows, height):
    total = sum(r.shape[0] for r in rows)
    if total < height:
        rows = rows + [jnp.zeros((height - total, 512), F32)]
    return jnp.concatenate(rows, 0)


def messages(fields, lat_out, lon_out, extra_lat=(), extra_lon=()):
    up = [partial_lat(fields, M_POISSON), partial_lat(fields, M_GRAVITY)]
    height = max(out.shape[0] for out in lat_out)
    post("lat", lat_out, stack(up + list(extra_lat), height), stack([fields[0]], height))
    up = [partial_lon(fields[i], M_POISSON) for i in range(4)]
    up += [partial_lon(fields[i], M_GRAVITY) for i in range(4)]
    down = [fields[i][0:1] for i in range(4)]
    height = max(out.shape[0] for out in lon_out)
    post("lon", lon_out, stack(up + list(extra_lon), height), stack(down, height))


def has_next():
    return jnp.where(lax.axis_index("lat") < LAT - 1, 1.0, 0.0).astype(F32)


def has_before():
    return jnp.where(lax.axis_index("lat") > 0, 1.0, 0.0).astype(F32)


def start_kernel(
    disp_h, vel_h, acc_h, phi_h, mat_h, flag_h, dens_h,
    disp_new, disp_out, phi_out, info_out, lon0, lon1,
    disp, vel, acc, mat, flag, dens, sems,
):
    moves = [
        pltpu.make_async_copy(src, dst, sems.at[n])
        for n, (src, dst) in enumerate(
            [
                (mat_h, mat), (flag_h, flag), (dens_h, dens), (phi_h, phi_out),
                (disp_h, disp), (vel_h, vel), (acc_h, acc),
            ]
        )
    ]
    for move in moves:
        move.start()
    for move in moves[:3]:
        move.wait()
    rho = jnp.zeros((1, 128), F32)
    for m in range(8):
        rho = jnp.where(mat[0] == m, dens[m], rho)
    shell = 1.0 + flag[0].astype(F32)
    info = jnp.concatenate([rho, shell, jnp.zeros((1, 256), F32)], 1)
    info_out[...] = jnp.concatenate([rho, shell, jnp.zeros((6, 128), F32)], 0)
    moves[3].wait()
    potential = [phi_out[i] for i in range(4)]
    for move in moves[4:]:
        move.wait()
    u = []
    for comp in range(3):
        planes = []
        for i in range(4):
            value = (
                disp[comp, i]
                + TIME_STEP * vel[comp, i]
                + 0.5 * TIME_STEP * TIME_STEP * acc[comp, i]
            )
            disp_new[comp, i] = value
            disp_out[comp, i] = value
            planes.append(value)
        u.append(planes)
    up = [partial_lon(u[1][i], M_SOURCE) for i in range(4)]
    up += [partial_lon(potential[i], M_POISSON) for i in range(4)]
    up += [partial_lon(potential[i], M_GRAVITY) for i in range(4)]
    down = [u[comp][i][0:1] for comp in range(3) for i in range(4)]
    down += [potential[i][0:1] for i in range(4)]
    post("lon", (lon0, lon1), stack(up + [info], 24), stack(down, 24))

def pack_kernel(disp, phi, own_info, lon_first, lon_second, _, lat0, lat1):
    below, above = arrived("lon", lon_first, lon_second)
    potential = [phi[i] for i in range(4)]
    info = jnp.concatenate(
        [own_info[0:1, :], own_info[1:2, :], jnp.zeros((1, 256), F32)], 1
    )
    up = [
        partial_lat([disp[0, i] for i in range(4)], M_SOURCE),
        partial_lat(potential, M_POISSON),
        partial_lat(potential, M_GRAVITY),
        info,
        below[12:13],
    ]
    down = [disp[0, 0], disp[1, 0], disp[2, 0], potential[0]]
    down += [above[4 * comp : 4 * comp + 1] for comp in range(3)]
    post("lat", (lat0, lat1), stack(up, 24), stack(down, 24))


def lat_rows(factor):
    cols, first = column(W[:4]), column([W[0], 0.0, 0.0, 0.0])
    own = cols * row_of(factor, 0) + first * row_of(factor, 2)
    back = cols * row_of(factor, 1) + first * row_of(factor, 3)
    return own, back


def lon_cols(factor):
    own = (factor[0:1] + factor[1:2], factor[0:1])
    back = (factor[2:3] + factor[3:4], factor[2:3])
    return own, back


def residual_kernel(
    disp_new, phi, own_info, lat_first, lat_second, lon_first, lon_second, _,
    coef, rho_coef, precond_out, w0_out, lat0, lat1, lon0, lon1,
):
    following, before = has_next(), has_before()
    lat_below, lat_above = arrived("lat", lat_first, lat_second)
    lon_below, lon_above = arrived("lon", lon_first, lon_second)
    rho, shell = (
        jnp.concatenate(
            [
                own_info[n : n + 1, :],
                before * lat_below[12:13, 128 * n : 128 * n + 128],
                lon_below[12:13, 128 * n : 128 * n + 128],
                before * lat_below[13:14, 128 * n : 128 * n + 128],
            ],
            0,
        )
        for n in range(2)
    )
    spread = (
        lax.broadcasted_iota(jnp.int32, (128, 512), 1) // 4
        == lax.broadcasted_iota(jnp.int32, (128, 512), 0)
    )
    spread = jnp.where(spread, 1.0, 0.0).astype(BF16)
    high, mid, low = split3(rho)
    parts = jnp.concatenate(
        [high.astype(F32), mid.astype(F32), low.astype(F32), shell], 0
    ).astype(BF16)
    parts = jnp.dot(parts, spread, preferred_element_type=F32)
    rho = parts[0:4] + parts[4:8] + parts[8:12]
    shell = parts[12:16]
    flagged = shell > 1.5
    valid = shell > 0.5
    stretch = jnp.where(valid, jnp.where(flagged, 3.0, 1.0), 0.0)
    inverse = jnp.where(valid, jnp.where(flagged, 1.0 / 3.0, 1.0), 0.0)
    rho_in = jnp.where(flagged, 0.0, rho)
    lane = lanes((4, 512))
    node = lane & 3
    joint = jnp.logical_and(node == 0, lane >= 4)
    weight = by_index(node, W[:4])

    def earlier(factor):
        return jnp.where(joint, pltpu.roll(factor, 4, 1), 0.0)

    def weighted(factor):
        return weight * factor + W[4] * earlier(factor)

    s_points = 0.5 * weighted(stretch)
    s_own, s_back = lat_rows(s_points)
    s_col, s_col_back = lon_cols(s_points)
    i_own, i_back = lat_rows(0.5 * inverse)
    j_own, j_back = lat_rows(0.5 * earlier(inverse))
    i_both, j_both = (i_own + i_back, i_own), (j_own + j_back, j_own)
    coef[0:4, :] = s_own
    coef[4:8, :] = s_back
    coef[8:12, :] = i_both[0]
    coef[12:16, :] = i_both[1]
    coef[16:20, :] = j_both[0]
    coef[20:24, :] = j_both[1]
    coef[24:25, :] = s_col[0]
    coef[25:26, :] = s_col[1]
    coef[26:27, :] = s_col_back[0]
    coef[27:28, :] = s_col_back[1]
    r_points = 0.25 * weighted(rho)
    r_own, r_back = lat_rows(r_points)
    r_col, r_col_back = lon_cols(r_points)
    scaled = 0.25 * rho * inverse
    g_own, g_back = lat_rows(scaled)
    h_own, h_back = lat_rows(earlier(scaled))
    rho_coef[0:4, :] = r_own
    rho_coef[4:8, :] = r_back
    rho_coef[8:12, :] = g_own + g_back
    rho_coef[12:16, :] = g_own
    rho_coef[16:20, :] = h_own + h_back
    rho_coef[20:24, :] = h_own
    rho_coef[24:25, :] = r_col[0]
    rho_coef[25:26, :] = r_col[1]
    rho_coef[26:27, :] = r_col_back[0]
    rho_coef[27:28, :] = r_col_back[1]
    q_points = 0.25 * weighted(rho_in)
    q_own, q_back = lat_rows(q_points)
    q_col, q_col_back = lon_cols(q_points)
    t_own, t_back = lat_rows(0.25 * rho_in)
    v_own, v_back = lat_rows(0.25 * earlier(rho_in))

    u = [[disp_new[comp, i] for i in range(4)] for comp in range(3)]
    potential = [phi[i] for i in range(4)]
    source_x = lat_part(
        u[0], following * lat_above[0:4, :], lat_below[0:4, :], M_SOURCE, q_own, q_back
    )
    source_y = lon_part(
        u[1], lon_above[4:8, :], lon_below[0:4, :], M_SOURCE, q_col, q_col_back
    )
    source_z = radial_part(u[2], M_SOURCE, (t_own + t_back, t_own), (v_own + v_back, v_own))
    image_x = lat_part(
        potential, following * lat_above[12:16, :], lat_below[4:8, :], M_POISSON, s_own, s_back
    )
    image_y = lon_part(
        potential, lon_above[12:16, :], lon_below[4:8, :], M_POISSON, s_col, s_col_back
    )
    image_z = radial_part(potential, M_POISSON, i_both, j_both)
    diag = [M_POISSON[a][a] for a in range(5)]
    diag_node = by_index(node, diag[:4])
    diag_col = column(diag[:4])
    first = column([1.0, 0.0, 0.0, 0.0])
    w0 = []
    for i in range(4):
        kind = min(i, 1)
        precond = diag[i] * s_own
        if i == 0:
            precond = precond + diag[4] * s_back
        precond = precond + W[i] * (
            diag_col * s_col[kind]
            + first * (diag[4] * s_col_back[kind])
            + i_both[kind] * diag_node
            + diag[4] * j_both[kind]
        )
        precond_out[i] = precond
        source = -(source_x[i] + source_y[i] + source_z[i])
        image = image_x[i] + image_y[i] + image_z[i]
        value = (source - image) / precond
        w0_out[i] = value
        w0.append(value)
    messages(w0, (lat0, lat1), (lon0, lon1))


def poisson(fields, coef, lat_first, lat_second, lon_first, lon_second):
    following = has_next()
    lat_below, lat_above = arrived("lat", lat_first, lat_second)
    lon_below, lon_above = arrived("lon", lon_first, lon_second)
    s_col = (coef[24:25, :], coef[25:26, :])
    s_col_back = (coef[26:27, :], coef[27:28, :])
    x = lat_part(
        fields, following * lat_above[0:4, :], lat_below[0:4, :], M_POISSON, coef[0:4, :], coef[4:8, :]
    )
    y = lon_part(fields, lon_above[0:4, :], lon_below[0:4, :], M_POISSON, s_col, s_col_back)
    z = radial_part(
        fields, M_POISSON, (coef[8:12, :], coef[12:16, :]), (coef[16:20, :], coef[20:24, :])
    )
    return [x[i] + y[i] + z[i] for i in range(4)]


def step(field, coef, precond, halo, out):
    fields = [field[i] for i in range(4)]
    image = poisson(fields, coef, *halo)
    result = []
    for i in range(4):
        value = image[i] / precond[i] - fields[i]
        out[i] = value
        result.append(value)
    return result


def second_kernel(
    field, coef, precond, lat_first, lat_second, lon_first, lon_second, lon_force,
    out, lat0, lat1, lon0, lon1,
):
    result = step(field, coef, precond, (lat_first, lat_second, lon_first, lon_second), out)
    messages(result, (lat0, lat1), (lon0, lon1), (), (lon_force[...],))


def third_kernel(
    field, coef, precond, lat_first, lat_second, lon_first, lon_second, lat_force, _,
    out, lat0, lat1, lon0, lon1,
):
    result = step(field, coef, precond, (lat_first, lat_second, lon_first, lon_second), out)
    below, _ = arrived("lon", lon_first, lon_second)
    first = column([1.0, 0.0, 0.0, 0.0])
    edges = []
    for comp in range(3):
        corner = 12 + 5 * comp
        edges.append(
            lat_force[4 * comp : 4 * comp + 4, :] + first * below[corner : corner + 1]
        )
    messages(result, (lat0, lat1), (lon0, lon1), edges)


def moment_kernel(w0, w1, w2, coef, precond, lat_first, lat_second, lon_first, lon_second, out):
    fields = [w2[i] for i in range(4)]
    image = poisson(fields, coef, lat_first, lat_second, lon_first, lon_second)
    sums = [None] * 6
    for i in range(4):
        m = precond[i]
        a, b, c = w0[i], w1[i], w2[i]
        ma, mb, mc = m * a, m * b, m * c
        terms = [a * ma, b * ma, b * mb, c * mb, c * mc, c * (image[i] - mc)]
        for k in range(6):
            sums[k] = terms[k] if sums[k] is None else sums[k] + terms[k]
    lane = lanes((1, 128))
    line = jnp.zeros((1, 128), F32)
    for k in range(6):
        total = jnp.sum(jnp.sum(sums[k], axis=0, keepdims=True), axis=1, keepdims=True)
        line = jnp.where(lane == k, total, line)
    out[...] = jnp.broadcast_to(line, out.shape)


def cg_coefficients(mu):
    zero = jnp.zeros_like(mu[0])

    def inner(a):
        total = zero
        for i in range(len(a)):
            for j in range(len(a)):
                total = total + a[i] * a[j] * mu[i + j]
        return total

    def energy(a):
        total = zero
        for i in range(len(a)):
            for j in range(len(a)):
                total = total + a[i] * a[j] * (mu[i + j + 1] + mu[i + j])
        return total

    def ratio(a, b):
        return jnp.where(b == 0.0, 0.0, a / jnp.where(b == 0.0, 1.0, b))

    y = [zero, zero, zero]
    z = [zero + 1.0]
    search = [zero + 1.0]
    rz = mu[0]
    for step in range(3):
        length = ratio(rz, energy(search))
        for i in range(len(search)):
            y[i] = y[i] + length * search[i]
        if step < 2:
            grown = [zero] * (len(search) + 1)
            for i in range(len(search)):
                grown[i] = grown[i] + search[i]
                grown[i + 1] = grown[i + 1] + search[i]
            z = z + [zero]
            z = [z[i] - length * grown[i] for i in range(len(z))]
            rz_next = inner(z)
            beta = ratio(rz_next, rz)
            padded = search + [zero]
            search = [z[i] + beta * padded[i] for i in range(len(z))]
            rz = rz_next
    return y


def final_kernel(
    moments, phi, w0, w1, w2, rho_coef, own_force,
    a0, a1, a2, a3, b0, b1, b2, b3, c0, c1, c2, c3, d0, d1, d2, d3,
    vel, acc, phi_new, acc_new, vel_new,
):
    total = jnp.sum(moments[...], axis=0, keepdims=True)
    lane = lanes((1, 128))
    mu = [
        jnp.broadcast_to(
            jnp.sum(jnp.where(lane == k, total, 0.0), axis=1, keepdims=True), (1, 128)
        )
        for k in range(6)
    ]
    y = cg_coefficients(mu)
    y = [jnp.concatenate([v] * 4, 1) for v in y]

    def combined(first, one, two, three):
        return first + y[0] * one + y[1] * two + y[2] * three

    potential = []
    for i in range(4):
        value = combined(phi[i], w0[i], w1[i], w2[i])
        phi_new[i] = value
        potential.append(value)
    following, before = has_next(), has_before()
    ma, na = arrived("lat", a0, a1)
    mb, nb = arrived("lat", b0, b1)
    mc, nc = arrived("lat", c0, c1)
    md, nd = arrived("lat", d0, d1)
    fa, ga = arrived("lon", a2, a3)
    fb, gb = arrived("lon", b2, b3)
    fc, gc = arrived("lon", c2, c3)
    fd, gd = arrived("lon", d2, d3)
    lat_below = combined(ma[8:12, :], mb[4:8, :], mc[4:8, :], md[4:8, :])
    lat_above = following * combined(na[12:16, :], nb[0:4, :], nc[0:4, :], nd[0:4, :])
    lon_below = combined(fa[8:12, :], fb[4:8, :], fc[4:8, :], fd[4:8, :])
    lon_above = combined(ga[12:16, :], gb[0:4, :], gc[0:4, :], gd[0:4, :])
    r_own, r_back = rho_coef[0:4, :], rho_coef[4:8, :]
    r_col = (rho_coef[24:25, :], rho_coef[25:26, :])
    r_col_back = (rho_coef[26:27, :], rho_coef[27:28, :])
    x = lat_part(potential, lat_above, lat_below, M_GRAVITY, r_own, r_back)
    y_part = lon_part(potential, lon_above, lon_below, M_GRAVITY, r_col, r_col_back)
    z = radial_part(
        potential,
        M_GRAVITY,
        (rho_coef[8:12, :], rho_coef[12:16, :]),
        (rho_coef[16:20, :], rho_coef[20:24, :]),
    )
    cols = column(W[:4])
    first = column([1.0, 0.0, 0.0, 0.0])
    gravity = (x, y_part, z)
    for i in range(4):
        mass = r_own + r_back if i == 0 else r_own
        mass = 0.5 * W[i] * mass
        for comp in range(3):
            force = own_force[comp, i]
            force = force + first * fc[8 + 5 * comp + i : 9 + 5 * comp + i, :]
            if i == 0:
                edge = md[8 + 4 * comp : 12 + 4 * comp, :]
                force = force + before * edge
            value = (-gravity[comp][i] - force) / mass
            acc_new[comp, i] = value
            vel_new[comp, i] = vel[comp, i] + 0.5 * TIME_STEP * (acc[comp, i] + value)


def split3(value):
    high = value.astype(BF16)
    rest = value - high.astype(F32)
    mid = rest.astype(BF16)
    low = (rest - mid.astype(F32)).astype(BF16)
    return high, mid, low


def prepare_kernel(
    disp, mat_h, moduli_h, decay_h, strength_h, stiff, rates, perm, elems,
    points, mat, moduli, decay, strength, sems,
):
    moves = [
        pltpu.make_async_copy(src, dst, sems.at[n])
        for n, (src, dst) in enumerate(
            [(mat_h, mat), (moduli_h, moduli), (decay_h, decay), (strength_h, strength)]
        )
    ]
    for move in moves:
        move.start()
    for c in range(4):
        hit = lax.broadcasted_iota(jnp.int32, (128, 512), 1) == (
            4 * lax.broadcasted_iota(jnp.int32, (128, 512), 0) + c
        )
        perm[128 * c : 128 * c + 128, :] = jnp.where(hit, 1.0, 0.0).astype(BF16)
    points[...] = jnp.zeros(points.shape, F32)
    for comp in range(3):
        for a in range(4):
            base = (comp * 4 + a) * 8
            points[base : base + 4, :] = disp[comp, a]
    to_nodes(points[...], perm, elems)
    for move in moves:
        move.wait()
    onehot = [mat[0] == m for m in range(8)]
    for k in range(6):
        for l in range(k, 6):
            value = jnp.zeros((1, 128), F32)
            for m in range(8):
                value = jnp.where(onehot[m], moduli[k, m, l], value)
            stiff[6 * k + l : 6 * k + l + 1, :] = value
    for l in range(3):
        rates[l : l + 1, :] = jnp.full((1, 128), decay[l], F32)
        rates[3 + l : 4 + l, :] = jnp.full((1, 128), (1.0 - decay[l]) * strength[l], F32)


def unpack_kernel(memory, rates, _, decayed, flag, old):
    for d in range(5):
        for a in range(5):
            for b in range(5):
                for c in range(5):
                    row = (b * 5 + c) * 4
                    old[row : row + 3, :] = memory[d, a, b, c].astype(F32)
            for c in range(5):
                for l in range(3):
                    was = old[pl.ds(4 * c + l, 8, stride=20), :]
                    decayed[((d * 5 + a) * 5 + c) * 3 + l] = rates[l : l + 1, :] * was
    flag[...] = jnp.zeros((8, 128), F32)


def repack_kernel(dense, memory_new, flag, new):
    for d in range(5):
        for a in range(5):
            for c in range(5):
                for l in range(3):
                    new[pl.ds(4 * c + l, 8, stride=20), :] = dense[((d * 5 + a) * 5 + c) * 3 + l]
            for b in range(5):
                for c in range(5):
                    row = (b * 5 + c) * 4
                    memory_new[d, a, b, c] = new[row : row + 3, :].astype(BF16)
    flag[...] = jnp.zeros((8, 128), F32)


def to_nodes(points, perm, elems):
    rows = points.shape[0]
    parts = jnp.concatenate(split3(points), 0)
    taken = lax.dot_general(
        parts, perm[...], (((1,), (1,)), ((), ())), preferred_element_type=F32
    )
    taken = taken[0:rows] + taken[rows : 2 * rows] + taken[2 * rows : 3 * rows]
    for c in range(4):
        elems[c] = taken[:, 128 * c : 128 * c + 128]
    lane = lanes((rows, 128))
    elems[4] = jnp.where(lane < 127, pltpu.roll(taken[:, 0:128], 127, 1), 0.0)


def elastic_kernel(
    lat_first, lat_second, lon_first, lon_second, stiff, rates, perm, own, decayed,
    dense, force, lat_force, lon_force,
    points, edge, elems, devs, flux,
):
    following = has_next()
    _, lat_above = arrived("lat", lat_first, lat_second)
    _, lon_above = arrived("lon", lon_first, lon_second)
    points[...] = jnp.zeros(points.shape, F32)
    for comp in range(3):
        points[8 * comp : 8 * comp + 4, :] = following * lat_above[4 * comp : 4 * comp + 4]
        points[8 * comp + 4 : 8 * comp + 5, :] = following * lat_above[16 + comp : 17 + comp]
    points[24:36, :] = lon_above[0:12]
    to_nodes(points[...], perm, edge)
    fifth = sublanes((8, 128)) == 4
    for c in range(5):
        for comp in range(3):
            for a in range(4):
                base, row = (comp * 5 + a) * 8, 24 + 4 * comp + a
                kept = own[c, (comp * 4 + a) * 8 : (comp * 4 + a) * 8 + 8, :]
                elems[c, base : base + 8, :] = jnp.where(
                    fifth, row_of(edge[c, 24:40, :], row - 24, 8), kept
                )
            base = (comp * 5 + 4) * 8
            elems[c, base : base + 8, :] = edge[c, 8 * comp : 8 * comp + 8, :]
    lane = lanes((128, 128))
    slopes = [
        by_index(sublanes((8, 128)), [2.0 * DERIV[b][p] for b in range(5)] + [0.0])
        for p in range(5)
    ]
    turned = [
        by_index(sublanes((8, 128)), [2.0 * DERIV[p][b] for b in range(5)] + [0.0])
        for p in range(5)
    ]
    weight_col = by_index(sublanes((8, 128)), W + [0.0])

    def slab(comp, a, c):
        base = (comp * 5 + a) * 8
        return elems[c, base : base + 8, :]

    def along_lon(cols, value):
        total = None
        for p in range(5):
            term = cols[p] * row_of(value, p, 8)
            total = term if total is None else total + term
        return total

    for a in range(5):
        elastic_of = []
        for c in range(5):
            dx, dy, dz = [], [], []
            for comp in range(3):
                dx.append(mix([2.0 * DERIV[a][p] for p in range(5)], [slab(comp, p, c) for p in range(5)]))
                dy.append(along_lon(slopes, slab(comp, a, c)))
                dz.append(mix([2.0 * DERIV[c][p] for p in range(5)], [slab(comp, a, p) for p in range(5)]))
            strain = [dx[0], dy[1], dz[2], dy[0] + dx[1], dz[0] + dx[2], dz[1] + dy[2]]
            elastic = []
            for k in range(6):
                total = None
                for l in range(6):
                    pos = 6 * min(k, l) + max(k, l)
                    term = stiff[pos : pos + 1, :] * strain[l]
                    total = term if total is None else total + term
                elastic.append(total)
            pressure = (elastic[0] + elastic[1] + elastic[2]) * (1.0 / 3.0)
            dev = [elastic[0] - pressure, elastic[1] - pressure, elastic[3], elastic[4], elastic[5]]
            for d in range(5):
                devs[d * 5 + c] = dev[d]
            elastic_of.append(elastic)
        relaxed = []
        for d in range(5):
            sums = []
            for c in range(5):
                dev = devs[d * 5 + c]
                total = None
                for l in range(3):
                    pos = ((d * 5 + a) * 5 + c) * 3 + l
                    now = decayed[pos] + rates[3 + l : 4 + l, :] * dev
                    now = now.astype(BF16).astype(F32)
                    dense[pos] = now
                    total = now if total is None else total + now
                sums.append(total)
            relaxed.append(sums)
        for c in range(5):
            e = elastic_of[c]
            r = [relaxed[d][c] for d in range(5)]
            weight = weight_col * (W[a] * W[c] / 8.0)
            stress = [e[0] - r[0], e[1] - r[1], e[2] + r[0] + r[1], e[3] - r[2], e[4] - r[3], e[5] - r[4]]
            for k in range(6):
                flux[k, a * 5 + c] = jnp.where(weight_col > 0.0, weight * stress[k], 0.0)
    flux_of = [[0, 3, 4], [3, 1, 5], [4, 5, 2]]
    for c in range(5):
        elems[c, 120:128, :] = jnp.zeros((8, 128), F32)
        for comp in range(3):
            for a in range(5):
                value = mix(
                    [2.0 * DERIV[p][a] for p in range(5)],
                    [flux[flux_of[comp][0], p * 5 + c] for p in range(5)],
                )
                value = value + along_lon(turned, flux[flux_of[comp][1], a * 5 + c])
                value = value + mix(
                    [2.0 * DERIV[p][c] for p in range(5)],
                    [flux[flux_of[comp][2], a * 5 + p] for p in range(5)],
                )
                base = (comp * 5 + a) * 8
                elems[c, base : base + 8, :] = value
    carried = jnp.where(lane > 0, pltpu.roll(elems[4], 1, 1), 0.0)
    merged = jnp.concatenate([elems[0] + carried, elems[1], elems[2], elems[3]], 1)
    parts = jnp.concatenate(split3(merged), 0)
    given = jnp.dot(parts, perm[...], preferred_element_type=F32)
    given = given[0:128] + given[128:256] + given[256:384]
    lat_force[12:16, :] = jnp.zeros((4, 512), F32)
    lon_force[15:16, :] = jnp.zeros((1, 512), F32)
    for comp in range(3):
        for a in range(5):
            base = (comp * 5 + a) * 8
            if a < 4:
                force[comp, a] = given[base : base + 4]
                lon_force[5 * comp + a : 5 * comp + a + 1, :] = given[base + 4 : base + 5]
            else:
                lat_force[4 * comp : 4 * comp + 4, :] = given[base : base + 4]
                lon_force[5 * comp + 4 : 5 * comp + 5, :] = given[base + 4 : base + 5]


def call(kernel, name, outs, ins, args, scratch=(), flops=1000000, moved=500000, vmem=24):
    return pl.pallas_call(
        kernel,
        name=name,
        out_shape=[jax.ShapeDtypeStruct(s, d) for s, d in outs],
        in_specs=ins,
        out_specs=[VMEM] * len(outs),
        scratch_shapes=list(scratch),
        compiler_params=pltpu.CompilerParams(vmem_limit_bytes=vmem * 1024 * 1024),
        cost_estimate=pl.CostEstimate(flops=flops, bytes_accessed=moved, transcendentals=0),
    )(*args)


def swap(array, axis, size, parity):
    pairs = []
    for i in range(parity, size, 2):
        j = (i + 1) % size
        pairs += [(i, j), (j, i)]
    return lax.ppermute(array, axis, pairs)


def swap_lat(first, second):
    return swap(first, "lat", LAT, 0), swap(second, "lat", LAT, 1)


def swap_lon(first, second):
    other = swap(second, "lon", LON, 1)
    return swap(first, "lon", LON, 0), other


def per_device(
    displacement, velocity, acceleration, potential, memory_vars, materials, shell_flags,
    moduli, densities, decay, strength,
):
    field = ((4, 4, 512), F32)
    vector = ((3, 4, 4, 512), F32)
    r8, r16, r24, r32 = (((n, 512), F32) for n in (8, 16, 24, 32))
    info = ((8, 128), F32)
    kept = pltpu.with_memory_space_constraint
    disp_new, disp, phi, own_info, *sent = call(
        start_kernel, "start", [vector, vector, field, info, r16, r24], [HBM] * 7,
        [
            kept(array, pltpu.HBM)
            for array in (
                displacement, velocity, acceleration, potential, materials, shell_flags, densities
            )
        ],
        [
            pltpu.VMEM((3, 4, 4, 512), F32),
            pltpu.VMEM((3, 4, 4, 512), F32),
            pltpu.VMEM((3, 4, 4, 512), F32),
            pltpu.VMEM((1, 1, 128), jnp.int32),
            pltpu.VMEM((1, 1, 128), jnp.int32),
            pltpu.SMEM((8,), F32),
            pltpu.SemaphoreType.DMA((7,)),
        ],
    )
    lon_a = swap_lon(*sent)
    tables = call(
        prepare_kernel, "prepare",
        [((40, 128), F32), info, ((512, 512), BF16), ((5, 96, 128), F32)],
        [VMEM] + [HBM] * 4,
        [disp]
        + [
            kept(array, pltpu.HBM)
            for array in (materials, moduli.transpose(1, 0, 2), decay, strength)
        ],
        [
            pltpu.VMEM((96, 512), F32),
            pltpu.VMEM((1, 1, 128), jnp.int32),
            pltpu.SMEM((6, 8, 6), F32),
            pltpu.SMEM((3,), F32),
            pltpu.SMEM((3,), F32),
            pltpu.SemaphoreType.DMA((4,)),
        ],
    )
    lat_a = call(
        pack_kernel, "pack", [r24, r24], [VMEM] * 6,
        (disp, phi, own_info, *lon_a, tables[1]),
    )
    halo_a = (*swap_lat(*lat_a), *lon_a)
    memory = memory_vars.reshape(3, 5, 5, 5, 5, 128).transpose(1, 2, 3, 4, 0, 5)
    every = ((375, 8, 128), F32)
    decayed, unpacked = call(
        unpack_kernel, "unpack", [every, info], [VMEM] * 3, (memory, tables[1], lat_a[0]),
        [pltpu.VMEM((160, 128), F32)],
    )
    coef, rho_coef, precond, w0, *sent = call(
        residual_kernel, "residual", [r32, r32, field, field, r8, r8, r8, r16], [VMEM] * 8,
        (disp, phi, own_info, *halo_a, unpacked),
    )
    lon_b = swap_lon(*sent[2:])
    halo_b = (*swap_lat(*sent[:2]), *lon_b)
    dense, force, lat_force, lon_force = call(
        elastic_kernel, "elastic", [every, vector, r16, r16], [VMEM] * 9,
        (*halo_a, *tables, decayed),
        [
            pltpu.VMEM((48, 512), F32),
            pltpu.VMEM((5, 48, 128), F32),
            pltpu.VMEM((5, 128, 128), F32),
            pltpu.VMEM((25, 8, 128), F32),
            pltpu.VMEM((6, 25, 8, 128), F32),
        ],
        flops=20000000, moved=2000000,
    )
    w1, *sent = call(
        second_kernel, "second", [field, r8, r8, r24, r32], [VMEM] * 8,
        (w0, coef, precond, *halo_b, lon_force),
    )
    lon_c = swap_lon(*sent[2:])
    halo_c = (*swap_lat(*sent[:2]), *lon_c)
    memory_new, packed = call(
        repack_kernel, "repack", [((5, 5, 5, 5, 3, 128), BF16), info], [VMEM], (dense,),
        [pltpu.VMEM((160, 128), F32)],
    )
    w2, *sent = call(
        third_kernel, "third", [field, r24, r24, r8, r32], [VMEM] * 9,
        (w1, coef, precond, *halo_c, lat_force, packed),
    )
    lon_d = swap_lon(*sent[2:])
    halo_d = (*swap_lat(*sent[:2]), *lon_d)
    (line,) = call(
        moment_kernel, "moments", [((LAT * LON, 128), F32)], [VMEM] * 9,
        (w0, w1, w2, coef, precond, *halo_d),
    )
    moments = lax.all_to_all(line, AXES, 0, 0, tiled=True)
    phi_new, acc_new, vel_new = call(
        final_kernel, "final", [field, vector, vector], [VMEM] * 25,
        (
            moments, phi, w0, w1, w2, rho_coef, force, *halo_a, *halo_b, *halo_c, *halo_d,
            velocity, acceleration,
        ),
    )
    memory_new = memory_new.transpose(4, 0, 1, 2, 3, 5).reshape(memory_vars.shape)
    return (disp_new, vel_new, acc_new, phi_new, memory_new)


def solution(mesh):
    vector = P(None, "lat", "lon", None)
    scalar = P("lat", "lon", None)
    memory = P(None, None, None, "lat", None, "lon", None, None)
    return jax.shard_map(
        per_device,
        mesh=mesh,
        in_specs=(vector, vector, vector, scalar, memory, scalar, scalar, P(), P(), P(), P()),
        out_specs=(vector, vector, vector, scalar, memory),
        check_vma=False,
    )
```

```python
import jax
import jax.numpy as jnp
import numpy as np
from jax import lax
from jax.experimental import pallas as pl
from jax.experimental.pallas import tpu as pltpu
from jax.sharding import PartitionSpec as P

TIME_STEP = 0.1
F32 = jnp.float32
BF16 = jnp.bfloat16
LAT, LON = 8, 32
AXES = ("lat", "lon")
VMEM = pl.BlockSpec(memory_space=pltpu.VMEM)
HBM = pl.BlockSpec(memory_space=pltpu.HBM)


def gll():
    points = np.array([-1.0, -np.sqrt(3.0 / 7.0), 0.0, np.sqrt(3.0 / 7.0), 1.0])
    weights = np.array([0.1, 49.0 / 90.0, 32.0 / 45.0, 49.0 / 90.0, 0.1])
    differ = points[:, None] - points[None, :] + np.eye(5)
    factors = np.prod(differ, axis=1)
    deriv = factors[:, None] / factors[None, :] / differ * (1.0 - np.eye(5))
    deriv = deriv - np.eye(5) * np.sum(deriv, axis=1)[:, None]
    return deriv, weights


DERIV, WEIGHTS = gll()
W = [float(v) for v in WEIGHTS]
M_POISSON = (DERIV.T @ np.diag(WEIGHTS) @ DERIV).tolist()
M_SOURCE = (np.diag(WEIGHTS) @ DERIV).T.tolist()
M_GRAVITY = (np.diag(WEIGHTS) @ DERIV).tolist()


def lanes(shape):
    return lax.broadcasted_iota(jnp.int32, shape, len(shape) - 1)


def sublanes(shape):
    return lax.broadcasted_iota(jnp.int32, shape, len(shape) - 2)


def by_index(index, values):
    out = jnp.full(index.shape, float(values[-1]), F32)
    for pos in range(len(values) - 2, -1, -1):
        out = jnp.where(index == pos, float(values[pos]), out)
    return out


def column(values, rows=4, width=512):
    return by_index(sublanes((rows, width)), list(values))


def row_of(array, pos, rows=4):
    return jnp.broadcast_to(array[pos : pos + 1], (rows, array.shape[1]))


def radial(field, matrix):
    lane = lanes((4, 512))
    node = lane & 3
    own, before = None, None
    for shift in range(-4, 5):
        moved = field if shift == 0 else pltpu.roll(field, (-shift) % 512, 1)
        if shift > -4:
            factors = [
                matrix[c][c + shift] if 0 <= c + shift <= 4 else 0.0 for c in range(4)
            ]
            table = by_index(node, factors)
            if shift > 0:
                table = jnp.where(lane < 512 - shift, table, 0.0)
            own = table * moved if own is None else own + table * moved
        if shift <= 0:
            term = float(matrix[4][4 + shift]) * moved
            before = term if before is None else before + term
    return own, before


def mix(matrix_row, arrays):
    total = None
    for factor, array in zip(matrix_row, arrays):
        term = float(factor) * array
        total = term if total is None else total + term
    return total


def lat_part(fields, above, below, matrix, own_row, back_row):
    out = []
    for i in range(4):
        value = own_row * mix(matrix[i], fields + [above])
        if i == 0:
            value = value + back_row * (float(matrix[4][4]) * fields[0] + below)
        out.append(value)
    return out


def lon_part(fields, above, below, matrix, own_col, back_col):
    columns = [column([matrix[b][p] for b in range(4)]) for p in range(5)]
    first = column([1.0, 0.0, 0.0, 0.0])
    out = []
    for i in range(4):
        value = columns[4] * row_of(above, i)
        for p in range(4):
            value = value + columns[p] * row_of(fields[i], p)
        edge = float(matrix[4][4]) * fields[i][0:1] + below[i : i + 1]
        kind = min(i, 1)
        value = own_col[kind] * value + first * (back_col[kind] * edge)
        out.append(W[i] * value)
    return out


def radial_part(fields, matrix, own, before):
    out = []
    for i in range(4):
        first, second = radial(fields[i], matrix)
        kind = min(i, 1)
        out.append(W[i] * (own[kind] * first + before[kind] * second))
    return out


def partial_lat(fields, matrix):
    return mix(matrix[4][:4], fields)


def partial_lon(field, matrix):
    weighted = column(matrix[4][:4]) * field
    return jnp.sum(weighted, axis=0, keepdims=True)


def even(axis):
    return lax.rem(lax.axis_index(axis), 2) == 0


def pick(axis, for_even, for_odd):
    return jnp.where(even(axis), for_even, for_odd)


def post(axis, outs, up, down):
    for out, sent in zip(outs, (pick(axis, up, down), pick(axis, down, up))):
        out[...] = sent[: out.shape[0]]


def arrived(axis, first, second):
    height = min(first.shape[0], second.shape[0])
    first, second = first[0:height], second[0:height]
    return pick(axis, second, first), pick(axis, first, second)


def stack(rows, height):
    total = sum(r.shape[0] for r in rows)
    if total < height:
        rows = rows + [jnp.zeros((height - total, 512), F32)]
    return jnp.concatenate(rows, 0)


def messages(fields, lat_out, lon_out, extra_lat=(), extra_lon=()):
    up = [partial_lat(fields, M_POISSON), partial_lat(fields, M_GRAVITY)]
    height = max(out.shape[0] for out in lat_out)
    post("lat", lat_out, stack(up + list(extra_lat), height), stack([fields[0]], height))
    up = [partial_lon(fields[i], M_POISSON) for i in range(4)]
    up += [partial_lon(fields[i], M_GRAVITY) for i in range(4)]
    down = [fields[i][0:1] for i in range(4)]
    height = max(out.shape[0] for out in lon_out)
    post("lon", lon_out, stack(up + list(extra_lon), height), stack(down, height))


def has_next():
    return jnp.where(lax.axis_index("lat") < LAT - 1, 1.0, 0.0).astype(F32)


def has_before():
    return jnp.where(lax.axis_index("lat") > 0, 1.0, 0.0).astype(F32)


def start_kernel(
    disp_h, vel_h, acc_h, phi_h, mat_h, flag_h, dens_h,
    disp_out, phi_out, info_out, lon0, lon1,
    disp, vel, acc, mat, flag, dens, sems,
):
    moves = [
        pltpu.make_async_copy(src, dst, sems.at[n])
        for n, (src, dst) in enumerate(
            [
                (mat_h, mat), (flag_h, flag), (dens_h, dens), (phi_h, phi_out),
                (disp_h, disp), (vel_h, vel), (acc_h, acc),
            ]
        )
    ]
    for move in moves:
        move.start()
    for move in moves[:3]:
        move.wait()
    rho = jnp.zeros((1, 128), F32)
    for m in range(8):
        rho = jnp.where(mat[0] == m, dens[m], rho)
    shell = 1.0 + flag[0].astype(F32)
    info = jnp.concatenate([rho, shell, jnp.zeros((1, 256), F32)], 1)
    info_out[...] = jnp.concatenate([rho, shell, jnp.zeros((6, 128), F32)], 0)
    moves[3].wait()
    potential = [phi_out[i] for i in range(4)]
    for move in moves[4:]:
        move.wait()
    u = []
    for comp in range(3):
        planes = []
        for i in range(4):
            value = (
                disp[comp, i]
                + TIME_STEP * vel[comp, i]
                + 0.5 * TIME_STEP * TIME_STEP * acc[comp, i]
            )
            disp_out[comp, i] = value
            planes.append(value)
        u.append(planes)
    up = [partial_lon(u[1][i], M_SOURCE) for i in range(4)]
    up += [partial_lon(potential[i], M_POISSON) for i in range(4)]
    up += [partial_lon(potential[i], M_GRAVITY) for i in range(4)]
    down = [u[comp][i][0:1] for comp in range(3) for i in range(4)]
    down += [potential[i][0:1] for i in range(4)]
    post("lon", (lon0, lon1), stack(up + [info], 24), stack(down, 24))

def pack_kernel(disp, phi, own_info, lon_first, lon_second, _, lat0, lat1):
    below, above = arrived("lon", lon_first, lon_second)
    potential = [phi[i] for i in range(4)]
    info = jnp.concatenate(
        [own_info[0:1, :], own_info[1:2, :], jnp.zeros((1, 256), F32)], 1
    )
    up = [
        partial_lat([disp[0, i] for i in range(4)], M_SOURCE),
        partial_lat(potential, M_POISSON),
        partial_lat(potential, M_GRAVITY),
        info,
        below[12:13],
    ]
    down = [disp[0, 0], disp[1, 0], disp[2, 0], potential[0]]
    down += [above[4 * comp : 4 * comp + 1] for comp in range(3)]
    post("lat", (lat0, lat1), stack(up, 24), stack(down, 24))


def lat_rows(factor):
    cols, first = column(W[:4]), column([W[0], 0.0, 0.0, 0.0])
    own = cols * row_of(factor, 0) + first * row_of(factor, 2)
    back = cols * row_of(factor, 1) + first * row_of(factor, 3)
    return own, back


def lon_cols(factor):
    own = (factor[0:1] + factor[1:2], factor[0:1])
    back = (factor[2:3] + factor[3:4], factor[2:3])
    return own, back


def radial_tools():
    lane = lanes((4, 512))
    node = lane & 3
    joint = jnp.logical_and(node == 0, lane >= 4)
    weight = by_index(node, W[:4])

    def earlier(factor):
        return jnp.where(joint, pltpu.roll(factor, 4, 1), 0.0)

    def weighted(factor):
        return weight * factor + W[4] * earlier(factor)

    return node, weight, earlier, weighted


def density_kernel(coef, disp, _, rho_coef, disp_new, flag):
    _, _, earlier, weighted = radial_tools()
    rho, inverse = coef[28:32, :], coef[32:36, :]
    r_points = 0.25 * weighted(rho)
    r_own, r_back = lat_rows(r_points)
    r_col, r_col_back = lon_cols(r_points)
    scaled = 0.25 * rho * inverse
    g_own, g_back = lat_rows(scaled)
    h_own, h_back = lat_rows(earlier(scaled))
    rho_coef[0:4, :] = r_own
    rho_coef[4:8, :] = r_back
    rho_coef[8:12, :] = g_own + g_back
    rho_coef[12:16, :] = g_own
    rho_coef[16:20, :] = h_own + h_back
    rho_coef[20:24, :] = h_own
    rho_coef[24:25, :] = r_col[0]
    rho_coef[25:26, :] = r_col[1]
    rho_coef[26:27, :] = r_col_back[0]
    rho_coef[27:28, :] = r_col_back[1]
    flag[...] = jnp.zeros((8, 128), F32)
    disp_new[...] = disp[...]


def residual_kernel(
    disp_new, phi, own_info, lat_first, lat_second, lon_first, lon_second, _,
    coef, precond_out, w0_out, lat0, lat1, lon0, lon1,
):
    following, before = has_next(), has_before()
    lat_below, lat_above = arrived("lat", lat_first, lat_second)
    lon_below, lon_above = arrived("lon", lon_first, lon_second)
    rho, shell = (
        jnp.concatenate(
            [
                own_info[n : n + 1, :],
                before * lat_below[12:13, 128 * n : 128 * n + 128],
                lon_below[12:13, 128 * n : 128 * n + 128],
                before * lat_below[13:14, 128 * n : 128 * n + 128],
            ],
            0,
        )
        for n in range(2)
    )
    spread = (
        lax.broadcasted_iota(jnp.int32, (128, 512), 1) // 4
        == lax.broadcasted_iota(jnp.int32, (128, 512), 0)
    )
    spread = jnp.where(spread, 1.0, 0.0).astype(BF16)
    high, mid, low = split3(rho)
    parts = jnp.concatenate(
        [high.astype(F32), mid.astype(F32), low.astype(F32), shell], 0
    ).astype(BF16)
    parts = jnp.dot(parts, spread, preferred_element_type=F32)
    rho = parts[0:4] + parts[4:8] + parts[8:12]
    shell = parts[12:16]
    flagged = shell > 1.5
    valid = shell > 0.5
    stretch = jnp.where(valid, jnp.where(flagged, 3.0, 1.0), 0.0)
    inverse = jnp.where(valid, jnp.where(flagged, 1.0 / 3.0, 1.0), 0.0)
    rho_in = jnp.where(flagged, 0.0, rho)
    node, weight, earlier, weighted = radial_tools()
    s_points = 0.5 * weighted(stretch)
    s_own, s_back = lat_rows(s_points)
    s_col, s_col_back = lon_cols(s_points)
    i_own, i_back = lat_rows(0.5 * inverse)
    j_own, j_back = lat_rows(0.5 * earlier(inverse))
    i_both, j_both = (i_own + i_back, i_own), (j_own + j_back, j_own)
    coef[0:4, :] = s_own
    coef[4:8, :] = s_back
    coef[8:12, :] = i_both[0]
    coef[12:16, :] = i_both[1]
    coef[16:20, :] = j_both[0]
    coef[20:24, :] = j_both[1]
    coef[24:25, :] = s_col[0]
    coef[25:26, :] = s_col[1]
    coef[26:27, :] = s_col_back[0]
    coef[27:28, :] = s_col_back[1]
    coef[28:32, :] = rho
    coef[32:36, :] = inverse
    q_points = 0.25 * weighted(rho_in)
    q_own, q_back = lat_rows(q_points)
    q_col, q_col_back = lon_cols(q_points)
    t_own, t_back = lat_rows(0.25 * rho_in)
    v_own, v_back = lat_rows(0.25 * earlier(rho_in))

    u = [[disp_new[comp, i] for i in range(4)] for comp in range(3)]
    potential = [phi[i] for i in range(4)]
    source_x = lat_part(
        u[0], following * lat_above[0:4, :], lat_below[0:4, :], M_SOURCE, q_own, q_back
    )
    source_y = lon_part(
        u[1], lon_above[4:8, :], lon_below[0:4, :], M_SOURCE, q_col, q_col_back
    )
    source_z = radial_part(u[2], M_SOURCE, (t_own + t_back, t_own), (v_own + v_back, v_own))
    image_x = lat_part(
        potential, following * lat_above[12:16, :], lat_below[4:8, :], M_POISSON, s_own, s_back
    )
    image_y = lon_part(
        potential, lon_above[12:16, :], lon_below[4:8, :], M_POISSON, s_col, s_col_back
    )
    image_z = radial_part(potential, M_POISSON, i_both, j_both)
    diag = [M_POISSON[a][a] for a in range(5)]
    diag_node = by_index(node, diag[:4])
    diag_col = column(diag[:4])
    first = column([1.0, 0.0, 0.0, 0.0])
    w0 = []
    for i in range(4):
        kind = min(i, 1)
        precond = diag[i] * s_own
        if i == 0:
            precond = precond + diag[4] * s_back
        precond = precond + W[i] * (
            diag_col * s_col[kind]
            + first * (diag[4] * s_col_back[kind])
            + i_both[kind] * diag_node
            + diag[4] * j_both[kind]
        )
        precond_out[i] = precond
        source = -(source_x[i] + source_y[i] + source_z[i])
        image = image_x[i] + image_y[i] + image_z[i]
        value = (source - image) / precond
        w0_out[i] = value
        w0.append(value)
    messages(w0, (lat0, lat1), (lon0, lon1))


def poisson(fields, coef, lat_first, lat_second, lon_first, lon_second):
    following = has_next()
    lat_below, lat_above = arrived("lat", lat_first, lat_second)
    lon_below, lon_above = arrived("lon", lon_first, lon_second)
    s_col = (coef[24:25, :], coef[25:26, :])
    s_col_back = (coef[26:27, :], coef[27:28, :])
    x = lat_part(
        fields, following * lat_above[0:4, :], lat_below[0:4, :], M_POISSON, coef[0:4, :], coef[4:8, :]
    )
    y = lon_part(fields, lon_above[0:4, :], lon_below[0:4, :], M_POISSON, s_col, s_col_back)
    z = radial_part(
        fields, M_POISSON, (coef[8:12, :], coef[12:16, :]), (coef[16:20, :], coef[20:24, :])
    )
    return [x[i] + y[i] + z[i] for i in range(4)]


def step(field, coef, precond, halo, out):
    fields = [field[i] for i in range(4)]
    image = poisson(fields, coef, *halo)
    result = []
    for i in range(4):
        value = image[i] / precond[i] - fields[i]
        out[i] = value
        result.append(value)
    return result


def second_kernel(
    field, coef, precond, lat_first, lat_second, lon_first, lon_second, lon_force,
    out, lat0, lat1, lon0, lon1,
):
    result = step(field, coef, precond, (lat_first, lat_second, lon_first, lon_second), out)
    messages(result, (lat0, lat1), (lon0, lon1), (), (lon_force[...],))


def third_kernel(
    field, coef, precond, lat_first, lat_second, lon_first, lon_second, lat_force, _,
    out, lat0, lat1, lon0, lon1,
):
    result = step(field, coef, precond, (lat_first, lat_second, lon_first, lon_second), out)
    below, _ = arrived("lon", lon_first, lon_second)
    first = column([1.0, 0.0, 0.0, 0.0])
    edges = []
    for comp in range(3):
        corner = 12 + 5 * comp
        edges.append(
            lat_force[4 * comp : 4 * comp + 4, :] + first * below[corner : corner + 1]
        )
    messages(result, (lat0, lat1), (lon0, lon1), edges)


def moment_kernel(
    w0, w1, w2, coef, precond, lat_first, lat_second, lon_first, lon_second, _, out
):
    fields = [w2[i] for i in range(4)]
    image = poisson(fields, coef, lat_first, lat_second, lon_first, lon_second)
    sums = [None] * 6
    for i in range(4):
        m = precond[i]
        a, b, c = w0[i], w1[i], w2[i]
        ma, mb, mc = m * a, m * b, m * c
        terms = [a * ma, b * ma, b * mb, c * mb, c * mc, c * (image[i] - mc)]
        for k in range(6):
            sums[k] = terms[k] if sums[k] is None else sums[k] + terms[k]
    lane = lanes((1, 128))
    line = jnp.zeros((1, 128), F32)
    for k in range(6):
        total = jnp.sum(jnp.sum(sums[k], axis=0, keepdims=True), axis=1, keepdims=True)
        line = jnp.where(lane == k, total, line)
    out[...] = jnp.broadcast_to(line, out.shape)


def cg_coefficients(mu):
    zero = jnp.zeros_like(mu[0])

    def inner(a):
        total = zero
        for i in range(len(a)):
            for j in range(len(a)):
                total = total + a[i] * a[j] * mu[i + j]
        return total

    def energy(a):
        total = zero
        for i in range(len(a)):
            for j in range(len(a)):
                total = total + a[i] * a[j] * (mu[i + j + 1] + mu[i + j])
        return total

    def ratio(a, b):
        return jnp.where(b == 0.0, 0.0, a / jnp.where(b == 0.0, 1.0, b))

    y = [zero, zero, zero]
    z = [zero + 1.0]
    search = [zero + 1.0]
    rz = mu[0]
    for step in range(3):
        length = ratio(rz, energy(search))
        for i in range(len(search)):
            y[i] = y[i] + length * search[i]
        if step < 2:
            grown = [zero] * (len(search) + 1)
            for i in range(len(search)):
                grown[i] = grown[i] + search[i]
                grown[i + 1] = grown[i + 1] + search[i]
            z = z + [zero]
            z = [z[i] - length * grown[i] for i in range(len(z))]
            rz_next = inner(z)
            beta = ratio(rz_next, rz)
            padded = search + [zero]
            search = [z[i] + beta * padded[i] for i in range(len(z))]
            rz = rz_next
    return y


def final_kernel(
    moments, phi, w0, w1, w2, rho_coef, own_force,
    a0, a1, a2, a3, b0, b1, b2, b3, c0, c1, c2, c3, d0, d1, d2, d3,
    vel, acc, phi_new, acc_new, vel_new,
):
    total = jnp.sum(moments[...], axis=0, keepdims=True)
    lane = lanes((1, 128))
    mu = [
        jnp.broadcast_to(
            jnp.sum(jnp.where(lane == k, total, 0.0), axis=1, keepdims=True), (1, 128)
        )
        for k in range(6)
    ]
    y = cg_coefficients(mu)
    y = [jnp.concatenate([v] * 4, 1) for v in y]

    def combined(first, one, two, three):
        return first + y[0] * one + y[1] * two + y[2] * three

    potential = []
    for i in range(4):
        value = combined(phi[i], w0[i], w1[i], w2[i])
        phi_new[i] = value
        potential.append(value)
    following, before = has_next(), has_before()
    ma, na = arrived("lat", a0, a1)
    mb, nb = arrived("lat", b0, b1)
    mc, nc = arrived("lat", c0, c1)
    md, nd = arrived("lat", d0, d1)
    fa, ga = arrived("lon", a2, a3)
    fb, gb = arrived("lon", b2, b3)
    fc, gc = arrived("lon", c2, c3)
    fd, gd = arrived("lon", d2, d3)
    lat_below = combined(ma[8:12, :], mb[4:8, :], mc[4:8, :], md[4:8, :])
    lat_above = following * combined(na[12:16, :], nb[0:4, :], nc[0:4, :], nd[0:4, :])
    lon_below = combined(fa[8:12, :], fb[4:8, :], fc[4:8, :], fd[4:8, :])
    lon_above = combined(ga[12:16, :], gb[0:4, :], gc[0:4, :], gd[0:4, :])
    r_own, r_back = rho_coef[0:4, :], rho_coef[4:8, :]
    r_col = (rho_coef[24:25, :], rho_coef[25:26, :])
    r_col_back = (rho_coef[26:27, :], rho_coef[27:28, :])
    x = lat_part(potential, lat_above, lat_below, M_GRAVITY, r_own, r_back)
    y_part = lon_part(potential, lon_above, lon_below, M_GRAVITY, r_col, r_col_back)
    z = radial_part(
        potential,
        M_GRAVITY,
        (rho_coef[8:12, :], rho_coef[12:16, :]),
        (rho_coef[16:20, :], rho_coef[20:24, :]),
    )
    cols = column(W[:4])
    first = column([1.0, 0.0, 0.0, 0.0])
    gravity = (x, y_part, z)
    for i in range(4):
        mass = r_own + r_back if i == 0 else r_own
        mass = 0.5 * W[i] * mass
        for comp in range(3):
            force = own_force[comp, i]
            force = force + first * fc[8 + 5 * comp + i : 9 + 5 * comp + i, :]
            if i == 0:
                edge = md[8 + 4 * comp : 12 + 4 * comp, :]
                force = force + before * edge
            value = (-gravity[comp][i] - force) / mass
            acc_new[comp, i] = value
            vel_new[comp, i] = vel[comp, i] + 0.5 * TIME_STEP * (acc[comp, i] + value)


def split3(value):
    high = value.astype(BF16)
    rest = value - high.astype(F32)
    mid = rest.astype(BF16)
    low = (rest - mid.astype(F32)).astype(BF16)
    return high, mid, low


def prepare_kernel(
    disp, mat_h, moduli_h, decay_h, strength_h, stiff, rates, perm, elems,
    points, mat, moduli, decay, strength, sems,
):
    moves = [
        pltpu.make_async_copy(src, dst, sems.at[n])
        for n, (src, dst) in enumerate(
            [(mat_h, mat), (moduli_h, moduli), (decay_h, decay), (strength_h, strength)]
        )
    ]
    for move in moves:
        move.start()
    for c in range(4):
        hit = lax.broadcasted_iota(jnp.int32, (128, 512), 1) == (
            4 * lax.broadcasted_iota(jnp.int32, (128, 512), 0) + c
        )
        perm[128 * c : 128 * c + 128, :] = jnp.where(hit, 1.0, 0.0).astype(BF16)
    points[...] = jnp.zeros(points.shape, F32)
    for comp in range(3):
        for a in range(4):
            base = (comp * 4 + a) * 8
            points[base : base + 4, :] = disp[comp, a]
    to_nodes(points[...], perm, elems)
    for move in moves:
        move.wait()
    onehot = [mat[0] == m for m in range(8)]
    for k in range(6):
        for l in range(k, 6):
            value = jnp.zeros((1, 128), F32)
            for m in range(8):
                value = jnp.where(onehot[m], moduli[k, m, l], value)
            stiff[6 * k + l : 6 * k + l + 1, :] = value
    for l in range(3):
        rates[l : l + 1, :] = jnp.full((1, 128), decay[l], F32)
        rates[3 + l : 4 + l, :] = jnp.full((1, 128), (1.0 - decay[l]) * strength[l], F32)


def unpack_kernel(memory, rates, _, decayed, flag, old):
    for d in range(5):
        for a in range(5):
            for b in range(5):
                for c in range(5):
                    row = (b * 5 + c) * 4
                    old[row : row + 3, :] = memory[d, a, b, c].astype(F32)
            for c in range(5):
                for l in range(3):
                    was = old[pl.ds(4 * c + l, 8, stride=20), :]
                    decayed[((d * 5 + a) * 5 + c) * 3 + l] = rates[l : l + 1, :] * was
    flag[...] = jnp.zeros((8, 128), F32)


def repack_kernel(dense, memory_new, flag, new):
    for d in range(5):
        for a in range(5):
            for c in range(5):
                for l in range(3):
                    new[pl.ds(4 * c + l, 8, stride=20), :] = dense[((d * 5 + a) * 5 + c) * 3 + l]
            for b in range(5):
                for c in range(5):
                    row = (b * 5 + c) * 4
                    memory_new[d, a, b, c] = new[row : row + 3, :].astype(BF16)
    flag[...] = jnp.zeros((8, 128), F32)


def to_nodes(points, perm, elems):
    rows = points.shape[0]
    parts = jnp.concatenate(split3(points), 0)
    taken = lax.dot_general(
        parts, perm[...], (((1,), (1,)), ((), ())), preferred_element_type=F32
    )
    taken = taken[0:rows] + taken[rows : 2 * rows] + taken[2 * rows : 3 * rows]
    for c in range(4):
        elems[c] = taken[:, 128 * c : 128 * c + 128]
    lane = lanes((rows, 128))
    elems[4] = jnp.where(lane < 127, pltpu.roll(taken[:, 0:128], 127, 1), 0.0)


def elastic_kernel(
    lat_first, lat_second, lon_first, lon_second, stiff, rates, perm, own, decayed,
    dense, force, lat_force, lon_force,
    points, edge, elems, devs, flux,
):
    following = has_next()
    _, lat_above = arrived("lat", lat_first, lat_second)
    _, lon_above = arrived("lon", lon_first, lon_second)
    points[...] = jnp.zeros(points.shape, F32)
    for comp in range(3):
        points[8 * comp : 8 * comp + 4, :] = following * lat_above[4 * comp : 4 * comp + 4]
        points[8 * comp + 4 : 8 * comp + 5, :] = following * lat_above[16 + comp : 17 + comp]
    points[24:36, :] = lon_above[0:12]
    to_nodes(points[...], perm, edge)
    fifth = sublanes((8, 128)) == 4
    for c in range(5):
        for comp in range(3):
            for a in range(4):
                base, row = (comp * 5 + a) * 8, 24 + 4 * comp + a
                kept = own[c, (comp * 4 + a) * 8 : (comp * 4 + a) * 8 + 8, :]
                elems[c, base : base + 8, :] = jnp.where(
                    fifth, row_of(edge[c, 24:40, :], row - 24, 8), kept
                )
            base = (comp * 5 + 4) * 8
            elems[c, base : base + 8, :] = edge[c, 8 * comp : 8 * comp + 8, :]
    lane = lanes((128, 128))
    slopes = [
        by_index(sublanes((8, 128)), [2.0 * DERIV[b][p] for b in range(5)] + [0.0])
        for p in range(5)
    ]
    turned = [
        by_index(sublanes((8, 128)), [2.0 * DERIV[p][b] for b in range(5)] + [0.0])
        for p in range(5)
    ]
    weight_col = by_index(sublanes((8, 128)), W + [0.0])

    def slab(comp, a, c):
        base = (comp * 5 + a) * 8
        return elems[c, base : base + 8, :]

    def along_lon(cols, value):
        total = None
        for p in range(5):
            term = cols[p] * row_of(value, p, 8)
            total = term if total is None else total + term
        return total

    for a in range(5):
        elastic_of = []
        for c in range(5):
            dx, dy, dz = [], [], []
            for comp in range(3):
                dx.append(mix([2.0 * DERIV[a][p] for p in range(5)], [slab(comp, p, c) for p in range(5)]))
                dy.append(along_lon(slopes, slab(comp, a, c)))
                dz.append(mix([2.0 * DERIV[c][p] for p in range(5)], [slab(comp, a, p) for p in range(5)]))
            strain = [dx[0], dy[1], dz[2], dy[0] + dx[1], dz[0] + dx[2], dz[1] + dy[2]]
            elastic = []
            for k in range(6):
                total = None
                for l in range(6):
                    pos = 6 * min(k, l) + max(k, l)
                    term = stiff[pos : pos + 1, :] * strain[l]
                    total = term if total is None else total + term
                elastic.append(total)
            pressure = (elastic[0] + elastic[1] + elastic[2]) * (1.0 / 3.0)
            dev = [elastic[0] - pressure, elastic[1] - pressure, elastic[3], elastic[4], elastic[5]]
            for d in range(5):
                devs[d * 5 + c] = dev[d]
            elastic_of.append(elastic)
        relaxed = []
        for d in range(5):
            sums = []
            for c in range(5):
                dev = devs[d * 5 + c]
                total = None
                for l in range(3):
                    pos = ((d * 5 + a) * 5 + c) * 3 + l
                    now = decayed[pos] + rates[3 + l : 4 + l, :] * dev
                    now = now.astype(BF16).astype(F32)
                    dense[pos] = now
                    total = now if total is None else total + now
                sums.append(total)
            relaxed.append(sums)
        for c in range(5):
            e = elastic_of[c]
            r = [relaxed[d][c] for d in range(5)]
            weight = weight_col * (W[a] * W[c] / 8.0)
            stress = [e[0] - r[0], e[1] - r[1], e[2] + r[0] + r[1], e[3] - r[2], e[4] - r[3], e[5] - r[4]]
            for k in range(6):
                flux[k, a * 5 + c] = jnp.where(weight_col > 0.0, weight * stress[k], 0.0)
    flux_of = [[0, 3, 4], [3, 1, 5], [4, 5, 2]]
    for c in range(5):
        elems[c, 120:128, :] = jnp.zeros((8, 128), F32)
        for comp in range(3):
            for a in range(5):
                value = mix(
                    [2.0 * DERIV[p][a] for p in range(5)],
                    [flux[flux_of[comp][0], p * 5 + c] for p in range(5)],
                )
                value = value + along_lon(turned, flux[flux_of[comp][1], a * 5 + c])
                value = value + mix(
                    [2.0 * DERIV[p][c] for p in range(5)],
                    [flux[flux_of[comp][2], a * 5 + p] for p in range(5)],
                )
                base = (comp * 5 + a) * 8
                elems[c, base : base + 8, :] = value
    carried = jnp.where(lane > 0, pltpu.roll(elems[4], 1, 1), 0.0)
    merged = jnp.concatenate([elems[0] + carried, elems[1], elems[2], elems[3]], 1)
    parts = jnp.concatenate(split3(merged), 0)
    given = jnp.dot(parts, perm[...], preferred_element_type=F32)
    given = given[0:128] + given[128:256] + given[256:384]
    lat_force[12:16, :] = jnp.zeros((4, 512), F32)
    lon_force[15:16, :] = jnp.zeros((1, 512), F32)
    for comp in range(3):
        for a in range(5):
            base = (comp * 5 + a) * 8
            if a < 4:
                force[comp, a] = given[base : base + 4]
                lon_force[5 * comp + a : 5 * comp + a + 1, :] = given[base + 4 : base + 5]
            else:
                lat_force[4 * comp : 4 * comp + 4, :] = given[base : base + 4]
                lon_force[5 * comp + 4 : 5 * comp + 5, :] = given[base + 4 : base + 5]


def call(kernel, name, outs, ins, args, scratch=(), flops=1000000, moved=500000, vmem=24):
    return pl.pallas_call(
        kernel,
        name=name,
        out_shape=[jax.ShapeDtypeStruct(s, d) for s, d in outs],
        in_specs=ins,
        out_specs=[VMEM] * len(outs),
        scratch_shapes=list(scratch),
        compiler_params=pltpu.CompilerParams(vmem_limit_bytes=vmem * 1024 * 1024),
        cost_estimate=pl.CostEstimate(flops=flops, bytes_accessed=moved, transcendentals=0),
    )(*args)


def swap(array, axis, size, parity):
    pairs = []
    for i in range(parity, size, 2):
        j = (i + 1) % size
        pairs += [(i, j), (j, i)]
    return lax.ppermute(array, axis, pairs)


def swap_lat(first, second):
    return swap(first, "lat", LAT, 0), swap(second, "lat", LAT, 1)


def swap_lon(first, second):
    other = swap(second, "lon", LON, 1)
    return swap(first, "lon", LON, 0), other


def per_device(
    displacement, velocity, acceleration, potential, memory_vars, materials, shell_flags,
    moduli, densities, decay, strength,
):
    field = ((4, 4, 512), F32)
    vector = ((3, 4, 4, 512), F32)
    r8, r16, r24, r32, r40 = (((n, 512), F32) for n in (8, 16, 24, 32, 40))
    info = ((8, 128), F32)
    kept = pltpu.with_memory_space_constraint
    disp, phi, own_info, *sent = call(
        start_kernel, "start", [vector, field, info, r16, r24], [HBM] * 7,
        [
            kept(array, pltpu.HBM)
            for array in (
                displacement, velocity, acceleration, potential, materials, shell_flags, densities
            )
        ],
        [
            pltpu.VMEM((3, 4, 4, 512), F32),
            pltpu.VMEM((3, 4, 4, 512), F32),
            pltpu.VMEM((3, 4, 4, 512), F32),
            pltpu.VMEM((1, 1, 128), jnp.int32),
            pltpu.VMEM((1, 1, 128), jnp.int32),
            pltpu.SMEM((8,), F32),
            pltpu.SemaphoreType.DMA((7,)),
        ],
    )
    lon_a = swap_lon(*sent)
    tables = call(
        prepare_kernel, "prepare",
        [((40, 128), F32), info, ((512, 512), BF16), ((5, 96, 128), F32)],
        [VMEM] + [HBM] * 4,
        [disp]
        + [
            kept(array, pltpu.HBM)
            for array in (materials, moduli.transpose(1, 0, 2), decay, strength)
        ],
        [
            pltpu.VMEM((96, 512), F32),
            pltpu.VMEM((1, 1, 128), jnp.int32),
            pltpu.SMEM((6, 8, 6), F32),
            pltpu.SMEM((3,), F32),
            pltpu.SMEM((3,), F32),
            pltpu.SemaphoreType.DMA((4,)),
        ],
    )
    lat_a = call(
        pack_kernel, "pack", [r24, r24], [VMEM] * 6,
        (disp, phi, own_info, *lon_a, tables[1]),
    )
    halo_a = (*swap_lat(*lat_a), *lon_a)
    memory = memory_vars.reshape(3, 5, 5, 5, 5, 128).transpose(1, 2, 3, 4, 0, 5)
    every = ((375, 8, 128), F32)
    decayed, unpacked = call(
        unpack_kernel, "unpack", [every, info], [VMEM] * 3, (memory, tables[1], lat_a[0]),
        [pltpu.VMEM((160, 128), F32)],
    )
    coef, precond, w0, *sent = call(
        residual_kernel, "residual", [r40, field, field, r8, r8, r8, r16], [VMEM] * 8,
        (disp, phi, own_info, *halo_a, unpacked),
    )
    lon_b = swap_lon(*sent[2:])
    halo_b = (*swap_lat(*sent[:2]), *lon_b)
    dense, force, lat_force, lon_force = call(
        elastic_kernel, "elastic", [every, vector, r16, r16], [VMEM] * 9,
        (*halo_a, *tables, decayed),
        [
            pltpu.VMEM((48, 512), F32),
            pltpu.VMEM((5, 48, 128), F32),
            pltpu.VMEM((5, 128, 128), F32),
            pltpu.VMEM((25, 8, 128), F32),
            pltpu.VMEM((6, 25, 8, 128), F32),
        ],
        flops=20000000, moved=2000000,
    )
    w1, *sent = call(
        second_kernel, "second", [field, r8, r8, r24, r32], [VMEM] * 8,
        (w0, coef, precond, *halo_b, lon_force),
    )
    lon_c = swap_lon(*sent[2:])
    halo_c = (*swap_lat(*sent[:2]), *lon_c)
    memory_new, packed = call(
        repack_kernel, "repack", [((5, 5, 5, 5, 3, 128), BF16), info], [VMEM], (dense,),
        [pltpu.VMEM((160, 128), F32)],
    )
    w2, *sent = call(
        third_kernel, "third", [field, r24, r24, r8, r32], [VMEM] * 9,
        (w1, coef, precond, *halo_c, lat_force, packed),
    )
    lon_d = swap_lon(*sent[2:])
    halo_d = (*swap_lat(*sent[:2]), *lon_d)
    rho_coef, disp_new, dense_done = call(
        density_kernel, "density", [r32, vector, info], [VMEM] * 3, (coef, disp, sent[0])
    )
    (line,) = call(
        moment_kernel, "moments", [((LAT * LON, 128), F32)], [VMEM] * 10,
        (w0, w1, w2, coef, precond, *halo_d, dense_done),
    )
    moments = lax.all_to_all(line, AXES, 0, 0, tiled=True)
    phi_new, acc_new, vel_new = call(
        final_kernel, "final", [field, vector, vector], [VMEM] * 25,
        (
            moments, phi, w0, w1, w2, rho_coef, force, *halo_a, *halo_b, *halo_c, *halo_d,
            velocity, acceleration,
        ),
    )
    memory_new = memory_new.transpose(4, 0, 1, 2, 3, 5).reshape(memory_vars.shape)
    return (disp_new, vel_new, acc_new, phi_new, memory_new)


def solution(mesh):
    vector = P(None, "lat", "lon", None)
    scalar = P("lat", "lon", None)
    memory = P(None, None, None, "lat", None, "lon", None, None)
    return jax.shard_map(
        per_device,
        mesh=mesh,
        in_specs=(vector, vector, vector, scalar, memory, scalar, scalar, P(), P(), P(), P()),
        out_specs=(vector, vector, vector, scalar, memory),
        check_vma=False,
    )
```

```python
import jax
import jax.numpy as jnp
import numpy as np
from jax import lax
from jax.experimental import pallas as pl
from jax.experimental.pallas import tpu as pltpu
from jax.sharding import PartitionSpec as P

TIME_STEP = 0.1
F32 = jnp.float32
BF16 = jnp.bfloat16
LAT, LON = 8, 32
AXES = ("lat", "lon")
VMEM = pl.BlockSpec(memory_space=pltpu.VMEM)
HBM = pl.BlockSpec(memory_space=pltpu.HBM)


def gll():
    points = np.array([-1.0, -np.sqrt(3.0 / 7.0), 0.0, np.sqrt(3.0 / 7.0), 1.0])
    weights = np.array([0.1, 49.0 / 90.0, 32.0 / 45.0, 49.0 / 90.0, 0.1])
    differ = points[:, None] - points[None, :] + np.eye(5)
    factors = np.prod(differ, axis=1)
    deriv = factors[:, None] / factors[None, :] / differ * (1.0 - np.eye(5))
    deriv = deriv - np.eye(5) * np.sum(deriv, axis=1)[:, None]
    return deriv, weights


DERIV, WEIGHTS = gll()
W = [float(v) for v in WEIGHTS]
M_POISSON = (DERIV.T @ np.diag(WEIGHTS) @ DERIV).tolist()
M_SOURCE = (np.diag(WEIGHTS) @ DERIV).T.tolist()
M_GRAVITY = (np.diag(WEIGHTS) @ DERIV).tolist()


def lanes(shape):
    return lax.broadcasted_iota(jnp.int32, shape, len(shape) - 1)


def sublanes(shape):
    return lax.broadcasted_iota(jnp.int32, shape, len(shape) - 2)


def by_index(index, values):
    out = jnp.full(index.shape, float(values[-1]), F32)
    for pos in range(len(values) - 2, -1, -1):
        out = jnp.where(index == pos, float(values[pos]), out)
    return out


def column(values, rows=4, width=512):
    return by_index(sublanes((rows, width)), list(values))


def row_of(array, pos, rows=4):
    return jnp.broadcast_to(array[pos : pos + 1], (rows, array.shape[1]))


def radial(field, matrix):
    lane = lanes((4, 512))
    node = lane & 3
    own, before = None, None
    for shift in range(-4, 5):
        moved = field if shift == 0 else pltpu.roll(field, (-shift) % 512, 1)
        if shift > -4:
            factors = [
                matrix[c][c + shift] if 0 <= c + shift <= 4 else 0.0 for c in range(4)
            ]
            table = by_index(node, factors)
            if shift > 0:
                table = jnp.where(lane < 512 - shift, table, 0.0)
            own = table * moved if own is None else own + table * moved
        if shift <= 0:
            term = float(matrix[4][4 + shift]) * moved
            before = term if before is None else before + term
    return own, before


def mix(matrix_row, arrays):
    total = None
    for factor, array in zip(matrix_row, arrays):
        term = float(factor) * array
        total = term if total is None else total + term
    return total


def lat_part(fields, above, below, matrix, own_row, back_row):
    out = []
    for i in range(4):
        value = own_row * mix(matrix[i], fields + [above])
        if i == 0:
            value = value + back_row * (float(matrix[4][4]) * fields[0] + below)
        out.append(value)
    return out


def lon_part(fields, above, below, matrix, own_col, back_col):
    columns = [column([matrix[b][p] for b in range(4)]) for p in range(5)]
    first = column([1.0, 0.0, 0.0, 0.0])
    out = []
    for i in range(4):
        value = columns[4] * row_of(above, i)
        for p in range(4):
            value = value + columns[p] * row_of(fields[i], p)
        edge = float(matrix[4][4]) * fields[i][0:1] + below[i : i + 1]
        kind = min(i, 1)
        value = own_col[kind] * value + first * (back_col[kind] * edge)
        out.append(W[i] * value)
    return out


def radial_part(fields, matrix, own, before):
    out = []
    for i in range(4):
        first, second = radial(fields[i], matrix)
        kind = min(i, 1)
        out.append(W[i] * (own[kind] * first + before[kind] * second))
    return out


def partial_lat(fields, matrix):
    return mix(matrix[4][:4], fields)


def partial_lon(field, matrix):
    weighted = column(matrix[4][:4]) * field
    return jnp.sum(weighted, axis=0, keepdims=True)


def even(axis):
    return lax.rem(lax.axis_index(axis), 2) == 0


def pick(axis, for_even, for_odd):
    return jnp.where(even(axis), for_even, for_odd)


def post(axis, outs, up, down):
    for out, sent in zip(outs, (pick(axis, up, down), pick(axis, down, up))):
        out[...] = sent[: out.shape[0]]


def arrived(axis, first, second):
    height = min(first.shape[0], second.shape[0])
    first, second = first[0:height], second[0:height]
    return pick(axis, second, first), pick(axis, first, second)


def stack(rows, height):
    total = sum(r.shape[0] for r in rows)
    if total < height:
        rows = rows + [jnp.zeros((height - total, 512), F32)]
    return jnp.concatenate(rows, 0)


def messages(fields, lat_out, lon_out, extra_lat=(), extra_lon=()):
    up = [partial_lat(fields, M_POISSON), partial_lat(fields, M_GRAVITY)]
    height = max(out.shape[0] for out in lat_out)
    post("lat", lat_out, stack(up + list(extra_lat), height), stack([fields[0]], height))
    up = [partial_lon(fields[i], M_POISSON) for i in range(4)]
    up += [partial_lon(fields[i], M_GRAVITY) for i in range(4)]
    down = [fields[i][0:1] for i in range(4)]
    height = max(out.shape[0] for out in lon_out)
    post("lon", lon_out, stack(up + list(extra_lon), height), stack(down, height))


def has_next():
    return jnp.where(lax.axis_index("lat") < LAT - 1, 1.0, 0.0).astype(F32)


def has_before():
    return jnp.where(lax.axis_index("lat") > 0, 1.0, 0.0).astype(F32)


def start_kernel(
    disp_h, vel_h, acc_h, phi_h, mat_h, flag_h, dens_h,
    disp_out, phi_out, info_out, lon0, lon1,
    disp, vel, acc, mat, flag, dens, sems,
):
    moves = [
        pltpu.make_async_copy(src, dst, sems.at[n])
        for n, (src, dst) in enumerate(
            [
                (mat_h, mat), (flag_h, flag), (dens_h, dens), (phi_h, phi_out),
                (disp_h, disp), (vel_h, vel), (acc_h, acc),
            ]
        )
    ]
    for move in moves:
        move.start()
    for move in moves[:3]:
        move.wait()
    rho = jnp.zeros((1, 128), F32)
    for m in range(8):
        rho = jnp.where(mat[0] == m, dens[m], rho)
    shell = 1.0 + flag[0].astype(F32)
    info = jnp.concatenate([rho, shell, jnp.zeros((1, 256), F32)], 1)
    info_out[...] = jnp.concatenate([rho, shell, jnp.zeros((6, 128), F32)], 0)
    moves[3].wait()
    potential = [phi_out[i] for i in range(4)]
    for move in moves[4:]:
        move.wait()
    u = []
    for comp in range(3):
        planes = []
        for i in range(4):
            value = (
                disp[comp, i]
                + TIME_STEP * vel[comp, i]
                + 0.5 * TIME_STEP * TIME_STEP * acc[comp, i]
            )
            disp_out[comp, i] = value
            planes.append(value)
        u.append(planes)
    up = [partial_lon(u[1][i], M_SOURCE) for i in range(4)]
    up += [partial_lon(potential[i], M_POISSON) for i in range(4)]
    up += [partial_lon(potential[i], M_GRAVITY) for i in range(4)]
    down = [u[comp][i][0:1] for comp in range(3) for i in range(4)]
    down += [potential[i][0:1] for i in range(4)]
    post("lon", (lon0, lon1), stack(up + [info], 16), stack(down, 16))

def pack_kernel(lon_second, lon_first, disp, phi, own_info, _, lat0, lat1):
    below, above = arrived("lon", lon_first, lon_second)
    potential = [phi[i] for i in range(4)]
    info = jnp.concatenate(
        [own_info[0:1, :], own_info[1:2, :], jnp.zeros((1, 256), F32)], 1
    )
    up = [
        partial_lat([disp[0, i] for i in range(4)], M_SOURCE),
        partial_lat(potential, M_POISSON),
        partial_lat(potential, M_GRAVITY),
        info,
        below[12:13],
    ]
    down = [disp[0, 0], disp[1, 0], disp[2, 0], potential[0]]
    down += [above[4 * comp : 4 * comp + 1] for comp in range(3)]
    post("lat", (lat0, lat1), stack(up, 24), stack(down, 24))


def lat_rows(factor):
    cols, first = column(W[:4]), column([W[0], 0.0, 0.0, 0.0])
    own = cols * row_of(factor, 0) + first * row_of(factor, 2)
    back = cols * row_of(factor, 1) + first * row_of(factor, 3)
    return own, back


def lon_cols(factor):
    own = (factor[0:1] + factor[1:2], factor[0:1])
    back = (factor[2:3] + factor[3:4], factor[2:3])
    return own, back


def radial_tools():
    lane = lanes((4, 512))
    node = lane & 3
    joint = jnp.logical_and(node == 0, lane >= 4)
    weight = by_index(node, W[:4])

    def earlier(factor):
        return jnp.where(joint, pltpu.roll(factor, 4, 1), 0.0)

    def weighted(factor):
        return weight * factor + W[4] * earlier(factor)

    return node, weight, earlier, weighted


def density_kernel(coef, disp, _, rho_coef, disp_new, flag):
    _, _, earlier, weighted = radial_tools()
    rho, inverse = coef[28:32, :], coef[32:36, :]
    r_points = 0.25 * weighted(rho)
    r_own, r_back = lat_rows(r_points)
    r_col, r_col_back = lon_cols(r_points)
    scaled = 0.25 * rho * inverse
    g_own, g_back = lat_rows(scaled)
    h_own, h_back = lat_rows(earlier(scaled))
    rho_coef[0:4, :] = r_own
    rho_coef[4:8, :] = r_back
    rho_coef[8:12, :] = g_own + g_back
    rho_coef[12:16, :] = g_own
    rho_coef[16:20, :] = h_own + h_back
    rho_coef[20:24, :] = h_own
    rho_coef[24:25, :] = r_col[0]
    rho_coef[25:26, :] = r_col[1]
    rho_coef[26:27, :] = r_col_back[0]
    rho_coef[27:28, :] = r_col_back[1]
    flag[...] = jnp.zeros((8, 128), F32)
    disp_new[...] = disp[...]


def residual_kernel(
    disp_new, phi, own_info, lon_second, lat_first, lat_second, lon_first, _,
    coef, precond_out, w0_out, lat0, lat1, lon0, lon1,
):
    following, before = has_next(), has_before()
    lat_below, lat_above = arrived("lat", lat_first, lat_second)
    lon_below, lon_above = arrived("lon", lon_first, lon_second)
    rho, shell = (
        jnp.concatenate(
            [
                own_info[n : n + 1, :],
                before * lat_below[12:13, 128 * n : 128 * n + 128],
                lon_below[12:13, 128 * n : 128 * n + 128],
                before * lat_below[13:14, 128 * n : 128 * n + 128],
            ],
            0,
        )
        for n in range(2)
    )
    spread = (
        lax.broadcasted_iota(jnp.int32, (128, 512), 1) // 4
        == lax.broadcasted_iota(jnp.int32, (128, 512), 0)
    )
    spread = jnp.where(spread, 1.0, 0.0).astype(BF16)
    high, mid, low = split3(rho)
    parts = jnp.concatenate(
        [high.astype(F32), mid.astype(F32), low.astype(F32), shell], 0
    ).astype(BF16)
    parts = jnp.dot(parts, spread, preferred_element_type=F32)
    rho = parts[0:4] + parts[4:8] + parts[8:12]
    shell = parts[12:16]
    flagged = shell > 1.5
    valid = shell > 0.5
    stretch = jnp.where(valid, jnp.where(flagged, 3.0, 1.0), 0.0)
    inverse = jnp.where(valid, jnp.where(flagged, 1.0 / 3.0, 1.0), 0.0)
    rho_in = jnp.where(flagged, 0.0, rho)
    node, weight, earlier, weighted = radial_tools()
    s_points = 0.5 * weighted(stretch)
    s_own, s_back = lat_rows(s_points)
    s_col, s_col_back = lon_cols(s_points)
    i_own, i_back = lat_rows(0.5 * inverse)
    j_own, j_back = lat_rows(0.5 * earlier(inverse))
    i_both, j_both = (i_own + i_back, i_own), (j_own + j_back, j_own)
    coef[0:4, :] = s_own
    coef[4:8, :] = s_back
    coef[8:12, :] = i_both[0]
    coef[12:16, :] = i_both[1]
    coef[16:20, :] = j_both[0]
    coef[20:24, :] = j_both[1]
    coef[24:25, :] = s_col[0]
    coef[25:26, :] = s_col[1]
    coef[26:27, :] = s_col_back[0]
    coef[27:28, :] = s_col_back[1]
    coef[28:32, :] = rho
    coef[32:36, :] = inverse
    q_points = 0.25 * weighted(rho_in)
    q_own, q_back = lat_rows(q_points)
    q_col, q_col_back = lon_cols(q_points)
    t_own, t_back = lat_rows(0.25 * rho_in)
    v_own, v_back = lat_rows(0.25 * earlier(rho_in))

    u = [[disp_new[comp, i] for i in range(4)] for comp in range(3)]
    potential = [phi[i] for i in range(4)]
    source_x = lat_part(
        u[0], following * lat_above[0:4, :], lat_below[0:4, :], M_SOURCE, q_own, q_back
    )
    source_y = lon_part(
        u[1], lon_above[4:8, :], lon_below[0:4, :], M_SOURCE, q_col, q_col_back
    )
    source_z = radial_part(u[2], M_SOURCE, (t_own + t_back, t_own), (v_own + v_back, v_own))
    image_x = lat_part(
        potential, following * lat_above[12:16, :], lat_below[4:8, :], M_POISSON, s_own, s_back
    )
    image_y = lon_part(
        potential, lon_above[12:16, :], lon_below[4:8, :], M_POISSON, s_col, s_col_back
    )
    image_z = radial_part(potential, M_POISSON, i_both, j_both)
    diag = [M_POISSON[a][a] for a in range(5)]
    diag_node = by_index(node, diag[:4])
    diag_col = column(diag[:4])
    first = column([1.0, 0.0, 0.0, 0.0])
    w0 = []
    for i in range(4):
        kind = min(i, 1)
        precond = diag[i] * s_own
        if i == 0:
            precond = precond + diag[4] * s_back
        precond = precond + W[i] * (
            diag_col * s_col[kind]
            + first * (diag[4] * s_col_back[kind])
            + i_both[kind] * diag_node
            + diag[4] * j_both[kind]
        )
        precond_out[i] = precond
        source = -(source_x[i] + source_y[i] + source_z[i])
        image = image_x[i] + image_y[i] + image_z[i]
        value = (source - image) / precond
        w0_out[i] = value
        w0.append(value)
    messages(w0, (lat0, lat1), (lon0, lon1))


def poisson(fields, coef, lon_second, lat_first, lat_second, lon_first):
    following = has_next()
    lat_below, lat_above = arrived("lat", lat_first, lat_second)
    lon_below, lon_above = arrived("lon", lon_first, lon_second)
    s_col = (coef[24:25, :], coef[25:26, :])
    s_col_back = (coef[26:27, :], coef[27:28, :])
    x = lat_part(
        fields, following * lat_above[0:4, :], lat_below[0:4, :], M_POISSON, coef[0:4, :], coef[4:8, :]
    )
    y = lon_part(fields, lon_above[0:4, :], lon_below[0:4, :], M_POISSON, s_col, s_col_back)
    z = radial_part(
        fields, M_POISSON, (coef[8:12, :], coef[12:16, :]), (coef[16:20, :], coef[20:24, :])
    )
    return [x[i] + y[i] + z[i] for i in range(4)]


def step(field, coef, precond, halo, out):
    fields = [field[i] for i in range(4)]
    image = poisson(fields, coef, *halo)
    result = []
    for i in range(4):
        value = image[i] / precond[i] - fields[i]
        out[i] = value
        result.append(value)
    return result


def second_kernel(
    field, coef, precond, lon_second, lat_first, lat_second, lon_first, lon_force,
    out, lat0, lat1, lon0, lon1,
):
    result = step(field, coef, precond, (lon_second, lat_first, lat_second, lon_first), out)
    messages(result, (lat0, lat1), (lon0, lon1), (), (lon_force[...],))


def third_kernel(
    field, coef, precond, lon_second, lat_first, lat_second, lon_first, lat_force, _,
    out, lat0, lat1, lon0, lon1,
):
    result = step(field, coef, precond, (lon_second, lat_first, lat_second, lon_first), out)
    below, _ = arrived("lon", lon_first, lon_second)
    first = column([1.0, 0.0, 0.0, 0.0])
    edges = []
    for comp in range(3):
        corner = 12 + 5 * comp
        edges.append(
            lat_force[4 * comp : 4 * comp + 4, :] + first * below[corner : corner + 1]
        )
    messages(result, (lat0, lat1), (lon0, lon1), edges)


def moment_kernel(
    w0, w1, w2, coef, precond, lon_second, lat_first, lat_second, lon_first, _, out
):
    fields = [w2[i] for i in range(4)]
    image = poisson(fields, coef, lon_second, lat_first, lat_second, lon_first)
    sums = [None] * 6
    for i in range(4):
        m = precond[i]
        a, b, c = w0[i], w1[i], w2[i]
        ma, mb, mc = m * a, m * b, m * c
        terms = [a * ma, b * ma, b * mb, c * mb, c * mc, c * (image[i] - mc)]
        for k in range(6):
            sums[k] = terms[k] if sums[k] is None else sums[k] + terms[k]
    lane = lanes((1, 128))
    line = jnp.zeros((1, 128), F32)
    for k in range(6):
        total = jnp.sum(jnp.sum(sums[k], axis=0, keepdims=True), axis=1, keepdims=True)
        line = jnp.where(lane == k, total, line)
    out[...] = jnp.broadcast_to(line, out.shape)


def cg_coefficients(mu):
    zero = jnp.zeros_like(mu[0])

    def inner(a):
        total = zero
        for i in range(len(a)):
            for j in range(len(a)):
                total = total + a[i] * a[j] * mu[i + j]
        return total

    def energy(a):
        total = zero
        for i in range(len(a)):
            for j in range(len(a)):
                total = total + a[i] * a[j] * (mu[i + j + 1] + mu[i + j])
        return total

    def ratio(a, b):
        return jnp.where(b == 0.0, 0.0, a / jnp.where(b == 0.0, 1.0, b))

    y = [zero, zero, zero]
    z = [zero + 1.0]
    search = [zero + 1.0]
    rz = mu[0]
    for step in range(3):
        length = ratio(rz, energy(search))
        for i in range(len(search)):
            y[i] = y[i] + length * search[i]
        if step < 2:
            grown = [zero] * (len(search) + 1)
            for i in range(len(search)):
                grown[i] = grown[i] + search[i]
                grown[i + 1] = grown[i + 1] + search[i]
            z = z + [zero]
            z = [z[i] - length * grown[i] for i in range(len(z))]
            rz_next = inner(z)
            beta = ratio(rz_next, rz)
            padded = search + [zero]
            search = [z[i] + beta * padded[i] for i in range(len(z))]
            rz = rz_next
    return y


def final_kernel(
    moments, phi, w0, w1, w2, rho_coef, own_force,
    a0, a1, a2, a3, b0, b1, b2, b3, c0, c1, c2, c3, d0, d1, d2, d3,
    vel, acc, phi_new, acc_new, vel_new,
):
    total = jnp.sum(moments[...], axis=0, keepdims=True)
    lane = lanes((1, 128))
    mu = [
        jnp.broadcast_to(
            jnp.sum(jnp.where(lane == k, total, 0.0), axis=1, keepdims=True), (1, 128)
        )
        for k in range(6)
    ]
    y = cg_coefficients(mu)
    y = [jnp.concatenate([v] * 4, 1) for v in y]

    def combined(first, one, two, three):
        return first + y[0] * one + y[1] * two + y[2] * three

    potential = []
    for i in range(4):
        value = combined(phi[i], w0[i], w1[i], w2[i])
        phi_new[i] = value
        potential.append(value)
    following, before = has_next(), has_before()
    ma, na = arrived("lat", a1, a2)
    mb, nb = arrived("lat", b1, b2)
    mc, nc = arrived("lat", c1, c2)
    md, nd = arrived("lat", d1, d2)
    fa, ga = arrived("lon", a3, a0)
    fb, gb = arrived("lon", b3, b0)
    fc, gc = arrived("lon", c3, c0)
    fd, gd = arrived("lon", d3, d0)
    lat_below = combined(ma[8:12, :], mb[4:8, :], mc[4:8, :], md[4:8, :])
    lat_above = following * combined(na[12:16, :], nb[0:4, :], nc[0:4, :], nd[0:4, :])
    lon_below = combined(fa[8:12, :], fb[4:8, :], fc[4:8, :], fd[4:8, :])
    lon_above = combined(ga[12:16, :], gb[0:4, :], gc[0:4, :], gd[0:4, :])
    r_own, r_back = rho_coef[0:4, :], rho_coef[4:8, :]
    r_col = (rho_coef[24:25, :], rho_coef[25:26, :])
    r_col_back = (rho_coef[26:27, :], rho_coef[27:28, :])
    x = lat_part(potential, lat_above, lat_below, M_GRAVITY, r_own, r_back)
    y_part = lon_part(potential, lon_above, lon_below, M_GRAVITY, r_col, r_col_back)
    z = radial_part(
        potential,
        M_GRAVITY,
        (rho_coef[8:12, :], rho_coef[12:16, :]),
        (rho_coef[16:20, :], rho_coef[20:24, :]),
    )
    cols = column(W[:4])
    first = column([1.0, 0.0, 0.0, 0.0])
    gravity = (x, y_part, z)
    for i in range(4):
        mass = r_own + r_back if i == 0 else r_own
        mass = 0.5 * W[i] * mass
        for comp in range(3):
            force = own_force[comp, i]
            force = force + first * fc[8 + 5 * comp + i : 9 + 5 * comp + i, :]
            if i == 0:
                edge = md[8 + 4 * comp : 12 + 4 * comp, :]
                force = force + before * edge
            value = (-gravity[comp][i] - force) / mass
            acc_new[comp, i] = value
            vel_new[comp, i] = vel[comp, i] + 0.5 * TIME_STEP * (acc[comp, i] + value)


def split3(value):
    high = value.astype(BF16)
    rest = value - high.astype(F32)
    mid = rest.astype(BF16)
    low = (rest - mid.astype(F32)).astype(BF16)
    return high, mid, low


def prepare_kernel(
    disp, mat_h, moduli_h, decay_h, strength_h, stiff, rates, perm, elems,
    points, mat, moduli, decay, strength, sems,
):
    moves = [
        pltpu.make_async_copy(src, dst, sems.at[n])
        for n, (src, dst) in enumerate(
            [(mat_h, mat), (moduli_h, moduli), (decay_h, decay), (strength_h, strength)]
        )
    ]
    for move in moves:
        move.start()
    for c in range(4):
        hit = lax.broadcasted_iota(jnp.int32, (128, 512), 1) == (
            4 * lax.broadcasted_iota(jnp.int32, (128, 512), 0) + c
        )
        perm[128 * c : 128 * c + 128, :] = jnp.where(hit, 1.0, 0.0).astype(BF16)
    points[...] = jnp.zeros(points.shape, F32)
    for comp in range(3):
        for a in range(4):
            base = (comp * 4 + a) * 8
            points[base : base + 4, :] = disp[comp, a]
    to_nodes(points[...], perm, elems)
    for move in moves:
        move.wait()
    onehot = [mat[0] == m for m in range(8)]
    for k in range(6):
        for l in range(k, 6):
            value = jnp.zeros((1, 128), F32)
            for m in range(8):
                value = jnp.where(onehot[m], moduli[k, m, l], value)
            stiff[6 * k + l : 6 * k + l + 1, :] = value
    for l in range(3):
        rates[l : l + 1, :] = jnp.full((1, 128), decay[l], F32)
        rates[3 + l : 4 + l, :] = jnp.full((1, 128), (1.0 - decay[l]) * strength[l], F32)


def unpack_kernel(memory, rates, _, decayed, flag, old):
    for d in range(5):
        for a in range(5):
            for b in range(5):
                for c in range(5):
                    row = (b * 5 + c) * 4
                    old[row : row + 3, :] = memory[d, a, b, c].astype(F32)
            for c in range(5):
                for l in range(3):
                    was = old[pl.ds(4 * c + l, 8, stride=20), :]
                    decayed[((d * 5 + a) * 5 + c) * 3 + l] = rates[l : l + 1, :] * was
    flag[...] = jnp.zeros((8, 128), F32)


def repack_kernel(dense, memory_new, flag, new):
    for d in range(5):
        for a in range(5):
            for c in range(5):
                for l in range(3):
                    new[pl.ds(4 * c + l, 8, stride=20), :] = dense[((d * 5 + a) * 5 + c) * 3 + l]
            for b in range(5):
                for c in range(5):
                    row = (b * 5 + c) * 4
                    memory_new[d, a, b, c] = new[row : row + 3, :].astype(BF16)
    flag[...] = jnp.zeros((8, 128), F32)


def to_nodes(points, perm, elems):
    rows = points.shape[0]
    parts = jnp.concatenate(split3(points), 0)
    taken = lax.dot_general(
        parts, perm[...], (((1,), (1,)), ((), ())), preferred_element_type=F32
    )
    taken = taken[0:rows] + taken[rows : 2 * rows] + taken[2 * rows : 3 * rows]
    for c in range(4):
        elems[c] = taken[:, 128 * c : 128 * c + 128]
    lane = lanes((rows, 128))
    elems[4] = jnp.where(lane < 127, pltpu.roll(taken[:, 0:128], 127, 1), 0.0)


def elastic_kernel(
    lon_second, lat_first, lat_second, lon_first, stiff, rates, perm, own, decayed,
    dense, force, lat_force, lon_force,
    points, edge, elems, devs, flux,
):
    following = has_next()
    _, lat_above = arrived("lat", lat_first, lat_second)
    _, lon_above = arrived("lon", lon_first, lon_second)
    points[...] = jnp.zeros(points.shape, F32)
    for comp in range(3):
        points[8 * comp : 8 * comp + 4, :] = following * lat_above[4 * comp : 4 * comp + 4]
        points[8 * comp + 4 : 8 * comp + 5, :] = following * lat_above[16 + comp : 17 + comp]
    points[24:36, :] = lon_above[0:12]
    to_nodes(points[...], perm, edge)
    fifth = sublanes((8, 128)) == 4
    for c in range(5):
        for comp in range(3):
            for a in range(4):
                base, row = (comp * 5 + a) * 8, 24 + 4 * comp + a
                kept = own[c, (comp * 4 + a) * 8 : (comp * 4 + a) * 8 + 8, :]
                elems[c, base : base + 8, :] = jnp.where(
                    fifth, row_of(edge[c, 24:40, :], row - 24, 8), kept
                )
            base = (comp * 5 + 4) * 8
            elems[c, base : base + 8, :] = edge[c, 8 * comp : 8 * comp + 8, :]
    lane = lanes((128, 128))
    slopes = [
        by_index(sublanes((8, 128)), [2.0 * DERIV[b][p] for b in range(5)] + [0.0])
        for p in range(5)
    ]
    turned = [
        by_index(sublanes((8, 128)), [2.0 * DERIV[p][b] for b in range(5)] + [0.0])
        for p in range(5)
    ]
    weight_col = by_index(sublanes((8, 128)), W + [0.0])

    def slab(comp, a, c):
        base = (comp * 5 + a) * 8
        return elems[c, base : base + 8, :]

    def along_lon(cols, value):
        total = None
        for p in range(5):
            term = cols[p] * row_of(value, p, 8)
            total = term if total is None else total + term
        return total

    for a in range(5):
        elastic_of = []
        for c in range(5):
            dx, dy, dz = [], [], []
            for comp in range(3):
                dx.append(mix([2.0 * DERIV[a][p] for p in range(5)], [slab(comp, p, c) for p in range(5)]))
                dy.append(along_lon(slopes, slab(comp, a, c)))
                dz.append(mix([2.0 * DERIV[c][p] for p in range(5)], [slab(comp, a, p) for p in range(5)]))
            strain = [dx[0], dy[1], dz[2], dy[0] + dx[1], dz[0] + dx[2], dz[1] + dy[2]]
            elastic = []
            for k in range(6):
                total = None
                for l in range(6):
                    pos = 6 * min(k, l) + max(k, l)
                    term = stiff[pos : pos + 1, :] * strain[l]
                    total = term if total is None else total + term
                elastic.append(total)
            pressure = (elastic[0] + elastic[1] + elastic[2]) * (1.0 / 3.0)
            dev = [elastic[0] - pressure, elastic[1] - pressure, elastic[3], elastic[4], elastic[5]]
            for d in range(5):
                devs[d * 5 + c] = dev[d]
            elastic_of.append(elastic)
        relaxed = []
        for d in range(5):
            sums = []
            for c in range(5):
                dev = devs[d * 5 + c]
                total = None
                for l in range(3):
                    pos = ((d * 5 + a) * 5 + c) * 3 + l
                    now = decayed[pos] + rates[3 + l : 4 + l, :] * dev
                    now = now.astype(BF16).astype(F32)
                    dense[pos] = now
                    total = now if total is None else total + now
                sums.append(total)
            relaxed.append(sums)
        for c in range(5):
            e = elastic_of[c]
            r = [relaxed[d][c] for d in range(5)]
            weight = weight_col * (W[a] * W[c] / 8.0)
            stress = [e[0] - r[0], e[1] - r[1], e[2] + r[0] + r[1], e[3] - r[2], e[4] - r[3], e[5] - r[4]]
            for k in range(6):
                flux[k, a * 5 + c] = jnp.where(weight_col > 0.0, weight * stress[k], 0.0)
    flux_of = [[0, 3, 4], [3, 1, 5], [4, 5, 2]]
    for c in range(5):
        elems[c, 120:128, :] = jnp.zeros((8, 128), F32)
        for comp in range(3):
            for a in range(5):
                value = mix(
                    [2.0 * DERIV[p][a] for p in range(5)],
                    [flux[flux_of[comp][0], p * 5 + c] for p in range(5)],
                )
                value = value + along_lon(turned, flux[flux_of[comp][1], a * 5 + c])
                value = value + mix(
                    [2.0 * DERIV[p][c] for p in range(5)],
                    [flux[flux_of[comp][2], a * 5 + p] for p in range(5)],
                )
                base = (comp * 5 + a) * 8
                elems[c, base : base + 8, :] = value
    carried = jnp.where(lane > 0, pltpu.roll(elems[4], 1, 1), 0.0)
    merged = jnp.concatenate([elems[0] + carried, elems[1], elems[2], elems[3]], 1)
    parts = jnp.concatenate(split3(merged), 0)
    given = jnp.dot(parts, perm[...], preferred_element_type=F32)
    given = given[0:128] + given[128:256] + given[256:384]
    lat_force[12:16, :] = jnp.zeros((4, 512), F32)
    lon_force[15:16, :] = jnp.zeros((1, 512), F32)
    for comp in range(3):
        for a in range(5):
            base = (comp * 5 + a) * 8
            if a < 4:
                force[comp, a] = given[base : base + 4]
                lon_force[5 * comp + a : 5 * comp + a + 1, :] = given[base + 4 : base + 5]
            else:
                lat_force[4 * comp : 4 * comp + 4, :] = given[base : base + 4]
                lon_force[5 * comp + 4 : 5 * comp + 5, :] = given[base + 4 : base + 5]


def call(kernel, name, outs, ins, args, scratch=(), flops=1000000, moved=500000, vmem=24):
    return pl.pallas_call(
        kernel,
        name=name,
        out_shape=[jax.ShapeDtypeStruct(s, d) for s, d in outs],
        in_specs=ins,
        out_specs=[VMEM] * len(outs),
        scratch_shapes=list(scratch),
        compiler_params=pltpu.CompilerParams(vmem_limit_bytes=vmem * 1024 * 1024),
        cost_estimate=pl.CostEstimate(flops=flops, bytes_accessed=moved, transcendentals=0),
    )(*args)


def swap(array, axis, size, parity):
    pairs = []
    for i in range(parity, size, 2):
        j = (i + 1) % size
        pairs += [(i, j), (j, i)]
    return lax.ppermute(array, axis, pairs)


def swap_lat(first, second):
    return swap(first, "lat", LAT, 0), swap(second, "lat", LAT, 1)


def swap_lon(first, second):
    other = swap(second, "lon", LON, 1)
    return swap(first, "lon", LON, 0), other


def per_device(
    displacement, velocity, acceleration, potential, memory_vars, materials, shell_flags,
    moduli, densities, decay, strength,
):
    field = ((4, 4, 512), F32)
    vector = ((3, 4, 4, 512), F32)
    r8, r16, r24, r32, r40 = (((n, 512), F32) for n in (8, 16, 24, 32, 40))
    info = ((8, 128), F32)
    kept = pltpu.with_memory_space_constraint
    disp, phi, own_info, *sent = call(
        start_kernel, "start", [vector, field, info, r16, r16], [HBM] * 7,
        [
            kept(array, pltpu.HBM)
            for array in (
                displacement, velocity, acceleration, potential, materials, shell_flags, densities
            )
        ],
        [
            pltpu.VMEM((3, 4, 4, 512), F32),
            pltpu.VMEM((3, 4, 4, 512), F32),
            pltpu.VMEM((3, 4, 4, 512), F32),
            pltpu.VMEM((1, 1, 128), jnp.int32),
            pltpu.VMEM((1, 1, 128), jnp.int32),
            pltpu.SMEM((8,), F32),
            pltpu.SemaphoreType.DMA((7,)),
        ],
    )
    lon_a = swap_lon(*sent)
    tables = call(
        prepare_kernel, "prepare",
        [((40, 128), F32), info, ((512, 512), BF16), ((5, 96, 128), F32)],
        [VMEM] + [HBM] * 4,
        [disp]
        + [
            kept(array, pltpu.HBM)
            for array in (materials, moduli.transpose(1, 0, 2), decay, strength)
        ],
        [
            pltpu.VMEM((96, 512), F32),
            pltpu.VMEM((1, 1, 128), jnp.int32),
            pltpu.SMEM((6, 8, 6), F32),
            pltpu.SMEM((3,), F32),
            pltpu.SMEM((3,), F32),
            pltpu.SemaphoreType.DMA((4,)),
        ],
    )
    lat_a = call(
        pack_kernel, "pack", [r24, r24], [VMEM] * 6,
        (lon_a[1], lon_a[0], disp, phi, own_info, tables[1]),
    )
    halo_a = (lon_a[1], *swap_lat(*lat_a), lon_a[0])
    memory = memory_vars.reshape(3, 5, 5, 5, 5, 128).transpose(1, 2, 3, 4, 0, 5)
    every = ((375, 8, 128), F32)
    decayed, unpacked = call(
        unpack_kernel, "unpack", [every, info], [VMEM] * 3, (memory, tables[1], lat_a[0]),
        [pltpu.VMEM((160, 128), F32)],
    )
    coef, precond, w0, *sent = call(
        residual_kernel, "residual", [r40, field, field, r8, r8, r8, r8], [VMEM] * 8,
        (disp, phi, own_info, *halo_a, unpacked),
    )
    lon_b = swap_lon(*sent[2:])
    halo_b = (lon_b[1], *swap_lat(*sent[:2]), lon_b[0])
    dense, force, lat_force, lon_force = call(
        elastic_kernel, "elastic", [every, vector, r16, r16], [VMEM] * 9,
        (*halo_a, *tables, decayed),
        [
            pltpu.VMEM((48, 512), F32),
            pltpu.VMEM((5, 48, 128), F32),
            pltpu.VMEM((5, 128, 128), F32),
            pltpu.VMEM((25, 8, 128), F32),
            pltpu.VMEM((6, 25, 8, 128), F32),
        ],
        flops=20000000, moved=2000000,
    )
    w1, *sent = call(
        second_kernel, "second", [field, r8, r8, r24, r24], [VMEM] * 8,
        (w0, coef, precond, *halo_b, lon_force),
    )
    lon_c = swap_lon(*sent[2:])
    halo_c = (lon_c[1], *swap_lat(*sent[:2]), lon_c[0])
    memory_new, packed = call(
        repack_kernel, "repack", [((5, 5, 5, 5, 3, 128), BF16), info], [VMEM], (dense,),
        [pltpu.VMEM((160, 128), F32)],
    )
    w2, *sent = call(
        third_kernel, "third", [field, r24, r24, r8, r32], [VMEM] * 9,
        (w1, coef, precond, *halo_c, lat_force, packed),
    )
    lon_d = swap_lon(*sent[2:])
    halo_d = (lon_d[1], *swap_lat(*sent[:2]), lon_d[0])
    rho_coef, disp_new, dense_done = call(
        density_kernel, "density", [r32, vector, info], [VMEM] * 3, (coef, disp, sent[0])
    )
    (line,) = call(
        moment_kernel, "moments", [((LAT * LON, 128), F32)], [VMEM] * 10,
        (w0, w1, w2, coef, precond, *halo_d, dense_done),
    )
    moments = lax.all_to_all(line, AXES, 0, 0, tiled=True)
    phi_new, acc_new, vel_new = call(
        final_kernel, "final", [field, vector, vector], [VMEM] * 25,
        (
            moments, phi, w0, w1, w2, rho_coef, force, *halo_a, *halo_b, *halo_c, *halo_d,
            velocity, acceleration,
        ),
    )
    memory_new = memory_new.transpose(4, 0, 1, 2, 3, 5).reshape(memory_vars.shape)
    return (disp_new, vel_new, acc_new, phi_new, memory_new)


def solution(mesh):
    vector = P(None, "lat", "lon", None)
    scalar = P("lat", "lon", None)
    memory = P(None, None, None, "lat", None, "lon", None, None)
    return jax.shard_map(
        per_device,
        mesh=mesh,
        in_specs=(vector, vector, vector, scalar, memory, scalar, scalar, P(), P(), P(), P()),
        out_specs=(vector, vector, vector, scalar, memory),
        check_vma=False,
    )
```

```python
import jax
import jax.numpy as jnp
import numpy as np
from jax import lax
from jax.experimental import pallas as pl
from jax.experimental.pallas import tpu as pltpu
from jax.sharding import PartitionSpec as P

TIME_STEP = 0.1
F32 = jnp.float32
BF16 = jnp.bfloat16
LAT, LON = 8, 32
AXES = ("lat", "lon")
VMEM = pl.BlockSpec(memory_space=pltpu.VMEM)
HBM = pl.BlockSpec(memory_space=pltpu.HBM)


def gll():
    points = np.array([-1.0, -np.sqrt(3.0 / 7.0), 0.0, np.sqrt(3.0 / 7.0), 1.0])
    weights = np.array([0.1, 49.0 / 90.0, 32.0 / 45.0, 49.0 / 90.0, 0.1])
    differ = points[:, None] - points[None, :] + np.eye(5)
    factors = np.prod(differ, axis=1)
    deriv = factors[:, None] / factors[None, :] / differ * (1.0 - np.eye(5))
    deriv = deriv - np.eye(5) * np.sum(deriv, axis=1)[:, None]
    return deriv, weights


DERIV, WEIGHTS = gll()
W = [float(v) for v in WEIGHTS]
M_POISSON = (DERIV.T @ np.diag(WEIGHTS) @ DERIV).tolist()
M_SOURCE = (np.diag(WEIGHTS) @ DERIV).T.tolist()
M_GRAVITY = (np.diag(WEIGHTS) @ DERIV).tolist()


def lanes(shape):
    return lax.broadcasted_iota(jnp.int32, shape, len(shape) - 1)


def sublanes(shape):
    return lax.broadcasted_iota(jnp.int32, shape, len(shape) - 2)


def by_index(index, values):
    out = jnp.full(index.shape, float(values[-1]), F32)
    for pos in range(len(values) - 2, -1, -1):
        out = jnp.where(index == pos, float(values[pos]), out)
    return out


def column(values, rows=4, width=512):
    return by_index(sublanes((rows, width)), list(values))


def row_of(array, pos, rows=4):
    return jnp.broadcast_to(array[pos : pos + 1], (rows, array.shape[1]))


def radial(field, matrix):
    lane = lanes((4, 512))
    node = lane & 3
    own, before = None, None
    for shift in range(-4, 5):
        moved = field if shift == 0 else pltpu.roll(field, (-shift) % 512, 1)
        if shift > -4:
            factors = [
                matrix[c][c + shift] if 0 <= c + shift <= 4 else 0.0 for c in range(4)
            ]
            table = by_index(node, factors)
            if shift > 0:
                table = jnp.where(lane < 512 - shift, table, 0.0)
            own = table * moved if own is None else own + table * moved
        if shift <= 0:
            term = float(matrix[4][4 + shift]) * moved
            before = term if before is None else before + term
    return own, before


def mix(matrix_row, arrays):
    total = None
    for factor, array in zip(matrix_row, arrays):
        term = float(factor) * array
        total = term if total is None else total + term
    return total


def lat_part(fields, above, below, matrix, own_row, back_row):
    out = []
    for i in range(4):
        value = own_row * mix(matrix[i], fields + [above])
        if i == 0:
            value = value + back_row * (float(matrix[4][4]) * fields[0] + below)
        out.append(value)
    return out


def lon_part(fields, above, below, matrix, own_col, back_col):
    columns = [column([matrix[b][p] for b in range(4)]) for p in range(5)]
    first = column([1.0, 0.0, 0.0, 0.0])
    out = []
    for i in range(4):
        value = columns[4] * row_of(above, i)
        for p in range(4):
            value = value + columns[p] * row_of(fields[i], p)
        edge = float(matrix[4][4]) * fields[i][0:1] + below[i : i + 1]
        kind = min(i, 1)
        value = own_col[kind] * value + first * (back_col[kind] * edge)
        out.append(W[i] * value)
    return out


def radial_part(fields, matrix, own, before):
    out = []
    for i in range(4):
        first, second = radial(fields[i], matrix)
        kind = min(i, 1)
        out.append(W[i] * (own[kind] * first + before[kind] * second))
    return out


def partial_lat(fields, matrix):
    return mix(matrix[4][:4], fields)


def partial_lon(field, matrix):
    weighted = column(matrix[4][:4]) * field
    return jnp.sum(weighted, axis=0, keepdims=True)


def even(axis):
    return lax.rem(lax.axis_index(axis), 2) == 0


def pick(axis, for_even, for_odd):
    return jnp.where(even(axis), for_even, for_odd)


def post(axis, outs, up, down):
    for out, sent in zip(outs, (pick(axis, up, down), pick(axis, down, up))):
        out[...] = sent[: out.shape[0]]


def arrived(axis, first, second):
    height = min(first.shape[0], second.shape[0])
    first, second = first[0:height], second[0:height]
    return pick(axis, second, first), pick(axis, first, second)


def stack(rows, height):
    total = sum(r.shape[0] for r in rows)
    if total < height:
        rows = rows + [jnp.zeros((height - total, 512), F32)]
    return jnp.concatenate(rows, 0)


def messages(fields, lat_out, lon_out, extra_lat=(), extra_lon=()):
    up = [partial_lat(fields, M_POISSON), partial_lat(fields, M_GRAVITY)]
    height = max(out.shape[0] for out in lat_out)
    post("lat", lat_out, stack(up + list(extra_lat), height), stack([fields[0]], height))
    up = [partial_lon(fields[i], M_POISSON) for i in range(4)]
    up += [partial_lon(fields[i], M_GRAVITY) for i in range(4)]
    down = [fields[i][0:1] for i in range(4)]
    height = max(out.shape[0] for out in lon_out)
    post("lon", lon_out, stack(up + list(extra_lon), height), stack(down, height))


def has_next():
    return jnp.where(lax.axis_index("lat") < LAT - 1, 1.0, 0.0).astype(F32)


def has_before():
    return jnp.where(lax.axis_index("lat") > 0, 1.0, 0.0).astype(F32)


def start_kernel(
    disp_h, vel_h, acc_h, phi_h, mat_h, flag_h, dens_h,
    disp_out, phi_out, info_out, down_lat, lon0, lon1,
    disp, vel, acc, mat, flag, dens, sems,
):
    moves = [
        pltpu.make_async_copy(src, dst, sems.at[n])
        for n, (src, dst) in enumerate(
            [
                (mat_h, mat), (flag_h, flag), (dens_h, dens), (phi_h, phi_out),
                (disp_h, disp), (vel_h, vel), (acc_h, acc),
            ]
        )
    ]
    for move in moves:
        move.start()
    for move in moves[:3]:
        move.wait()
    rho = jnp.zeros((1, 128), F32)
    for m in range(8):
        rho = jnp.where(mat[0] == m, dens[m], rho)
    shell = 1.0 + flag[0].astype(F32)
    info = jnp.concatenate([rho, shell, jnp.zeros((1, 256), F32)], 1)
    info_out[...] = jnp.concatenate([rho, shell, jnp.zeros((6, 128), F32)], 0)
    moves[3].wait()
    potential = [phi_out[i] for i in range(4)]
    for move in moves[4:]:
        move.wait()
    u = []
    for comp in range(3):
        planes = []
        for i in range(4):
            value = (
                disp[comp, i]
                + TIME_STEP * vel[comp, i]
                + 0.5 * TIME_STEP * TIME_STEP * acc[comp, i]
            )
            disp_out[comp, i] = value
            planes.append(value)
        u.append(planes)
    up = [partial_lon(u[1][i], M_SOURCE) for i in range(4)]
    up += [partial_lon(potential[i], M_POISSON) for i in range(4)]
    up += [partial_lon(potential[i], M_GRAVITY) for i in range(4)]
    down = [u[comp][i][0:1] for comp in range(3) for i in range(4)]
    down += [potential[i][0:1] for i in range(4)]
    post("lon", (lon0, lon1), stack(up + [info], 16), stack(down, 16))
    for comp in range(3):
        down_lat[4 * comp : 4 * comp + 4, :] = u[comp][0]
    down_lat[12:16, :] = potential[0]

def pack_kernel(lon_second, lon_first, disp, phi, own_info, _, up_lat, corner):
    below, above = arrived("lon", lon_first, lon_second)
    potential = [phi[i] for i in range(4)]
    info = jnp.concatenate(
        [own_info[0:1, :], own_info[1:2, :], jnp.zeros((1, 256), F32)], 1
    )
    up = [
        partial_lat([disp[0, i] for i in range(4)], M_SOURCE),
        partial_lat(potential, M_POISSON),
        partial_lat(potential, M_GRAVITY),
        info,
        below[12:13],
    ]
    up_lat[...] = stack(up, 16)
    corner[...] = stack([above[4 * comp : 4 * comp + 1] for comp in range(3)], 8)


def lat_rows(factor):
    cols, first = column(W[:4]), column([W[0], 0.0, 0.0, 0.0])
    own = cols * row_of(factor, 0) + first * row_of(factor, 2)
    back = cols * row_of(factor, 1) + first * row_of(factor, 3)
    return own, back


def lon_cols(factor):
    own = (factor[0:1] + factor[1:2], factor[0:1])
    back = (factor[2:3] + factor[3:4], factor[2:3])
    return own, back


def radial_tools():
    lane = lanes((4, 512))
    node = lane & 3
    joint = jnp.logical_and(node == 0, lane >= 4)
    weight = by_index(node, W[:4])

    def earlier(factor):
        return jnp.where(joint, pltpu.roll(factor, 4, 1), 0.0)

    def weighted(factor):
        return weight * factor + W[4] * earlier(factor)

    return node, weight, earlier, weighted


def density_kernel(coef, disp, _, rho_coef, disp_new, flag):
    _, _, earlier, weighted = radial_tools()
    rho, inverse = coef[28:32, :], coef[32:36, :]
    r_points = 0.25 * weighted(rho)
    r_own, r_back = lat_rows(r_points)
    r_col, r_col_back = lon_cols(r_points)
    scaled = 0.25 * rho * inverse
    g_own, g_back = lat_rows(scaled)
    h_own, h_back = lat_rows(earlier(scaled))
    rho_coef[0:4, :] = r_own
    rho_coef[4:8, :] = r_back
    rho_coef[8:12, :] = g_own + g_back
    rho_coef[12:16, :] = g_own
    rho_coef[16:20, :] = h_own + h_back
    rho_coef[20:24, :] = h_own
    rho_coef[24:25, :] = r_col[0]
    rho_coef[25:26, :] = r_col[1]
    rho_coef[26:27, :] = r_col_back[0]
    rho_coef[27:28, :] = r_col_back[1]
    flag[...] = jnp.zeros((8, 128), F32)
    disp_new[...] = disp[...]


def residual_kernel(
    disp_new, phi, own_info, lon_second, lat_below, lat_above, lon_first, _,
    coef, precond_out, w0_out, lat0, lat1, lon0, lon1,
):
    following, before = has_next(), has_before()
    lon_below, lon_above = arrived("lon", lon_first, lon_second)
    rho, shell = (
        jnp.concatenate(
            [
                own_info[n : n + 1, :],
                before * lat_below[12:13, 128 * n : 128 * n + 128],
                lon_below[12:13, 128 * n : 128 * n + 128],
                before * lat_below[13:14, 128 * n : 128 * n + 128],
            ],
            0,
        )
        for n in range(2)
    )
    spread = (
        lax.broadcasted_iota(jnp.int32, (128, 512), 1) // 4
        == lax.broadcasted_iota(jnp.int32, (128, 512), 0)
    )
    spread = jnp.where(spread, 1.0, 0.0).astype(BF16)
    high, mid, low = split3(rho)
    parts = jnp.concatenate(
        [high.astype(F32), mid.astype(F32), low.astype(F32), shell], 0
    ).astype(BF16)
    parts = jnp.dot(parts, spread, preferred_element_type=F32)
    rho = parts[0:4] + parts[4:8] + parts[8:12]
    shell = parts[12:16]
    flagged = shell > 1.5
    valid = shell > 0.5
    stretch = jnp.where(valid, jnp.where(flagged, 3.0, 1.0), 0.0)
    inverse = jnp.where(valid, jnp.where(flagged, 1.0 / 3.0, 1.0), 0.0)
    rho_in = jnp.where(flagged, 0.0, rho)
    node, weight, earlier, weighted = radial_tools()
    s_points = 0.5 * weighted(stretch)
    s_own, s_back = lat_rows(s_points)
    s_col, s_col_back = lon_cols(s_points)
    i_own, i_back = lat_rows(0.5 * inverse)
    j_own, j_back = lat_rows(0.5 * earlier(inverse))
    i_both, j_both = (i_own + i_back, i_own), (j_own + j_back, j_own)
    coef[0:4, :] = s_own
    coef[4:8, :] = s_back
    coef[8:12, :] = i_both[0]
    coef[12:16, :] = i_both[1]
    coef[16:20, :] = j_both[0]
    coef[20:24, :] = j_both[1]
    coef[24:25, :] = s_col[0]
    coef[25:26, :] = s_col[1]
    coef[26:27, :] = s_col_back[0]
    coef[27:28, :] = s_col_back[1]
    coef[28:32, :] = rho
    coef[32:36, :] = inverse
    q_points = 0.25 * weighted(rho_in)
    q_own, q_back = lat_rows(q_points)
    q_col, q_col_back = lon_cols(q_points)
    t_own, t_back = lat_rows(0.25 * rho_in)
    v_own, v_back = lat_rows(0.25 * earlier(rho_in))

    u = [[disp_new[comp, i] for i in range(4)] for comp in range(3)]
    potential = [phi[i] for i in range(4)]
    source_x = lat_part(
        u[0], following * lat_above[0:4, :], lat_below[0:4, :], M_SOURCE, q_own, q_back
    )
    source_y = lon_part(
        u[1], lon_above[4:8, :], lon_below[0:4, :], M_SOURCE, q_col, q_col_back
    )
    source_z = radial_part(u[2], M_SOURCE, (t_own + t_back, t_own), (v_own + v_back, v_own))
    image_x = lat_part(
        potential, following * lat_above[12:16, :], lat_below[4:8, :], M_POISSON, s_own, s_back
    )
    image_y = lon_part(
        potential, lon_above[12:16, :], lon_below[4:8, :], M_POISSON, s_col, s_col_back
    )
    image_z = radial_part(potential, M_POISSON, i_both, j_both)
    diag = [M_POISSON[a][a] for a in range(5)]
    diag_node = by_index(node, diag[:4])
    diag_col = column(diag[:4])
    first = column([1.0, 0.0, 0.0, 0.0])
    w0 = []
    for i in range(4):
        kind = min(i, 1)
        precond = diag[i] * s_own
        if i == 0:
            precond = precond + diag[4] * s_back
        precond = precond + W[i] * (
            diag_col * s_col[kind]
            + first * (diag[4] * s_col_back[kind])
            + i_both[kind] * diag_node
            + diag[4] * j_both[kind]
        )
        precond_out[i] = precond
        source = -(source_x[i] + source_y[i] + source_z[i])
        image = image_x[i] + image_y[i] + image_z[i]
        value = (source - image) / precond
        w0_out[i] = value
        w0.append(value)
    messages(w0, (lat0, lat1), (lon0, lon1))


def poisson(fields, coef, lon_second, lat_first, lat_second, lon_first):
    following = has_next()
    lat_below, lat_above = arrived("lat", lat_first, lat_second)
    lon_below, lon_above = arrived("lon", lon_first, lon_second)
    s_col = (coef[24:25, :], coef[25:26, :])
    s_col_back = (coef[26:27, :], coef[27:28, :])
    x = lat_part(
        fields, following * lat_above[0:4, :], lat_below[0:4, :], M_POISSON, coef[0:4, :], coef[4:8, :]
    )
    y = lon_part(fields, lon_above[0:4, :], lon_below[0:4, :], M_POISSON, s_col, s_col_back)
    z = radial_part(
        fields, M_POISSON, (coef[8:12, :], coef[12:16, :]), (coef[16:20, :], coef[20:24, :])
    )
    return [x[i] + y[i] + z[i] for i in range(4)]


def step(field, coef, precond, halo, out):
    fields = [field[i] for i in range(4)]
    image = poisson(fields, coef, *halo)
    result = []
    for i in range(4):
        value = image[i] / precond[i] - fields[i]
        out[i] = value
        result.append(value)
    return result


def second_kernel(
    field, coef, precond, lon_second, lat_first, lat_second, lon_first, lon_force,
    out, lat0, lat1, lon0, lon1,
):
    result = step(field, coef, precond, (lon_second, lat_first, lat_second, lon_first), out)
    messages(result, (lat0, lat1), (lon0, lon1), (), (lon_force[...],))


def third_kernel(
    field, coef, precond, lon_second, lat_first, lat_second, lon_first, lat_force, _,
    out, lat0, lat1, lon0, lon1,
):
    result = step(field, coef, precond, (lon_second, lat_first, lat_second, lon_first), out)
    below, _ = arrived("lon", lon_first, lon_second)
    first = column([1.0, 0.0, 0.0, 0.0])
    edges = []
    for comp in range(3):
        corner = 12 + 5 * comp
        edges.append(
            lat_force[4 * comp : 4 * comp + 4, :] + first * below[corner : corner + 1]
        )
    messages(result, (lat0, lat1), (lon0, lon1), edges)


def moment_kernel(
    w0, w1, w2, coef, precond, lon_second, lat_first, lat_second, lon_first, _, out
):
    fields = [w2[i] for i in range(4)]
    image = poisson(fields, coef, lon_second, lat_first, lat_second, lon_first)
    sums = [None] * 6
    for i in range(4):
        m = precond[i]
        a, b, c = w0[i], w1[i], w2[i]
        ma, mb, mc = m * a, m * b, m * c
        terms = [a * ma, b * ma, b * mb, c * mb, c * mc, c * (image[i] - mc)]
        for k in range(6):
            sums[k] = terms[k] if sums[k] is None else sums[k] + terms[k]
    lane = lanes((1, 128))
    line = jnp.zeros((1, 128), F32)
    for k in range(6):
        total = jnp.sum(jnp.sum(sums[k], axis=0, keepdims=True), axis=1, keepdims=True)
        line = jnp.where(lane == k, total, line)
    out[...] = jnp.broadcast_to(line, out.shape)


def cg_coefficients(mu):
    zero = jnp.zeros_like(mu[0])

    def inner(a):
        total = zero
        for i in range(len(a)):
            for j in range(len(a)):
                total = total + a[i] * a[j] * mu[i + j]
        return total

    def energy(a):
        total = zero
        for i in range(len(a)):
            for j in range(len(a)):
                total = total + a[i] * a[j] * (mu[i + j + 1] + mu[i + j])
        return total

    def ratio(a, b):
        return jnp.where(b == 0.0, 0.0, a / jnp.where(b == 0.0, 1.0, b))

    y = [zero, zero, zero]
    z = [zero + 1.0]
    search = [zero + 1.0]
    rz = mu[0]
    for step in range(3):
        length = ratio(rz, energy(search))
        for i in range(len(search)):
            y[i] = y[i] + length * search[i]
        if step < 2:
            grown = [zero] * (len(search) + 1)
            for i in range(len(search)):
                grown[i] = grown[i] + search[i]
                grown[i + 1] = grown[i + 1] + search[i]
            z = z + [zero]
            z = [z[i] - length * grown[i] for i in range(len(z))]
            rz_next = inner(z)
            beta = ratio(rz_next, rz)
            padded = search + [zero]
            search = [z[i] + beta * padded[i] for i in range(len(z))]
            rz = rz_next
    return y


def final_kernel(
    moments, phi, w0, w1, w2, rho_coef, own_force,
    a0, a1, a2, a3, b0, b1, b2, b3, c0, c1, c2, c3, d0, d1, d2, d3,
    vel, acc, phi_new, acc_new, vel_new,
):
    total = jnp.sum(moments[...], axis=0, keepdims=True)
    lane = lanes((1, 128))
    mu = [
        jnp.broadcast_to(
            jnp.sum(jnp.where(lane == k, total, 0.0), axis=1, keepdims=True), (1, 128)
        )
        for k in range(6)
    ]
    y = cg_coefficients(mu)
    y = [jnp.concatenate([v] * 4, 1) for v in y]

    def combined(first, one, two, three):
        return first + y[0] * one + y[1] * two + y[2] * three

    potential = []
    for i in range(4):
        value = combined(phi[i], w0[i], w1[i], w2[i])
        phi_new[i] = value
        potential.append(value)
    following, before = has_next(), has_before()
    ma, na = a1[...], a2[...]
    mb, nb = arrived("lat", b1, b2)
    mc, nc = arrived("lat", c1, c2)
    md, nd = arrived("lat", d1, d2)
    fa, ga = arrived("lon", a3, a0)
    fb, gb = arrived("lon", b3, b0)
    fc, gc = arrived("lon", c3, c0)
    fd, gd = arrived("lon", d3, d0)
    lat_below = combined(ma[8:12, :], mb[4:8, :], mc[4:8, :], md[4:8, :])
    lat_above = following * combined(na[12:16, :], nb[0:4, :], nc[0:4, :], nd[0:4, :])
    lon_below = combined(fa[8:12, :], fb[4:8, :], fc[4:8, :], fd[4:8, :])
    lon_above = combined(ga[12:16, :], gb[0:4, :], gc[0:4, :], gd[0:4, :])
    r_own, r_back = rho_coef[0:4, :], rho_coef[4:8, :]
    r_col = (rho_coef[24:25, :], rho_coef[25:26, :])
    r_col_back = (rho_coef[26:27, :], rho_coef[27:28, :])
    x = lat_part(potential, lat_above, lat_below, M_GRAVITY, r_own, r_back)
    y_part = lon_part(potential, lon_above, lon_below, M_GRAVITY, r_col, r_col_back)
    z = radial_part(
        potential,
        M_GRAVITY,
        (rho_coef[8:12, :], rho_coef[12:16, :]),
        (rho_coef[16:20, :], rho_coef[20:24, :]),
    )
    cols = column(W[:4])
    first = column([1.0, 0.0, 0.0, 0.0])
    gravity = (x, y_part, z)
    for i in range(4):
        mass = r_own + r_back if i == 0 else r_own
        mass = 0.5 * W[i] * mass
        for comp in range(3):
            force = own_force[comp, i]
            force = force + first * fc[8 + 5 * comp + i : 9 + 5 * comp + i, :]
            if i == 0:
                edge = md[8 + 4 * comp : 12 + 4 * comp, :]
                force = force + before * edge
            value = (-gravity[comp][i] - force) / mass
            acc_new[comp, i] = value
            vel_new[comp, i] = vel[comp, i] + 0.5 * TIME_STEP * (acc[comp, i] + value)


def split3(value):
    high = value.astype(BF16)
    rest = value - high.astype(F32)
    mid = rest.astype(BF16)
    low = (rest - mid.astype(F32)).astype(BF16)
    return high, mid, low


def prepare_kernel(
    disp, mat_h, moduli_h, decay_h, strength_h, stiff, rates, perm, elems,
    points, mat, moduli, decay, strength, sems,
):
    moves = [
        pltpu.make_async_copy(src, dst, sems.at[n])
        for n, (src, dst) in enumerate(
            [(mat_h, mat), (moduli_h, moduli), (decay_h, decay), (strength_h, strength)]
        )
    ]
    for move in moves:
        move.start()
    for c in range(4):
        hit = lax.broadcasted_iota(jnp.int32, (128, 512), 1) == (
            4 * lax.broadcasted_iota(jnp.int32, (128, 512), 0) + c
        )
        perm[128 * c : 128 * c + 128, :] = jnp.where(hit, 1.0, 0.0).astype(BF16)
    points[...] = jnp.zeros(points.shape, F32)
    for comp in range(3):
        for a in range(4):
            base = (comp * 4 + a) * 8
            points[base : base + 4, :] = disp[comp, a]
    to_nodes(points[...], perm, elems)
    for move in moves:
        move.wait()
    onehot = [mat[0] == m for m in range(8)]
    for k in range(6):
        for l in range(k, 6):
            value = jnp.zeros((1, 128), F32)
            for m in range(8):
                value = jnp.where(onehot[m], moduli[k, m, l], value)
            stiff[6 * k + l : 6 * k + l + 1, :] = value
    for l in range(3):
        rates[l : l + 1, :] = jnp.full((1, 128), decay[l], F32)
        rates[3 + l : 4 + l, :] = jnp.full((1, 128), (1.0 - decay[l]) * strength[l], F32)


def unpack_kernel(memory, rates, _, decayed, flag, old):
    for d in range(5):
        for a in range(5):
            for b in range(5):
                for c in range(5):
                    row = (b * 5 + c) * 4
                    old[row : row + 3, :] = memory[d, a, b, c].astype(F32)
            for c in range(5):
                for l in range(3):
                    was = old[pl.ds(4 * c + l, 8, stride=20), :]
                    decayed[((d * 5 + a) * 5 + c) * 3 + l] = rates[l : l + 1, :] * was
    flag[...] = jnp.zeros((8, 128), F32)


def repack_kernel(dense, memory_new, flag, new):
    for d in range(5):
        for a in range(5):
            for c in range(5):
                for l in range(3):
                    new[pl.ds(4 * c + l, 8, stride=20), :] = dense[((d * 5 + a) * 5 + c) * 3 + l]
            for b in range(5):
                for c in range(5):
                    row = (b * 5 + c) * 4
                    memory_new[d, a, b, c] = new[row : row + 3, :].astype(BF16)
    flag[...] = jnp.zeros((8, 128), F32)


def to_nodes(points, perm, elems):
    rows = points.shape[0]
    parts = jnp.concatenate(split3(points), 0)
    taken = lax.dot_general(
        parts, perm[...], (((1,), (1,)), ((), ())), preferred_element_type=F32
    )
    taken = taken[0:rows] + taken[rows : 2 * rows] + taken[2 * rows : 3 * rows]
    for c in range(4):
        elems[c] = taken[:, 128 * c : 128 * c + 128]
    lane = lanes((rows, 128))
    elems[4] = jnp.where(lane < 127, pltpu.roll(taken[:, 0:128], 127, 1), 0.0)


def elastic_kernel(
    lon_second, corner, lat_above, lon_first, stiff, rates, perm, own, decayed,
    dense, force, lat_force, lon_force,
    points, edge, elems, devs, flux,
):
    following = has_next()
    _, lon_above = arrived("lon", lon_first, lon_second)
    points[...] = jnp.zeros(points.shape, F32)
    for comp in range(3):
        points[8 * comp : 8 * comp + 4, :] = following * lat_above[4 * comp : 4 * comp + 4, :]
        points[8 * comp + 4 : 8 * comp + 5, :] = following * corner[comp : comp + 1]
    points[24:36, :] = lon_above[0:12]
    to_nodes(points[...], perm, edge)
    fifth = sublanes((8, 128)) == 4
    for c in range(5):
        for comp in range(3):
            for a in range(4):
                base, row = (comp * 5 + a) * 8, 24 + 4 * comp + a
                kept = own[c, (comp * 4 + a) * 8 : (comp * 4 + a) * 8 + 8, :]
                elems[c, base : base + 8, :] = jnp.where(
                    fifth, row_of(edge[c, 24:40, :], row - 24, 8), kept
                )
            base = (comp * 5 + 4) * 8
            elems[c, base : base + 8, :] = edge[c, 8 * comp : 8 * comp + 8, :]
    lane = lanes((128, 128))
    slopes = [
        by_index(sublanes((8, 128)), [2.0 * DERIV[b][p] for b in range(5)] + [0.0])
        for p in range(5)
    ]
    turned = [
        by_index(sublanes((8, 128)), [2.0 * DERIV[p][b] for b in range(5)] + [0.0])
        for p in range(5)
    ]
    weight_col = by_index(sublanes((8, 128)), W + [0.0])

    def slab(comp, a, c):
        base = (comp * 5 + a) * 8
        return elems[c, base : base + 8, :]

    def along_lon(cols, value):
        total = None
        for p in range(5):
            term = cols[p] * row_of(value, p, 8)
            total = term if total is None else total + term
        return total

    for a in range(5):
        elastic_of = []
        for c in range(5):
            dx, dy, dz = [], [], []
            for comp in range(3):
                dx.append(mix([2.0 * DERIV[a][p] for p in range(5)], [slab(comp, p, c) for p in range(5)]))
                dy.append(along_lon(slopes, slab(comp, a, c)))
                dz.append(mix([2.0 * DERIV[c][p] for p in range(5)], [slab(comp, a, p) for p in range(5)]))
            strain = [dx[0], dy[1], dz[2], dy[0] + dx[1], dz[0] + dx[2], dz[1] + dy[2]]
            elastic = []
            for k in range(6):
                total = None
                for l in range(6):
                    pos = 6 * min(k, l) + max(k, l)
                    term = stiff[pos : pos + 1, :] * strain[l]
                    total = term if total is None else total + term
                elastic.append(total)
            pressure = (elastic[0] + elastic[1] + elastic[2]) * (1.0 / 3.0)
            dev = [elastic[0] - pressure, elastic[1] - pressure, elastic[3], elastic[4], elastic[5]]
            for d in range(5):
                devs[d * 5 + c] = dev[d]
            elastic_of.append(elastic)
        relaxed = []
        for d in range(5):
            sums = []
            for c in range(5):
                dev = devs[d * 5 + c]
                total = None
                for l in range(3):
                    pos = ((d * 5 + a) * 5 + c) * 3 + l
                    now = decayed[pos] + rates[3 + l : 4 + l, :] * dev
                    now = now.astype(BF16).astype(F32)
                    dense[pos] = now
                    total = now if total is None else total + now
                sums.append(total)
            relaxed.append(sums)
        for c in range(5):
            e = elastic_of[c]
            r = [relaxed[d][c] for d in range(5)]
            weight = weight_col * (W[a] * W[c] / 8.0)
            stress = [e[0] - r[0], e[1] - r[1], e[2] + r[0] + r[1], e[3] - r[2], e[4] - r[3], e[5] - r[4]]
            for k in range(6):
                flux[k, a * 5 + c] = jnp.where(weight_col > 0.0, weight * stress[k], 0.0)
    flux_of = [[0, 3, 4], [3, 1, 5], [4, 5, 2]]
    for c in range(5):
        elems[c, 120:128, :] = jnp.zeros((8, 128), F32)
        for comp in range(3):
            for a in range(5):
                value = mix(
                    [2.0 * DERIV[p][a] for p in range(5)],
                    [flux[flux_of[comp][0], p * 5 + c] for p in range(5)],
                )
                value = value + along_lon(turned, flux[flux_of[comp][1], a * 5 + c])
                value = value + mix(
                    [2.0 * DERIV[p][c] for p in range(5)],
                    [flux[flux_of[comp][2], a * 5 + p] for p in range(5)],
                )
                base = (comp * 5 + a) * 8
                elems[c, base : base + 8, :] = value
    carried = jnp.where(lane > 0, pltpu.roll(elems[4], 1, 1), 0.0)
    merged = jnp.concatenate([elems[0] + carried, elems[1], elems[2], elems[3]], 1)
    parts = jnp.concatenate(split3(merged), 0)
    given = jnp.dot(parts, perm[...], preferred_element_type=F32)
    given = given[0:128] + given[128:256] + given[256:384]
    lat_force[12:16, :] = jnp.zeros((4, 512), F32)
    lon_force[15:16, :] = jnp.zeros((1, 512), F32)
    for comp in range(3):
        for a in range(5):
            base = (comp * 5 + a) * 8
            if a < 4:
                force[comp, a] = given[base : base + 4]
                lon_force[5 * comp + a : 5 * comp + a + 1, :] = given[base + 4 : base + 5]
            else:
                lat_force[4 * comp : 4 * comp + 4, :] = given[base : base + 4]
                lon_force[5 * comp + 4 : 5 * comp + 5, :] = given[base + 4 : base + 5]


def call(kernel, name, outs, ins, args, scratch=(), flops=1000000, moved=500000, vmem=24):
    return pl.pallas_call(
        kernel,
        name=name,
        out_shape=[jax.ShapeDtypeStruct(s, d) for s, d in outs],
        in_specs=ins,
        out_specs=[VMEM] * len(outs),
        scratch_shapes=list(scratch),
        compiler_params=pltpu.CompilerParams(vmem_limit_bytes=vmem * 1024 * 1024),
        cost_estimate=pl.CostEstimate(flops=flops, bytes_accessed=moved, transcendentals=0),
    )(*args)


def swap(array, axis, size, parity):
    pairs = []
    for i in range(parity, size, 2):
        j = (i + 1) % size
        pairs += [(i, j), (j, i)]
    return lax.ppermute(array, axis, pairs)


def ring(array, axis, size, by):
    return lax.ppermute(array, axis, [(i, (i + by) % size) for i in range(size)])


def swap_lat(first, second):
    return swap(first, "lat", LAT, 0), swap(second, "lat", LAT, 1)


def swap_lon(first, second):
    other = swap(second, "lon", LON, 1)
    return swap(first, "lon", LON, 0), other


def per_device(
    displacement, velocity, acceleration, potential, memory_vars, materials, shell_flags,
    moduli, densities, decay, strength,
):
    field = ((4, 4, 512), F32)
    vector = ((3, 4, 4, 512), F32)
    r8, r16, r24, r32, r40 = (((n, 512), F32) for n in (8, 16, 24, 32, 40))
    info = ((8, 128), F32)
    kept = pltpu.with_memory_space_constraint
    disp, phi, own_info, down_lat, *sent = call(
        start_kernel, "start", [vector, field, info, r16, r16, r16], [HBM] * 7,
        [
            kept(array, pltpu.HBM)
            for array in (
                displacement, velocity, acceleration, potential, materials, shell_flags, densities
            )
        ],
        [
            pltpu.VMEM((3, 4, 4, 512), F32),
            pltpu.VMEM((3, 4, 4, 512), F32),
            pltpu.VMEM((3, 4, 4, 512), F32),
            pltpu.VMEM((1, 1, 128), jnp.int32),
            pltpu.VMEM((1, 1, 128), jnp.int32),
            pltpu.SMEM((8,), F32),
            pltpu.SemaphoreType.DMA((7,)),
        ],
    )
    lon_a = swap_lon(*sent)
    above_a = ring(down_lat, "lat", LAT, -1)
    tables = call(
        prepare_kernel, "prepare",
        [((40, 128), F32), info, ((512, 512), BF16), ((5, 96, 128), F32)],
        [VMEM] + [HBM] * 4,
        [disp]
        + [
            kept(array, pltpu.HBM)
            for array in (materials, moduli.transpose(1, 0, 2), decay, strength)
        ],
        [
            pltpu.VMEM((96, 512), F32),
            pltpu.VMEM((1, 1, 128), jnp.int32),
            pltpu.SMEM((6, 8, 6), F32),
            pltpu.SMEM((3,), F32),
            pltpu.SMEM((3,), F32),
            pltpu.SemaphoreType.DMA((4,)),
        ],
    )
    lat_a = call(
        pack_kernel, "pack", [r16, r8], [VMEM] * 6,
        (lon_a[1], lon_a[0], disp, phi, own_info, tables[1]),
    )
    halo_a = (lon_a[1], ring(lat_a[0], "lat", LAT, 1), above_a, lon_a[0])
    corner = ring(lat_a[1], "lat", LAT, -1)
    memory = memory_vars.reshape(3, 5, 5, 5, 5, 128).transpose(1, 2, 3, 4, 0, 5)
    every = ((375, 8, 128), F32)
    decayed, unpacked = call(
        unpack_kernel, "unpack", [every, info], [VMEM] * 3, (memory, tables[1], lat_a[0]),
        [pltpu.VMEM((160, 128), F32)],
    )
    coef, precond, w0, *sent = call(
        residual_kernel, "residual", [r40, field, field, r8, r8, r8, r8], [VMEM] * 8,
        (disp, phi, own_info, *halo_a, unpacked),
    )
    lon_b = swap_lon(*sent[2:])
    halo_b = (lon_b[1], *swap_lat(*sent[:2]), lon_b[0])
    dense, force, lat_force, lon_force = call(
        elastic_kernel, "elastic", [every, vector, r16, r16], [VMEM] * 9,
        (lon_a[1], corner, above_a, lon_a[0], *tables, decayed),
        [
            pltpu.VMEM((48, 512), F32),
            pltpu.VMEM((5, 48, 128), F32),
            pltpu.VMEM((5, 128, 128), F32),
            pltpu.VMEM((25, 8, 128), F32),
            pltpu.VMEM((6, 25, 8, 128), F32),
        ],
        flops=20000000, moved=2000000,
    )
    w1, *sent = call(
        second_kernel, "second", [field, r8, r8, r24, r24], [VMEM] * 8,
        (w0, coef, precond, *halo_b, lon_force),
    )
    lon_c = swap_lon(*sent[2:])
    halo_c = (lon_c[1], *swap_lat(*sent[:2]), lon_c[0])
    memory_new, packed = call(
        repack_kernel, "repack", [((5, 5, 5, 5, 3, 128), BF16), info], [VMEM], (dense,),
        [pltpu.VMEM((160, 128), F32)],
    )
    w2, *sent = call(
        third_kernel, "third", [field, r24, r24, r8, r32], [VMEM] * 9,
        (w1, coef, precond, *halo_c, lat_force, packed),
    )
    lon_d = swap_lon(*sent[2:])
    halo_d = (lon_d[1], *swap_lat(*sent[:2]), lon_d[0])
    rho_coef, disp_new, dense_done = call(
        density_kernel, "density", [r32, vector, info], [VMEM] * 3, (coef, disp, sent[0])
    )
    (line,) = call(
        moment_kernel, "moments", [((LAT * LON, 128), F32)], [VMEM] * 10,
        (w0, w1, w2, coef, precond, *halo_d, dense_done),
    )
    moments = lax.all_to_all(line, AXES, 0, 0, tiled=True)
    phi_new, acc_new, vel_new = call(
        final_kernel, "final", [field, vector, vector], [VMEM] * 25,
        (
            moments, phi, w0, w1, w2, rho_coef, force, *halo_a, *halo_b, *halo_c, *halo_d,
            velocity, acceleration,
        ),
    )
    memory_new = memory_new.transpose(4, 0, 1, 2, 3, 5).reshape(memory_vars.shape)
    return (disp_new, vel_new, acc_new, phi_new, memory_new)


def solution(mesh):
    vector = P(None, "lat", "lon", None)
    scalar = P("lat", "lon", None)
    memory = P(None, None, None, "lat", None, "lon", None, None)
    return jax.shard_map(
        per_device,
        mesh=mesh,
        in_specs=(vector, vector, vector, scalar, memory, scalar, scalar, P(), P(), P(), P()),
        out_specs=(vector, vector, vector, scalar, memory),
        check_vma=False,
    )
```

```python
import jax
import jax.numpy as jnp
import numpy as np
from jax import lax
from jax.experimental import pallas as pl
from jax.experimental.pallas import tpu as pltpu
from jax.sharding import PartitionSpec as P

TIME_STEP = 0.1
F32 = jnp.float32
BF16 = jnp.bfloat16
LAT, LON = 8, 32
AXES = ("lat", "lon")
VMEM = pl.BlockSpec(memory_space=pltpu.VMEM)
HBM = pl.BlockSpec(memory_space=pltpu.HBM)


def gll():
    points = np.array([-1.0, -np.sqrt(3.0 / 7.0), 0.0, np.sqrt(3.0 / 7.0), 1.0])
    weights = np.array([0.1, 49.0 / 90.0, 32.0 / 45.0, 49.0 / 90.0, 0.1])
    differ = points[:, None] - points[None, :] + np.eye(5)
    factors = np.prod(differ, axis=1)
    deriv = factors[:, None] / factors[None, :] / differ * (1.0 - np.eye(5))
    deriv = deriv - np.eye(5) * np.sum(deriv, axis=1)[:, None]
    return deriv, weights


DERIV, WEIGHTS = gll()
W = [float(v) for v in WEIGHTS]
M_POISSON = (DERIV.T @ np.diag(WEIGHTS) @ DERIV).tolist()
M_SOURCE = (np.diag(WEIGHTS) @ DERIV).T.tolist()
M_GRAVITY = (np.diag(WEIGHTS) @ DERIV).tolist()


def lanes(shape):
    return lax.broadcasted_iota(jnp.int32, shape, len(shape) - 1)


def sublanes(shape):
    return lax.broadcasted_iota(jnp.int32, shape, len(shape) - 2)


def by_index(index, values):
    out = jnp.full(index.shape, float(values[-1]), F32)
    for pos in range(len(values) - 2, -1, -1):
        out = jnp.where(index == pos, float(values[pos]), out)
    return out


def column(values, rows=4, width=512):
    return by_index(sublanes((rows, width)), list(values))


def row_of(array, pos, rows=4):
    return jnp.broadcast_to(array[pos : pos + 1], (rows, array.shape[1]))


def radial(field, matrix):
    lane = lanes((4, 512))
    node = lane & 3
    own, before = None, None
    for shift in range(-4, 5):
        moved = field if shift == 0 else pltpu.roll(field, (-shift) % 512, 1)
        if shift > -4:
            factors = [
                matrix[c][c + shift] if 0 <= c + shift <= 4 else 0.0 for c in range(4)
            ]
            table = by_index(node, factors)
            if shift > 0:
                table = jnp.where(lane < 512 - shift, table, 0.0)
            own = table * moved if own is None else own + table * moved
        if shift <= 0:
            term = float(matrix[4][4 + shift]) * moved
            before = term if before is None else before + term
    return own, before


def mix(matrix_row, arrays):
    total = None
    for factor, array in zip(matrix_row, arrays):
        term = float(factor) * array
        total = term if total is None else total + term
    return total


def lat_part(fields, above, below, matrix, own_row, back_row):
    out = []
    for i in range(4):
        value = own_row * mix(matrix[i], fields + [above])
        if i == 0:
            value = value + back_row * (float(matrix[4][4]) * fields[0] + below)
        out.append(value)
    return out


def lon_part(fields, above, below, matrix, own_col, back_col):
    columns = [column([matrix[b][p] for b in range(4)]) for p in range(5)]
    first = column([1.0, 0.0, 0.0, 0.0])
    out = []
    for i in range(4):
        value = columns[4] * row_of(above, i)
        for p in range(4):
            value = value + columns[p] * row_of(fields[i], p)
        edge = float(matrix[4][4]) * fields[i][0:1] + below[i : i + 1]
        kind = min(i, 1)
        value = own_col[kind] * value + first * (back_col[kind] * edge)
        out.append(W[i] * value)
    return out


def radial_part(fields, matrix, own, before):
    out = []
    for i in range(4):
        first, second = radial(fields[i], matrix)
        kind = min(i, 1)
        out.append(W[i] * (own[kind] * first + before[kind] * second))
    return out


def partial_lat(fields, matrix):
    return mix(matrix[4][:4], fields)


def partial_lon(field, matrix):
    weighted = column(matrix[4][:4]) * field
    return jnp.sum(weighted, axis=0, keepdims=True)


def even(axis):
    return lax.rem(lax.axis_index(axis), 2) == 0


def pick(axis, for_even, for_odd):
    return jnp.where(even(axis), for_even, for_odd)


def post(axis, outs, up, down):
    for out, sent in zip(outs, (pick(axis, up, down), pick(axis, down, up))):
        out[...] = sent[: out.shape[0]]


def arrived(axis, first, second):
    height = min(first.shape[0], second.shape[0])
    first, second = first[0:height], second[0:height]
    return pick(axis, second, first), pick(axis, first, second)


def stack(rows, height):
    total = sum(r.shape[0] for r in rows)
    if total < height:
        rows = rows + [jnp.zeros((height - total, 512), F32)]
    return jnp.concatenate(rows, 0)


def messages(fields, lat_out, lon_out, extra_lat=(), extra_lon=()):
    up = [partial_lat(fields, M_POISSON), partial_lat(fields, M_GRAVITY)]
    height = max(out.shape[0] for out in lat_out)
    post("lat", lat_out, stack(up + list(extra_lat), height), stack([fields[0]], height))
    up = [partial_lon(fields[i], M_POISSON) for i in range(4)]
    up += [partial_lon(fields[i], M_GRAVITY) for i in range(4)]
    down = [fields[i][0:1] for i in range(4)]
    height = max(out.shape[0] for out in lon_out)
    post("lon", lon_out, stack(up + list(extra_lon), height), stack(down, height))


def has_next():
    return jnp.where(lax.axis_index("lat") < LAT - 1, 1.0, 0.0).astype(F32)


def has_before():
    return jnp.where(lax.axis_index("lat") > 0, 1.0, 0.0).astype(F32)


def start_kernel(
    disp_h, vel_h, acc_h, phi_h, mat_h, flag_h, dens_h,
    disp_out, phi_out, info_out, down_lat, lon0, lon1,
    disp, vel, acc, mat, flag, dens, sems,
):
    moves = [
        pltpu.make_async_copy(src, dst, sems.at[n])
        for n, (src, dst) in enumerate(
            [
                (mat_h, mat), (flag_h, flag), (dens_h, dens), (phi_h, phi_out),
                (disp_h, disp), (vel_h, vel), (acc_h, acc),
            ]
        )
    ]
    for move in moves:
        move.start()
    for move in moves[:3]:
        move.wait()
    rho = jnp.zeros((1, 128), F32)
    for m in range(8):
        rho = jnp.where(mat[0] == m, dens[m], rho)
    shell = 1.0 + flag[0].astype(F32)
    info = jnp.concatenate([rho, shell, jnp.zeros((1, 256), F32)], 1)
    info_out[...] = jnp.concatenate([rho, shell, jnp.zeros((6, 128), F32)], 0)
    moves[3].wait()
    potential = [phi_out[i] for i in range(4)]
    for move in moves[4:]:
        move.wait()
    u = []
    for comp in range(3):
        planes = []
        for i in range(4):
            value = (
                disp[comp, i]
                + TIME_STEP * vel[comp, i]
                + 0.5 * TIME_STEP * TIME_STEP * acc[comp, i]
            )
            disp_out[comp, i] = value
            planes.append(value)
        u.append(planes)
    up = [partial_lon(u[1][i], M_SOURCE) for i in range(4)]
    up += [partial_lon(potential[i], M_POISSON) for i in range(4)]
    up += [partial_lon(potential[i], M_GRAVITY) for i in range(4)]
    down = [u[comp][i][0:1] for comp in range(3) for i in range(4)]
    down += [potential[i][0:1] for i in range(4)]
    post("lon", (lon0, lon1), stack(up + [info], 16), stack(down, 16))
    for comp in range(3):
        down_lat[4 * comp : 4 * comp + 4, :] = u[comp][0]
    down_lat[12:16, :] = potential[0]

def pack_kernel(lon_second, lon_first, disp, phi, own_info, _, up_lat, corner):
    below, above = arrived("lon", lon_first, lon_second)
    potential = [phi[i] for i in range(4)]
    info = jnp.concatenate(
        [own_info[0:1, :], own_info[1:2, :], jnp.zeros((1, 256), F32)], 1
    )
    up = [
        partial_lat([disp[0, i] for i in range(4)], M_SOURCE),
        partial_lat(potential, M_POISSON),
        partial_lat(potential, M_GRAVITY),
        info,
        below[12:13],
    ]
    up_lat[...] = stack(up, 16)
    corner[...] = stack([above[4 * comp : 4 * comp + 1] for comp in range(3)], 8)


def lat_rows(factor):
    cols, first = column(W[:4]), column([W[0], 0.0, 0.0, 0.0])
    own = cols * row_of(factor, 0) + first * row_of(factor, 2)
    back = cols * row_of(factor, 1) + first * row_of(factor, 3)
    return own, back


def lon_cols(factor):
    own = (factor[0:1] + factor[1:2], factor[0:1])
    back = (factor[2:3] + factor[3:4], factor[2:3])
    return own, back


def radial_tools():
    lane = lanes((4, 512))
    node = lane & 3
    joint = jnp.logical_and(node == 0, lane >= 4)
    weight = by_index(node, W[:4])

    def earlier(factor):
        return jnp.where(joint, pltpu.roll(factor, 4, 1), 0.0)

    def weighted(factor):
        return weight * factor + W[4] * earlier(factor)

    return node, weight, earlier, weighted


def density_kernel(coef, disp, _, rho_coef, disp_new, flag):
    _, _, earlier, weighted = radial_tools()
    rho, inverse = coef[28:32, :], coef[32:36, :]
    r_points = 0.25 * weighted(rho)
    r_own, r_back = lat_rows(r_points)
    r_col, r_col_back = lon_cols(r_points)
    scaled = 0.25 * rho * inverse
    g_own, g_back = lat_rows(scaled)
    h_own, h_back = lat_rows(earlier(scaled))
    rho_coef[0:4, :] = r_own
    rho_coef[4:8, :] = r_back
    rho_coef[8:12, :] = g_own + g_back
    rho_coef[12:16, :] = g_own
    rho_coef[16:20, :] = h_own + h_back
    rho_coef[20:24, :] = h_own
    rho_coef[24:25, :] = r_col[0]
    rho_coef[25:26, :] = r_col[1]
    rho_coef[26:27, :] = r_col_back[0]
    rho_coef[27:28, :] = r_col_back[1]
    flag[...] = jnp.zeros((8, 128), F32)
    disp_new[...] = disp[...]


def residual_kernel(
    disp_new, phi, own_info, lon_second, lat_below, lat_above, lon_first,
    coef, precond_out, w0_out, lat0, lat1, lon0, lon1,
):
    following, before = has_next(), has_before()
    lon_below, lon_above = arrived("lon", lon_first, lon_second)
    rho, shell = (
        jnp.concatenate(
            [
                own_info[n : n + 1, :],
                before * lat_below[12:13, 128 * n : 128 * n + 128],
                lon_below[12:13, 128 * n : 128 * n + 128],
                before * lat_below[13:14, 128 * n : 128 * n + 128],
            ],
            0,
        )
        for n in range(2)
    )
    spread = (
        lax.broadcasted_iota(jnp.int32, (128, 512), 1) // 4
        == lax.broadcasted_iota(jnp.int32, (128, 512), 0)
    )
    spread = jnp.where(spread, 1.0, 0.0).astype(BF16)
    high, mid, low = split3(rho)
    parts = jnp.concatenate(
        [high.astype(F32), mid.astype(F32), low.astype(F32), shell], 0
    ).astype(BF16)
    parts = jnp.dot(parts, spread, preferred_element_type=F32)
    rho = parts[0:4] + parts[4:8] + parts[8:12]
    shell = parts[12:16]
    flagged = shell > 1.5
    valid = shell > 0.5
    stretch = jnp.where(valid, jnp.where(flagged, 3.0, 1.0), 0.0)
    inverse = jnp.where(valid, jnp.where(flagged, 1.0 / 3.0, 1.0), 0.0)
    rho_in = jnp.where(flagged, 0.0, rho)
    node, weight, earlier, weighted = radial_tools()
    s_points = 0.5 * weighted(stretch)
    s_own, s_back = lat_rows(s_points)
    s_col, s_col_back = lon_cols(s_points)
    i_own, i_back = lat_rows(0.5 * inverse)
    j_own, j_back = lat_rows(0.5 * earlier(inverse))
    i_both, j_both = (i_own + i_back, i_own), (j_own + j_back, j_own)
    coef[0:4, :] = s_own
    coef[4:8, :] = s_back
    coef[8:12, :] = i_both[0]
    coef[12:16, :] = i_both[1]
    coef[16:20, :] = j_both[0]
    coef[20:24, :] = j_both[1]
    coef[24:25, :] = s_col[0]
    coef[25:26, :] = s_col[1]
    coef[26:27, :] = s_col_back[0]
    coef[27:28, :] = s_col_back[1]
    coef[28:32, :] = rho
    coef[32:36, :] = inverse
    q_points = 0.25 * weighted(rho_in)
    q_own, q_back = lat_rows(q_points)
    q_col, q_col_back = lon_cols(q_points)
    t_own, t_back = lat_rows(0.25 * rho_in)
    v_own, v_back = lat_rows(0.25 * earlier(rho_in))

    u = [[disp_new[comp, i] for i in range(4)] for comp in range(3)]
    potential = [phi[i] for i in range(4)]
    source_x = lat_part(
        u[0], following * lat_above[0:4, :], lat_below[0:4, :], M_SOURCE, q_own, q_back
    )
    source_y = lon_part(
        u[1], lon_above[4:8, :], lon_below[0:4, :], M_SOURCE, q_col, q_col_back
    )
    source_z = radial_part(u[2], M_SOURCE, (t_own + t_back, t_own), (v_own + v_back, v_own))
    image_x = lat_part(
        potential, following * lat_above[12:16, :], lat_below[4:8, :], M_POISSON, s_own, s_back
    )
    image_y = lon_part(
        potential, lon_above[12:16, :], lon_below[4:8, :], M_POISSON, s_col, s_col_back
    )
    image_z = radial_part(potential, M_POISSON, i_both, j_both)
    diag = [M_POISSON[a][a] for a in range(5)]
    diag_node = by_index(node, diag[:4])
    diag_col = column(diag[:4])
    first = column([1.0, 0.0, 0.0, 0.0])
    w0 = []
    for i in range(4):
        kind = min(i, 1)
        precond = diag[i] * s_own
        if i == 0:
            precond = precond + diag[4] * s_back
        precond = precond + W[i] * (
            diag_col * s_col[kind]
            + first * (diag[4] * s_col_back[kind])
            + i_both[kind] * diag_node
            + diag[4] * j_both[kind]
        )
        precond_out[i] = precond
        source = -(source_x[i] + source_y[i] + source_z[i])
        image = image_x[i] + image_y[i] + image_z[i]
        value = (source - image) / precond
        w0_out[i] = value
        w0.append(value)
    messages(w0, (lat0, lat1), (lon0, lon1))


def poisson(fields, coef, lon_second, lat_first, lat_second, lon_first):
    following = has_next()
    lat_below, lat_above = arrived("lat", lat_first, lat_second)
    lon_below, lon_above = arrived("lon", lon_first, lon_second)
    s_col = (coef[24:25, :], coef[25:26, :])
    s_col_back = (coef[26:27, :], coef[27:28, :])
    x = lat_part(
        fields, following * lat_above[0:4, :], lat_below[0:4, :], M_POISSON, coef[0:4, :], coef[4:8, :]
    )
    y = lon_part(fields, lon_above[0:4, :], lon_below[0:4, :], M_POISSON, s_col, s_col_back)
    z = radial_part(
        fields, M_POISSON, (coef[8:12, :], coef[12:16, :]), (coef[16:20, :], coef[20:24, :])
    )
    return [x[i] + y[i] + z[i] for i in range(4)]


def step(field, coef, precond, halo, out):
    fields = [field[i] for i in range(4)]
    image = poisson(fields, coef, *halo)
    result = []
    for i in range(4):
        value = image[i] / precond[i] - fields[i]
        out[i] = value
        result.append(value)
    return result


def second_kernel(
    field, coef, precond, lon_second, lat_first, lat_second, lon_first, lon_force,
    out, lat0, lat1, lon0, lon1,
):
    result = step(field, coef, precond, (lon_second, lat_first, lat_second, lon_first), out)
    messages(result, (lat0, lat1), (lon0, lon1), (), (lon_force[...],))


def third_kernel(
    field, coef, precond, lon_second, lat_first, lat_second, lon_first, lat_force, _,
    out, lat0, lat1, lon0, lon1,
):
    result = step(field, coef, precond, (lon_second, lat_first, lat_second, lon_first), out)
    below, _ = arrived("lon", lon_first, lon_second)
    first = column([1.0, 0.0, 0.0, 0.0])
    edges = []
    for comp in range(3):
        corner = 12 + 5 * comp
        edges.append(
            lat_force[4 * comp : 4 * comp + 4, :] + first * below[corner : corner + 1]
        )
    messages(result, (lat0, lat1), (lon0, lon1), edges)


def moment_kernel(
    w0, w1, w2, coef, precond, lon_second, lat_first, lat_second, lon_first, _, out
):
    fields = [w2[i] for i in range(4)]
    image = poisson(fields, coef, lon_second, lat_first, lat_second, lon_first)
    sums = [None] * 6
    for i in range(4):
        m = precond[i]
        a, b, c = w0[i], w1[i], w2[i]
        ma, mb, mc = m * a, m * b, m * c
        terms = [a * ma, b * ma, b * mb, c * mb, c * mc, c * (image[i] - mc)]
        for k in range(6):
            sums[k] = terms[k] if sums[k] is None else sums[k] + terms[k]
    lane = lanes((1, 128))
    line = jnp.zeros((1, 128), F32)
    for k in range(6):
        total = jnp.sum(jnp.sum(sums[k], axis=0, keepdims=True), axis=1, keepdims=True)
        line = jnp.where(lane == k, total, line)
    out[...] = jnp.broadcast_to(line, out.shape)


def cg_coefficients(mu):
    zero = jnp.zeros_like(mu[0])

    def inner(a):
        total = zero
        for i in range(len(a)):
            for j in range(len(a)):
                total = total + a[i] * a[j] * mu[i + j]
        return total

    def energy(a):
        total = zero
        for i in range(len(a)):
            for j in range(len(a)):
                total = total + a[i] * a[j] * (mu[i + j + 1] + mu[i + j])
        return total

    def ratio(a, b):
        return jnp.where(b == 0.0, 0.0, a / jnp.where(b == 0.0, 1.0, b))

    y = [zero, zero, zero]
    z = [zero + 1.0]
    search = [zero + 1.0]
    rz = mu[0]
    for step in range(3):
        length = ratio(rz, energy(search))
        for i in range(len(search)):
            y[i] = y[i] + length * search[i]
        if step < 2:
            grown = [zero] * (len(search) + 1)
            for i in range(len(search)):
                grown[i] = grown[i] + search[i]
                grown[i + 1] = grown[i + 1] + search[i]
            z = z + [zero]
            z = [z[i] - length * grown[i] for i in range(len(z))]
            rz_next = inner(z)
            beta = ratio(rz_next, rz)
            padded = search + [zero]
            search = [z[i] + beta * padded[i] for i in range(len(z))]
            rz = rz_next
    return y


def final_kernel(
    moments, phi, w0, w1, w2, rho_coef, own_force,
    a0, a1, a2, a3, b0, b1, b2, b3, c0, c1, c2, c3, d0, d1, d2, d3,
    vel, acc, phi_new, acc_new, vel_new,
):
    total = jnp.sum(moments[...], axis=0, keepdims=True)
    lane = lanes((1, 128))
    mu = [
        jnp.broadcast_to(
            jnp.sum(jnp.where(lane == k, total, 0.0), axis=1, keepdims=True), (1, 128)
        )
        for k in range(6)
    ]
    y = cg_coefficients(mu)
    y = [jnp.concatenate([v] * 4, 1) for v in y]

    def combined(first, one, two, three):
        return first + y[0] * one + y[1] * two + y[2] * three

    potential = []
    for i in range(4):
        value = combined(phi[i], w0[i], w1[i], w2[i])
        phi_new[i] = value
        potential.append(value)
    following, before = has_next(), has_before()
    ma, na = a1[...], a2[...]
    mb, nb = arrived("lat", b1, b2)
    mc, nc = arrived("lat", c1, c2)
    md, nd = arrived("lat", d1, d2)
    fa, ga = arrived("lon", a3, a0)
    fb, gb = arrived("lon", b3, b0)
    fc, gc = arrived("lon", c3, c0)
    fd, gd = arrived("lon", d3, d0)
    lat_below = combined(ma[8:12, :], mb[4:8, :], mc[4:8, :], md[4:8, :])
    lat_above = following * combined(na[12:16, :], nb[0:4, :], nc[0:4, :], nd[0:4, :])
    lon_below = combined(fa[8:12, :], fb[4:8, :], fc[4:8, :], fd[4:8, :])
    lon_above = combined(ga[12:16, :], gb[0:4, :], gc[0:4, :], gd[0:4, :])
    r_own, r_back = rho_coef[0:4, :], rho_coef[4:8, :]
    r_col = (rho_coef[24:25, :], rho_coef[25:26, :])
    r_col_back = (rho_coef[26:27, :], rho_coef[27:28, :])
    x = lat_part(potential, lat_above, lat_below, M_GRAVITY, r_own, r_back)
    y_part = lon_part(potential, lon_above, lon_below, M_GRAVITY, r_col, r_col_back)
    z = radial_part(
        potential,
        M_GRAVITY,
        (rho_coef[8:12, :], rho_coef[12:16, :]),
        (rho_coef[16:20, :], rho_coef[20:24, :]),
    )
    cols = column(W[:4])
    first = column([1.0, 0.0, 0.0, 0.0])
    gravity = (x, y_part, z)
    for i in range(4):
        mass = r_own + r_back if i == 0 else r_own
        mass = 0.5 * W[i] * mass
        for comp in range(3):
            force = own_force[comp, i]
            force = force + first * fc[8 + 5 * comp + i : 9 + 5 * comp + i, :]
            if i == 0:
                edge = md[8 + 4 * comp : 12 + 4 * comp, :]
                force = force + before * edge
            value = (-gravity[comp][i] - force) / mass
            acc_new[comp, i] = value
            vel_new[comp, i] = vel[comp, i] + 0.5 * TIME_STEP * (acc[comp, i] + value)


def split3(value):
    high = value.astype(BF16)
    rest = value - high.astype(F32)
    mid = rest.astype(BF16)
    low = (rest - mid.astype(F32)).astype(BF16)
    return high, mid, low


def prepare_kernel(
    disp, mat_h, moduli_h, decay_h, strength_h, stiff, rates, perm, elems,
    points, mat, moduli, decay, strength, sems,
):
    moves = [
        pltpu.make_async_copy(src, dst, sems.at[n])
        for n, (src, dst) in enumerate(
            [(mat_h, mat), (moduli_h, moduli), (decay_h, decay), (strength_h, strength)]
        )
    ]
    for move in moves:
        move.start()
    for c in range(4):
        hit = lax.broadcasted_iota(jnp.int32, (128, 512), 1) == (
            4 * lax.broadcasted_iota(jnp.int32, (128, 512), 0) + c
        )
        perm[128 * c : 128 * c + 128, :] = jnp.where(hit, 1.0, 0.0).astype(BF16)
    points[...] = jnp.zeros(points.shape, F32)
    for comp in range(3):
        for a in range(4):
            base = (comp * 4 + a) * 8
            points[base : base + 4, :] = disp[comp, a]
    to_nodes(points[...], perm, elems)
    for move in moves:
        move.wait()
    onehot = [mat[0] == m for m in range(8)]
    for k in range(6):
        for l in range(k, 6):
            value = jnp.zeros((1, 128), F32)
            for m in range(8):
                value = jnp.where(onehot[m], moduli[k, m, l], value)
            stiff[6 * k + l : 6 * k + l + 1, :] = value
    for l in range(3):
        rates[l : l + 1, :] = jnp.full((1, 128), decay[l], F32)
        rates[3 + l : 4 + l, :] = jnp.full((1, 128), (1.0 - decay[l]) * strength[l], F32)


def unpack_kernel(memory, rates, _, decayed, flag, old):
    for d in range(5):
        for a in range(5):
            for b in range(5):
                for c in range(5):
                    row = (b * 5 + c) * 4
                    old[row : row + 3, :] = memory[d, a, b, c].astype(F32)
            for c in range(5):
                for l in range(3):
                    was = old[pl.ds(4 * c + l, 8, stride=20), :]
                    decayed[((d * 5 + a) * 5 + c) * 3 + l] = rates[l : l + 1, :] * was
    flag[...] = jnp.zeros((8, 128), F32)


def repack_kernel(dense, memory_new, flag, new):
    for d in range(5):
        for a in range(5):
            for c in range(5):
                for l in range(3):
                    new[pl.ds(4 * c + l, 8, stride=20), :] = dense[((d * 5 + a) * 5 + c) * 3 + l]
            for b in range(5):
                for c in range(5):
                    row = (b * 5 + c) * 4
                    memory_new[d, a, b, c] = new[row : row + 3, :].astype(BF16)
    flag[...] = jnp.zeros((8, 128), F32)


def to_nodes(points, perm, elems):
    rows = points.shape[0]
    parts = jnp.concatenate(split3(points), 0)
    taken = lax.dot_general(
        parts, perm[...], (((1,), (1,)), ((), ())), preferred_element_type=F32
    )
    taken = taken[0:rows] + taken[rows : 2 * rows] + taken[2 * rows : 3 * rows]
    for c in range(4):
        elems[c] = taken[:, 128 * c : 128 * c + 128]
    lane = lanes((rows, 128))
    elems[4] = jnp.where(lane < 127, pltpu.roll(taken[:, 0:128], 127, 1), 0.0)


def elastic_kernel(
    lon_second, corner, lat_above, lon_first, stiff, rates, perm, own, decayed,
    dense, force, lat_force, lon_force,
    points, edge, elems, devs, flux,
):
    following = has_next()
    _, lon_above = arrived("lon", lon_first, lon_second)
    points[...] = jnp.zeros(points.shape, F32)
    for comp in range(3):
        points[8 * comp : 8 * comp + 4, :] = following * lat_above[4 * comp : 4 * comp + 4, :]
        points[8 * comp + 4 : 8 * comp + 5, :] = following * corner[comp : comp + 1]
    points[24:36, :] = lon_above[0:12]
    to_nodes(points[...], perm, edge)
    fifth = sublanes((8, 128)) == 4
    for c in range(5):
        for comp in range(3):
            for a in range(4):
                base, row = (comp * 5 + a) * 8, 24 + 4 * comp + a
                kept = own[c, (comp * 4 + a) * 8 : (comp * 4 + a) * 8 + 8, :]
                elems[c, base : base + 8, :] = jnp.where(
                    fifth, row_of(edge[c, 24:40, :], row - 24, 8), kept
                )
            base = (comp * 5 + 4) * 8
            elems[c, base : base + 8, :] = edge[c, 8 * comp : 8 * comp + 8, :]
    lane = lanes((128, 128))
    slopes = [
        by_index(sublanes((8, 128)), [2.0 * DERIV[b][p] for b in range(5)] + [0.0])
        for p in range(5)
    ]
    turned = [
        by_index(sublanes((8, 128)), [2.0 * DERIV[p][b] for b in range(5)] + [0.0])
        for p in range(5)
    ]
    weight_col = by_index(sublanes((8, 128)), W + [0.0])

    def slab(comp, a, c):
        base = (comp * 5 + a) * 8
        return elems[c, base : base + 8, :]

    def along_lon(cols, value):
        total = None
        for p in range(5):
            term = cols[p] * row_of(value, p, 8)
            total = term if total is None else total + term
        return total

    for a in range(5):
        elastic_of = []
        for c in range(5):
            dx, dy, dz = [], [], []
            for comp in range(3):
                dx.append(mix([2.0 * DERIV[a][p] for p in range(5)], [slab(comp, p, c) for p in range(5)]))
                dy.append(along_lon(slopes, slab(comp, a, c)))
                dz.append(mix([2.0 * DERIV[c][p] for p in range(5)], [slab(comp, a, p) for p in range(5)]))
            strain = [dx[0], dy[1], dz[2], dy[0] + dx[1], dz[0] + dx[2], dz[1] + dy[2]]
            elastic = []
            for k in range(6):
                total = None
                for l in range(6):
                    pos = 6 * min(k, l) + max(k, l)
                    term = stiff[pos : pos + 1, :] * strain[l]
                    total = term if total is None else total + term
                elastic.append(total)
            pressure = (elastic[0] + elastic[1] + elastic[2]) * (1.0 / 3.0)
            dev = [elastic[0] - pressure, elastic[1] - pressure, elastic[3], elastic[4], elastic[5]]
            for d in range(5):
                devs[d * 5 + c] = dev[d]
            elastic_of.append(elastic)
        relaxed = []
        for d in range(5):
            sums = []
            for c in range(5):
                dev = devs[d * 5 + c]
                total = None
                for l in range(3):
                    pos = ((d * 5 + a) * 5 + c) * 3 + l
                    now = decayed[pos] + rates[3 + l : 4 + l, :] * dev
                    now = now.astype(BF16).astype(F32)
                    dense[pos] = now
                    total = now if total is None else total + now
                sums.append(total)
            relaxed.append(sums)
        for c in range(5):
            e = elastic_of[c]
            r = [relaxed[d][c] for d in range(5)]
            weight = weight_col * (W[a] * W[c] / 8.0)
            stress = [e[0] - r[0], e[1] - r[1], e[2] + r[0] + r[1], e[3] - r[2], e[4] - r[3], e[5] - r[4]]
            for k in range(6):
                flux[k, a * 5 + c] = jnp.where(weight_col > 0.0, weight * stress[k], 0.0)
    flux_of = [[0, 3, 4], [3, 1, 5], [4, 5, 2]]
    for c in range(5):
        elems[c, 120:128, :] = jnp.zeros((8, 128), F32)
        for comp in range(3):
            for a in range(5):
                value = mix(
                    [2.0 * DERIV[p][a] for p in range(5)],
                    [flux[flux_of[comp][0], p * 5 + c] for p in range(5)],
                )
                value = value + along_lon(turned, flux[flux_of[comp][1], a * 5 + c])
                value = value + mix(
                    [2.0 * DERIV[p][c] for p in range(5)],
                    [flux[flux_of[comp][2], a * 5 + p] for p in range(5)],
                )
                base = (comp * 5 + a) * 8
                elems[c, base : base + 8, :] = value
    carried = jnp.where(lane > 0, pltpu.roll(elems[4], 1, 1), 0.0)
    merged = jnp.concatenate([elems[0] + carried, elems[1], elems[2], elems[3]], 1)
    parts = jnp.concatenate(split3(merged), 0)
    given = jnp.dot(parts, perm[...], preferred_element_type=F32)
    given = given[0:128] + given[128:256] + given[256:384]
    lat_force[12:16, :] = jnp.zeros((4, 512), F32)
    lon_force[15:16, :] = jnp.zeros((1, 512), F32)
    for comp in range(3):
        for a in range(5):
            base = (comp * 5 + a) * 8
            if a < 4:
                force[comp, a] = given[base : base + 4]
                lon_force[5 * comp + a : 5 * comp + a + 1, :] = given[base + 4 : base + 5]
            else:
                lat_force[4 * comp : 4 * comp + 4, :] = given[base : base + 4]
                lon_force[5 * comp + 4 : 5 * comp + 5, :] = given[base + 4 : base + 5]


def call(kernel, name, outs, ins, args, scratch=(), flops=1000000, moved=500000, vmem=24):
    return pl.pallas_call(
        kernel,
        name=name,
        out_shape=[jax.ShapeDtypeStruct(s, d) for s, d in outs],
        in_specs=ins,
        out_specs=[VMEM] * len(outs),
        scratch_shapes=list(scratch),
        compiler_params=pltpu.CompilerParams(vmem_limit_bytes=vmem * 1024 * 1024),
        cost_estimate=pl.CostEstimate(flops=flops, bytes_accessed=moved, transcendentals=0),
    )(*args)


def swap(array, axis, size, parity):
    pairs = []
    for i in range(parity, size, 2):
        j = (i + 1) % size
        pairs += [(i, j), (j, i)]
    return lax.ppermute(array, axis, pairs)


def ring(array, axis, size, by):
    return lax.ppermute(array, axis, [(i, (i + by) % size) for i in range(size)])


def swap_lat(first, second):
    return swap(first, "lat", LAT, 0), swap(second, "lat", LAT, 1)


def swap_lon(first, second):
    other = swap(second, "lon", LON, 1)
    return swap(first, "lon", LON, 0), other


def per_device(
    displacement, velocity, acceleration, potential, memory_vars, materials, shell_flags,
    moduli, densities, decay, strength,
):
    field = ((4, 4, 512), F32)
    vector = ((3, 4, 4, 512), F32)
    r8, r16, r24, r32, r40 = (((n, 512), F32) for n in (8, 16, 24, 32, 40))
    info = ((8, 128), F32)
    kept = pltpu.with_memory_space_constraint
    disp, phi, own_info, down_lat, *sent = call(
        start_kernel, "start", [vector, field, info, r16, r16, r16], [HBM] * 7,
        [
            kept(array, pltpu.HBM)
            for array in (
                displacement, velocity, acceleration, potential, materials, shell_flags, densities
            )
        ],
        [
            pltpu.VMEM((3, 4, 4, 512), F32),
            pltpu.VMEM((3, 4, 4, 512), F32),
            pltpu.VMEM((3, 4, 4, 512), F32),
            pltpu.VMEM((1, 1, 128), jnp.int32),
            pltpu.VMEM((1, 1, 128), jnp.int32),
            pltpu.SMEM((8,), F32),
            pltpu.SemaphoreType.DMA((7,)),
        ],
    )
    lon_a = swap_lon(*sent)
    above_a = ring(down_lat, "lat", LAT, -1)
    tables = call(
        prepare_kernel, "prepare",
        [((40, 128), F32), info, ((512, 512), BF16), ((5, 96, 128), F32)],
        [VMEM] + [HBM] * 4,
        [disp]
        + [
            kept(array, pltpu.HBM)
            for array in (materials, moduli.transpose(1, 0, 2), decay, strength)
        ],
        [
            pltpu.VMEM((96, 512), F32),
            pltpu.VMEM((1, 1, 128), jnp.int32),
            pltpu.SMEM((6, 8, 6), F32),
            pltpu.SMEM((3,), F32),
            pltpu.SMEM((3,), F32),
            pltpu.SemaphoreType.DMA((4,)),
        ],
    )
    lat_a = call(
        pack_kernel, "pack", [r16, r8], [VMEM] * 6,
        (lon_a[1], lon_a[0], disp, phi, own_info, tables[1]),
    )
    halo_a = (lon_a[1], ring(lat_a[0], "lat", LAT, 1), above_a, lon_a[0])
    corner = ring(lat_a[1], "lat", LAT, -1)
    memory = memory_vars.reshape(3, 5, 5, 5, 5, 128).transpose(1, 2, 3, 4, 0, 5)
    every = ((375, 8, 128), F32)
    coef, precond, w0, *sent = call(
        residual_kernel, "residual", [r40, field, field, r8, r8, r8, r8], [VMEM] * 7,
        (disp, phi, own_info, *halo_a),
    )
    decayed, _ = call(
        unpack_kernel, "unpack", [every, info], [VMEM] * 3, (memory, tables[1], sent[0]),
        [pltpu.VMEM((160, 128), F32)],
    )
    lon_b = swap_lon(*sent[2:])
    halo_b = (lon_b[1], *swap_lat(*sent[:2]), lon_b[0])
    dense, force, lat_force, lon_force = call(
        elastic_kernel, "elastic", [every, vector, r16, r16], [VMEM] * 9,
        (lon_a[1], corner, above_a, lon_a[0], *tables, decayed),
        [
            pltpu.VMEM((48, 512), F32),
            pltpu.VMEM((5, 48, 128), F32),
            pltpu.VMEM((5, 128, 128), F32),
            pltpu.VMEM((25, 8, 128), F32),
            pltpu.VMEM((6, 25, 8, 128), F32),
        ],
        flops=20000000, moved=2000000,
    )
    w1, *sent = call(
        second_kernel, "second", [field, r8, r8, r24, r24], [VMEM] * 8,
        (w0, coef, precond, *halo_b, lon_force),
    )
    lon_c = swap_lon(*sent[2:])
    halo_c = (lon_c[1], *swap_lat(*sent[:2]), lon_c[0])
    memory_new, packed = call(
        repack_kernel, "repack", [((5, 5, 5, 5, 3, 128), BF16), info], [VMEM], (dense,),
        [pltpu.VMEM((160, 128), F32)],
    )
    w2, *sent = call(
        third_kernel, "third", [field, r24, r24, r8, r32], [VMEM] * 9,
        (w1, coef, precond, *halo_c, lat_force, packed),
    )
    lon_d = swap_lon(*sent[2:])
    halo_d = (lon_d[1], *swap_lat(*sent[:2]), lon_d[0])
    rho_coef, disp_new, dense_done = call(
        density_kernel, "density", [r32, vector, info], [VMEM] * 3, (coef, disp, sent[0])
    )
    (line,) = call(
        moment_kernel, "moments", [((LAT * LON, 128), F32)], [VMEM] * 10,
        (w0, w1, w2, coef, precond, *halo_d, dense_done),
    )
    moments = lax.all_to_all(line, AXES, 0, 0, tiled=True)
    phi_new, acc_new, vel_new = call(
        final_kernel, "final", [field, vector, vector], [VMEM] * 25,
        (
            moments, phi, w0, w1, w2, rho_coef, force, *halo_a, *halo_b, *halo_c, *halo_d,
            velocity, acceleration,
        ),
    )
    memory_new = memory_new.transpose(4, 0, 1, 2, 3, 5).reshape(memory_vars.shape)
    return (disp_new, vel_new, acc_new, phi_new, memory_new)


def solution(mesh):
    vector = P(None, "lat", "lon", None)
    scalar = P("lat", "lon", None)
    memory = P(None, None, None, "lat", None, "lon", None, None)
    return jax.shard_map(
        per_device,
        mesh=mesh,
        in_specs=(vector, vector, vector, scalar, memory, scalar, scalar, P(), P(), P(), P()),
        out_specs=(vector, vector, vector, scalar, memory),
        check_vma=False,
    )
```
